32 devices in a mesh: grp: 4 (over z), seq: 8 (over y, x, core).
Axes of the slice: x: 2, y: 2, z: 4, core: 2. Of those that a mesh axis runs over, the one named last changes fastest.
Arguments:
- query: bfloat16 [4096, 1024], P(('grp', 'seq')), may hold values from -6 to 6
- keys: bfloat16 [4096, 1024], P(('grp', 'seq')), may hold values from -6 to 6
- values: bfloat16 [4096, 1024], P(('grp', 'seq')), may hold values from -6 to 6
- d_out: bfloat16 [4096, 1024], P(('grp', 'seq')), may hold values from -6 to 6
- rand_blocks: int32 [32, 3], replicated, may hold values from 0 to 31, as said below
- global_blocks: int32 [2], replicated, may hold values from 0 to 31, as said below
Outputs:
- attended: bfloat16 [4096, 1024], P(('grp', 'seq'))
- d_query: bfloat16 [4096, 1024], P(('grp', 'seq'))
- d_keys: bfloat16 [4096, 1024], P(('grp', 'seq'))
- d_values: bfloat16 [4096, 1024], P(('grp', 'seq'))
The draws below stay inside these ranges and needn't reach their ends.
Inputs may be any that keep to these rules, and one draw needn't show every extreme that they name: `rand_blocks`: the 3 entries of row b are distinct; each lies in another segment than b and in the same column: (r) % 8 equals (b) % 8 and r // 8 differs from b // 8. `global_blocks`: the 2 entries are distinct; one of them is the last block.
All inputs are finite; a program needn't handle non-finite values.
Results may differ from the reference program's by a relative error of at most 0.0074.
Values may be sent and summed in bfloat16 or wider, within the bound.
A program may use at most 128 MiB of HBM per device.

```python
import math
import jax
import jax.numpy as jnp
from jax import lax

D = 1024
HEADS = 16
HEAD_DIM = 64
BLOCK = 128
GLOBALS = 2
RANDOMS = 3
BLK_DEV = 1
SEGMENTS = 4
COLUMNS = 8
BLOCKS = 32
TOKENS = 4096


def rough_rows(key):
    return jnp.clip(jax.random.normal(jax.random.fold_in(key, 23), (TOKENS, D)), -6.0, 6.0)


def draw_query(key, part):
    base = rough_rows(jax.random.fold_in(key, 1))
    return base.astype(jnp.float32).astype(jnp.bfloat16)


def draw_keys(key, part):
    base = rough_rows(jax.random.fold_in(key, 2))
    return base.astype(jnp.float32).astype(jnp.bfloat16)


def draw_rand_blocks(key, part):
    block_ids = jnp.arange(BLOCKS, dtype=jnp.int32)
    device_ids = block_ids // BLK_DEV
    segment = device_ids // COLUMNS
    column = device_ids % COLUMNS
    split_keys = jax.random.split(jax.random.fold_in(key, 5), BLOCKS)
    offsets = jax.vmap(lambda one_key: jax.random.permutation(one_key, SEGMENTS - 1)[:RANDOMS] + 1)(split_keys)
    local_ids = jax.random.randint(jax.random.fold_in(key, 6), (BLOCKS, RANDOMS), 0, BLK_DEV)
    other = (segment[:, None] + offsets.astype(jnp.int32)) % SEGMENTS
    return ((other * COLUMNS + column[:, None]) * BLK_DEV + local_ids).astype(jnp.int32)


def draw_global_blocks(key, part):
    other = jax.random.randint(jax.random.fold_in(key, 8), (), 0, BLOCKS - 1)
    last = jnp.asarray(BLOCKS - 1, dtype=jnp.int32)
    flip = jax.random.randint(jax.random.fold_in(key, 9), (), 0, 2)
    first = jnp.where(flip == 0, other, last)
    second = jnp.where(flip == 0, last, other)
    return jnp.stack([first, second]).astype(jnp.int32)


def block_scale(own_key, dims, shards, least, top_value):
    gain = 1.0
    for axis_at, parts in shards:
        steps = jax.random.uniform(jax.random.fold_in(jax.random.fold_in(own_key, 6), axis_at), (parts,), jnp.float32, least / len(shards), top_value / len(shards))
        gain = gain * jnp.repeat(jnp.exp(steps), dims[axis_at] // parts).reshape((-1,) + (1,) * (len(dims) - 1 - axis_at))
    return gain


def bell_draw(key, extent, scale, bound, shards=(), kind=jnp.bfloat16):
    drawn = jax.random.normal(key, extent, jnp.float32) * scale
    if len(shards) > 0:
        drawn = block_scale(key, extent, shards, -0.22, 0.18) * drawn
    return jnp.clip(drawn, min=-bound, max=bound).astype(kind)


def setup_inputs(seed: int = 0) -> dict:
    streams_of = jax.random.split(jax.random.key(seed), 7)
    query = draw_query(jax.random.fold_in(streams_of[6], 71), 0)
    keys = draw_keys(jax.random.fold_in(streams_of[6], 71), 0)
    values = bell_draw(streams_of[2], (TOKENS, D), 1.0, 6.0, ((0, 32),))
    d_out = bell_draw(streams_of[3], (TOKENS, D), 1.0, 6.0, ((0, 32),))
    rand_blocks = draw_rand_blocks(jax.random.fold_in(streams_of[6], 71), 0)
    global_blocks = draw_global_blocks(jax.random.fold_in(streams_of[6], 71), 0)
    return dict(query=query, keys=keys, values=values, d_out=d_out, rand_blocks=rand_blocks, global_blocks=global_blocks)


def attend_blocks(queries, key_rows, value_rows, grad_rows, key_valid):
    factor = 1.0 / math.sqrt(queries.shape[-1])
    query_wide = queries.astype(jnp.float32)
    key_wide = key_rows.astype(jnp.float32)
    value_wide = value_rows.astype(jnp.float32)
    grad_wide = grad_rows.astype(jnp.float32)
    scores = jnp.einsum('nqhe,njkhe->nhqjk', query_wide, key_wide) * factor
    scores = jnp.where(key_valid[:, None, None, :, None], scores, -1e+30)
    row_max = lax.optimization_barrier(jnp.max(scores, axis=(3, 4), keepdims=True))
    raised = jnp.exp(scores - row_max)
    attn_prob = raised / lax.optimization_barrier(jnp.sum(raised, axis=(3, 4), keepdims=True))
    prob_half = lax.optimization_barrier(attn_prob.astype(jnp.bfloat16)).astype(jnp.float32)
    result = jnp.einsum('nhqjk,njkhe->nqhe', prob_half, value_wide)
    d_prob = jnp.einsum('nqhe,njkhe->nhqjk', grad_wide, value_wide)
    row_dot = lax.optimization_barrier(jnp.sum(attn_prob * d_prob, axis=(3, 4), keepdims=True))
    d_scores = attn_prob * (d_prob - row_dot) * factor
    d_scores = lax.optimization_barrier(d_scores.astype(jnp.bfloat16)).astype(jnp.float32)
    d_query = jnp.einsum('nhqjk,njkhe->nqhe', d_scores, key_wide)
    d_keys = jnp.einsum('nhqjk,nqhe->njkhe', d_scores, query_wide)
    d_values = jnp.einsum('nhqjk,nqhe->njkhe', prob_half, grad_wide)
    return (result, d_query, d_keys, d_values)

def reference(query, keys, values, d_out, rand_blocks, global_blocks):
    block_shape = (BLOCKS, BLOCK, HEADS, HEAD_DIM)
    query_blocks = query.reshape(block_shape)
    key_blocks = keys.reshape(block_shape)
    value_blocks = values.reshape(block_shape)
    grad_blocks = d_out.reshape(block_shape)
    own_ids = jnp.arange(BLOCKS, dtype=jnp.int32)
    left_ids = jnp.maximum(own_ids - 1, 0).astype(jnp.int32)
    right_ids = jnp.minimum(own_ids + 1, BLOCKS - 1).astype(jnp.int32)
    global_ids = jnp.broadcast_to(global_blocks.astype(jnp.int32)[None, :], (BLOCKS, GLOBALS))
    key_table = jnp.concatenate([left_ids[:, None], own_ids[:, None], right_ids[:, None], global_ids, rand_blocks.astype(jnp.int32)], axis=1)
    key_valid = jnp.concatenate([(own_ids > 0)[:, None], jnp.ones((BLOCKS, 1), dtype=jnp.bool_), (own_ids < BLOCKS - 1)[:, None], jnp.ones((BLOCKS, GLOBALS + RANDOMS), dtype=jnp.bool_)], axis=1)
    per_step = math.gcd(BLOCKS, 8)
    steps_count = BLOCKS // per_step

    def advance(totals, position):
        key_total, value_total = totals
        start = (position * per_step).astype(jnp.int32)
        listed = lax.dynamic_slice_in_dim(key_table, start, per_step, 0)
        allowed = lax.dynamic_slice_in_dim(key_valid, start, per_step, 0)
        query_rows = lax.dynamic_slice_in_dim(query_blocks, start, per_step, 0)
        grad_rows = lax.dynamic_slice_in_dim(grad_blocks, start, per_step, 0)
        result, d_query, d_keys, d_values = attend_blocks(query_rows, key_blocks[listed], value_blocks[listed], grad_rows, allowed)
        flat_ids = listed.reshape(-1)
        key_total = key_total.at[flat_ids].add(d_keys.reshape(-1, BLOCK, HEADS, HEAD_DIM))
        value_total = value_total.at[flat_ids].add(d_values.reshape(-1, BLOCK, HEADS, HEAD_DIM))
        return ((key_total, value_total), (result.astype(jnp.bfloat16), d_query.astype(jnp.bfloat16)))
    zero_total = jnp.zeros(block_shape, jnp.float32)
    totals, outputs = lax.scan(advance, (zero_total, zero_total), jnp.arange(steps_count, dtype=jnp.int32))
    attended = outputs[0].reshape(TOKENS, D)
    d_query = outputs[1].reshape(TOKENS, D)
    d_keys = totals[0].astype(jnp.bfloat16).reshape(TOKENS, D)
    d_values = totals[1].astype(jnp.bfloat16).reshape(TOKENS, D)
    return (attended, d_query, d_keys, d_values)
```

```python
import functools
import math

import jax
import jax.numpy as jnp
from jax import lax
from jax.experimental import pallas as pl
from jax.experimental.pallas import tpu as pltpu
from jax.sharding import PartitionSpec as P

HEAD_DIM = 64
BLOCK = 128
GLOBALS = 2
RANDOMS = 3
KEYS = 8


def extended(block, sides, width, periodic):
    for axis, dim in sides:
        count = lax.axis_size(axis)
        forward = [(i, i + 1) for i in range(count - 1)]
        if periodic:
            forward.append((count - 1, 0))
        backward = [(target, source) for source, target in forward]
        low = lax.ppermute(
            lax.slice_in_dim(block, block.shape[dim] - width, None, axis=dim), axis, forward
        )
        high = lax.ppermute(lax.slice_in_dim(block, 0, width, axis=dim), axis, backward)
        block = jnp.concatenate([low, block, high], axis=dim)
    return block


def broadcast(block, axis, source):
    block = jnp.where(lax.axis_index(axis) == source, block, jnp.zeros_like(block))
    return lax.psum(block, axis)


def attend_blocks(queries, key_rows, value_rows, grad_rows, key_valid):
    factor = 1.0 / math.sqrt(queries.shape[-1])
    scores = (
        jnp.einsum("nqhe,njkhe->nhqjk", queries, key_rows, preferred_element_type=jnp.float32)
        * factor
    )
    scores = jnp.where(key_valid[:, None, None, :, None], scores, -1e30)
    row_max = jnp.max(scores, axis=(3, 4), keepdims=True)
    raised = jnp.exp(scores - row_max)
    attn_prob = raised / jnp.sum(raised, axis=(3, 4), keepdims=True)
    prob_half = attn_prob.astype(jnp.bfloat16)
    result = jnp.einsum(
        "nhqjk,njkhe->nqhe", prob_half, value_rows, preferred_element_type=jnp.float32
    )
    d_prob = jnp.einsum(
        "nqhe,njkhe->nhqjk", grad_rows, value_rows, preferred_element_type=jnp.float32
    )
    row_dot = jnp.sum(attn_prob * d_prob, axis=(3, 4), keepdims=True)
    d_scores = (attn_prob * (d_prob - row_dot) * factor).astype(jnp.bfloat16)
    d_query = jnp.einsum(
        "nhqjk,njkhe->nqhe", d_scores, key_rows, preferred_element_type=jnp.float32
    )
    d_keys = jnp.einsum("nhqjk,nqhe->njkhe", d_scores, queries, preferred_element_type=jnp.float32)
    d_values = jnp.einsum(
        "nhqjk,nqhe->njkhe", prob_half, grad_rows, preferred_element_type=jnp.float32
    )
    return (result, d_query, d_keys, d_values)


def body(query, keys, values, d_out, rand_blocks, global_blocks):
    group_count = lax.axis_size("grp")
    column_count = lax.axis_size("seq")
    column = lax.axis_index("seq")
    tokens_dev = query.shape[0]
    width = query.shape[1]
    local_blocks = tokens_dev // BLOCK
    head_width = width // group_count
    heads_here = head_width // HEAD_DIM
    block_total = group_count * column_count * local_blocks
    segment_span = column_count * local_blocks
    stride = local_blocks + 2
    count = group_count * local_blocks
    per_step = 4
    steps_count = count // per_step
    stacked = jnp.stack([keys, values])
    widened = extended(stacked, ((("grp", "seq"), 1),), BLOCK, False)
    key_send = widened[0][None]
    value_send = widened[1][None]
    query_heads, grad_heads, key_heads, value_heads = (
        lax.all_to_all(
            query.reshape(1, tokens_dev, width), "grp", split_axis=2, concat_axis=0, tiled=True
        ),
        lax.all_to_all(
            d_out.reshape(1, tokens_dev, width), "grp", split_axis=2, concat_axis=0, tiled=True
        ),
        lax.all_to_all(key_send, "grp", split_axis=2, concat_axis=0, tiled=True),
        lax.all_to_all(value_send, "grp", split_axis=2, concat_axis=0, tiled=True),
    )
    ext_pair = jnp.stack([key_heads, value_heads]).reshape(
        2, group_count * stride, BLOCK, head_width
    )
    global_device = global_blocks // local_blocks
    global_segment = global_device // column_count
    global_column = global_device % column_count
    global_local = global_blocks % local_blocks
    global_rows = global_segment * stride + global_local + 1
    fetched = []
    for which in range(GLOBALS):
        fetched.append(broadcast(ext_pair[:, global_rows[which]], "seq", global_column[which]))
    global_pair = jnp.stack(fetched, axis=1)
    segment_of = jnp.repeat(jnp.arange(group_count, dtype=jnp.int32), local_blocks)
    local_of = jnp.tile(jnp.arange(local_blocks, dtype=jnp.int32), group_count)
    query_ids = (segment_of * column_count + column) * local_blocks + local_of
    rand_ids = jnp.take(rand_blocks, query_ids, axis=0)
    rand_rows = rand_ids // segment_span * stride + rand_ids % local_blocks + 1
    window_rows = (segment_of * stride + local_of)[:, None] + jnp.arange(3, dtype=jnp.int32)[
        None, :
    ]
    key_table = jnp.concatenate([window_rows, rand_rows], axis=1)
    key_valid = jnp.concatenate(
        [
            (query_ids > 0)[:, None],
            jnp.ones((count, 1), dtype=jnp.bool_),
            (query_ids < block_total - 1)[:, None],
            jnp.ones((count, GLOBALS + RANDOMS), dtype=jnp.bool_),
        ],
        axis=1,
    )
    query_steps = query_heads.reshape(steps_count, per_step, BLOCK, heads_here, HEAD_DIM)
    grad_steps = grad_heads.reshape(steps_count, per_step, BLOCK, heads_here, HEAD_DIM)
    table_steps = key_table.reshape(steps_count, per_step, 3 + RANDOMS)
    valid_steps = key_valid.reshape(steps_count, per_step, KEYS)
    global_spread = jnp.broadcast_to(
        global_pair[:, None], (2, per_step, GLOBALS, BLOCK, head_width)
    )

    def advance(totals, packed):
        ext_total, global_total = totals
        query_part, grad_part, rows_part, valid_part = packed
        taken = jnp.stack(
            [
                lax.dynamic_index_in_dim(ext_pair, row, axis=1, keepdims=False)
                for row in rows_part.reshape(-1)
            ],
            axis=1,
        ).reshape(2, per_step, 3 + RANDOMS, BLOCK, head_width)
        gathered = jnp.concatenate([taken[:, :, :3], global_spread, taken[:, :, 3:]], axis=2)
        gathered = gathered.reshape(2, per_step, KEYS, BLOCK, heads_here, HEAD_DIM)
        result, d_query, d_keys, d_values = attend_blocks(
            query_part, gathered[0], gathered[1], grad_part, valid_part
        )
        d_pair = jnp.stack([d_keys, d_values]).reshape(2, per_step, KEYS, BLOCK, head_width)
        spread_back = jnp.concatenate([d_pair[:, :, :3], d_pair[:, :, 3 + GLOBALS :]], axis=2)
        spread_back = spread_back.reshape(2, per_step * (3 + RANDOMS), BLOCK, head_width)
        ext_total = ext_total.at[:, rows_part.reshape(-1)].add(spread_back)
        global_total = global_total + jnp.sum(d_pair[:, :, 3 : 3 + GLOBALS], axis=1)
        return (
            (ext_total, global_total),
            (result.astype(jnp.bfloat16), d_query.astype(jnp.bfloat16)),
        )

    start_totals = (
        jnp.zeros((2, group_count * stride, BLOCK, head_width), jnp.float32),
        jnp.zeros((2, GLOBALS, BLOCK, head_width), jnp.float32),
    )
    totals, outputs = lax.scan(
        advance, start_totals, (query_steps, grad_steps, table_steps, valid_steps)
    )
    ext_total = totals[0].reshape(2, group_count, stride, BLOCK, head_width)
    global_sum = lax.psum(totals[1], "seq")
    own_grad = ext_total[:, :, 1 : local_blocks + 1]
    for which in range(GLOBALS):
        addend = jnp.where(column == global_column[which], global_sum[:, which], 0.0)
        own_grad = own_grad.at[:, global_segment[which], global_local[which]].add(addend)
    send_left = ext_total[:, :, 0]
    send_right = ext_total[:, :, local_blocks + 1]
    empty_edge = jnp.zeros_like(send_left[:, :1])
    send_left = jnp.where(
        column == 0, jnp.concatenate([send_left[:, 1:], empty_edge], axis=1), send_left
    )
    send_right = jnp.where(
        column == column_count - 1,
        jnp.concatenate([empty_edge, send_right[:, :-1]], axis=1),
        send_right,
    )
    edges = jnp.concatenate([send_left, send_right], axis=2)
    arrived = extended(edges, (("seq", 2),), BLOCK, True)
    own_grad = own_grad.at[:, :, 0].add(arrived[:, :, :BLOCK])
    own_grad = own_grad.at[:, :, local_blocks - 1].add(arrived[:, :, 3 * BLOCK :])
    head_shape = (group_count, tokens_dev, head_width)
    attended_heads = outputs[0].reshape(head_shape)
    d_query_heads = outputs[1].reshape(head_shape)
    d_key_heads = own_grad[0].reshape(head_shape).astype(jnp.bfloat16)
    d_value_heads = own_grad[1].reshape(head_shape).astype(jnp.bfloat16)
    returned = (
        lax.all_to_all(attended_heads, "grp", split_axis=0, concat_axis=2, tiled=True),
        lax.all_to_all(d_query_heads, "grp", split_axis=0, concat_axis=2, tiled=True),
        lax.all_to_all(d_key_heads, "grp", split_axis=0, concat_axis=2, tiled=True),
        lax.all_to_all(d_value_heads, "grp", split_axis=0, concat_axis=2, tiled=True),
    )
    return (
        returned[0].reshape(tokens_dev, width),
        returned[1].reshape(tokens_dev, width),
        returned[2].reshape(tokens_dev, width),
        returned[3].reshape(tokens_dev, width),
    )


MESH = pl.DeviceIdType.MESH
F32 = jnp.float32
BF16 = jnp.bfloat16
LANES = 128


def contract(left, right, dims):
    return lax.dot_general(left, right, (dims, ((), ())), preferred_element_type=F32)


def fused_kernel(
    groups, columns, global_ref, q_ref, k_ref, v_ref, g_ref,
    att_ref, dq_ref, dk_ref, dv_ref,
    qg, kv, side, cand, piece, glob, dsum, dside, dside_in, dg_out, dg_in, dg_sum,
    att_out, dq_out, dk_out, dv_out,
    own_sem, kv_recv, qg_recv, side_recv, ga_recv, gb_recv, ds_recv, da_recv, db_recv,
    in_send, side_send, glob_send, ds_send, out_send, out_recv, keep_sem,
):
    h = lax.axis_index("grp")
    c = lax.axis_index("seq")
    rows, width = q_ref.shape
    share = width // groups
    strip = rows // columns
    pairs = share // LANES

    def rows_of(index):
        return pl.ds(pl.multiple_of(index * strip, strip), strip)

    def remote(src, dst, send, recv, device):
        return pltpu.make_async_remote_copy(
            src_ref=src, dst_ref=dst, send_sem=send, recv_sem=recv,
            device_id=device, device_id_type=MESH,
        )

    def settle(ref, sem):
        pltpu.make_async_copy(ref, ref, sem).wait()

    right = lax.rem(c + 1, columns)
    left = lax.rem(c + columns - 1, columns)

    barrier = pltpu.get_barrier_semaphore()
    for d in range(1, groups):
        pl.semaphore_signal(
            barrier, inc=1, device_id=(lax.rem(h + d, groups), c), device_id_type=MESH
        )
    for e in range(1, columns):
        pl.semaphore_signal(
            barrier, inc=1, device_id=(h, lax.rem(c + e, columns)), device_id_type=MESH
        )

    def lanes_of(index, pair):
        return pl.ds(pl.multiple_of(index * share + pair * LANES, LANES), LANES)

    own = []
    for pair in range(pairs):
        for kind, (refs, buf) in enumerate((((k_ref, v_ref), kv), ((q_ref, g_ref), qg))):
            for a, ref in enumerate(refs):
                own.append(
                    pltpu.make_async_copy(
                        ref.at[:, lanes_of(h, pair)], buf.at[pair, a, h], own_sem.at[kind, pair]
                    )
                )
    for copy in own:
        copy.start()
    pl.semaphore_wait(barrier, groups + columns - 2)

    def send_in(kind, pair):
        refs, buf = (((k_ref, v_ref), kv), ((q_ref, g_ref), qg))[kind]
        for d in range(1, groups):
            target = lax.rem(h + d, groups)
            arrival = qg_recv.at[pair] if kind else kv_recv.at[pair, d - 1]
            for a, ref in enumerate(refs):
                remote(
                    ref.at[:, lanes_of(target, pair)], buf.at[pair, a, h],
                    in_send.at[kind], arrival, (target, c),
                ).start()

    def send_sides(pair, d):
        segment = lax.rem(h + groups - d, groups)
        for way, to in ((0, right), (1, left)):
            remote(
                kv.at[pair, :, segment], side.at[pair, way, :, segment],
                side_send.at[0], side_recv.at[pair], (h, to),
            ).start()

    def forward(pair, then=None):
        settle(kv.at[pair, :, h], own_sem.at[0, pair])
        send_sides(pair, 0)
        for d in range(1, groups):
            settle(kv.at[pair, :, lax.rem(h + groups - d, groups)], kv_recv.at[pair, d - 1])
            send_sides(pair, d)
            if d == 1 and then is not None:
                send_in(*then)

    seg_of = [lax.div(global_ref[w], columns) for w in range(GLOBALS)]
    col_of = [lax.rem(global_ref[w], columns) for w in range(GLOBALS)]

    def offer(pair):
        for w in range(GLOBALS):
            for a in range(2):
                chosen = kv[pair, a, 0]
                for t in range(1, groups):
                    chosen = jnp.where(seg_of[w] == t, kv[pair, a, t], chosen)
                cand[pair, 2 * w + a] = chosen
        for e in range(1, columns):
            to = lax.rem(c + e, columns)
            remote(
                cand.at[pair, :, rows_of(to), :], piece.at[pair, c],
                glob_send.at[0], ga_recv.at[pair], (h, to),
            ).start()
        piece[pair, c] = cand[pair, :, rows_of(c), :]

    def choose(pair):
        settle(piece.at[pair, pl.ds(0, columns - 1)], ga_recv.at[pair])
        for w in range(GLOBALS):
            for a in range(2):
                chosen = piece[pair, 0, 2 * w + a]
                for e in range(1, columns):
                    chosen = jnp.where(col_of[w] == e, piece[pair, e, 2 * w + a], chosen)
                glob[pair, 2 * w + a, rows_of(c), :] = chosen
        for e in range(1, columns):
            to = lax.rem(c + e, columns)
            remote(
                glob.at[pair, :, rows_of(c), :], glob.at[pair, :, rows_of(c), :],
                glob_send.at[1], gb_recv.at[pair], (h, to),
            ).start()

    lane = lax.broadcasted_iota(jnp.int32, (rows, LANES), 1)
    factor = 1.0 / math.sqrt(HEAD_DIM)
    last = groups * columns - 1

    def stacked(block):
        zero = jnp.zeros_like(block)
        low = jnp.where(lane < HEAD_DIM, block, zero)
        high = jnp.where(lane < HEAD_DIM, zero, block)
        return jnp.concatenate([low, high], axis=0)

    def picked(wide):
        return jnp.concatenate(
            [wide[:HEAD_DIM, :rows], wide[HEAD_DIM:, rows:]], axis=0
        ).T

    outgoing = ((att_out, att_ref), (dq_out, dq_ref), (dk_out, dk_ref), (dv_out, dv_ref))

    def send_out(pair, i, first):
        segment = lax.rem(h + i + 1, groups)
        for buf, ref in outgoing[first : first + 2]:
            if i < groups - 1:
                remote(
                    buf.at[pair, segment], ref.at[:, lanes_of(h, pair)],
                    out_send.at[first // 2], out_recv.at[first // 2], (segment, c),
                ).start()
            else:
                pltpu.make_async_copy(
                    buf.at[pair, h], ref.at[:, lanes_of(h, pair)], keep_sem.at[0]
                ).start()

    def send_dsides(pair, j):
        steps = pl.ds(2 * j, 2)
        for way, to in ((0, left), (1, right)):
            remote(
                dside.at[pair, way, :, steps], dside_in.at[pair, way, :, steps],
                ds_send.at[0], ds_recv.at[pair], (h, to),
            ).start()

    at_first = jnp.where(c == 0, 1, 0)
    at_last = jnp.where(c == columns - 1, 1, 0)
    dense = (groups + GLOBALS) * rows

    def unit(pair, i):
        segment = lax.rem(h + i + 1, groups)
        block = segment * columns + c
        before = lax.rem(segment + groups - at_first, groups)
        after = lax.rem(segment + at_last, groups)

        def listed(a):
            return jnp.concatenate(
                [kv[pair, a, t] for t in range(groups)]
                + [glob[pair, 2 * w + a] for w in range(GLOBALS)]
                + [side[pair, 0, a, before], side[pair, 1, a, after]],
                axis=0,
            )

        key = listed(0)
        value = listed(1)
        query = stacked(qg[pair, 0, segment] * jnp.asarray(factor, BF16))
        grad = stacked(qg[pair, 1, segment])
        scores = contract(key, query, ((1,), (1,)))
        scores = jnp.concatenate(
            [
                scores[:dense],
                jnp.where(block > 0, scores[dense : dense + rows], -1e30),
                jnp.where(block < last, scores[dense + rows :], -1e30),
            ],
            axis=0,
        )
        raised = jnp.exp(scores - jnp.max(scores, axis=0, keepdims=True))
        prob = raised * (1.0 / jnp.sum(raised, axis=0, keepdims=True))
        half = prob.astype(BF16)
        d_prob = contract(value, grad, ((1,), (1,)))
        result = contract(value, half, ((0,), (0,)))
        row_dot = jnp.sum(prob * d_prob, axis=0, keepdims=True)
        d_scores = (prob * (d_prob - row_dot)).astype(BF16)
        d_query = contract(key, d_scores, ((0,), (0,))) * factor
        d_value = contract(half, grad, ((1,), (0,)))
        d_key = contract(d_scores, query, ((1,), (0,)))
        att_out[pair, segment] = picked(result).astype(BF16)
        dq_out[pair, segment] = picked(d_query).astype(BF16)
        return d_key, d_value

    def halves(pair, j):
        both = [unit(pair, i) for i in (2 * j, 2 * j + 1)]
        for a in range(2):
            summed = both[0][a][:dense] + both[1][a][:dense]
            if j == 0:
                dsum[pair, a] = summed
            else:
                dsum[pair, a] += summed
            for i in range(2):
                dside[pair, 0, a, 2 * j + i] = both[i][a][dense : dense + rows].astype(BF16)
                dside[pair, 1, a, 2 * j + i] = both[i][a][dense + rows :].astype(BF16)
        send_dsides(pair, j)
        for i in (2 * j, 2 * j + 1):
            send_out(pair, i, 0)

    def arrive(pair):
        settle(qg.at[pair, :, h], own_sem.at[1, pair])
        settle(qg.at[pair, :, pl.ds(0, groups - 1)], qg_recv.at[pair])
        settle(side.at[pair], side_recv.at[pair])
        settle(glob.at[pair, :, pl.ds(0, rows - strip)], gb_recv.at[pair])

    def scatter(pair):
        for w in range(GLOBALS):
            for a in range(2):
                start = (groups + w) * rows
                dg_out[pair, 2 * w + a] = dsum[pair, a, start : start + rows].astype(BF16)
        for e in range(1, columns):
            to = lax.rem(c + e, columns)
            remote(
                dg_out.at[pair, :, rows_of(to), :], dg_in.at[pair, c],
                glob_send.at[2], da_recv.at[pair], (h, to),
            ).start()
        dg_in[pair, c] = dg_out[pair, :, rows_of(c), :]

    def gather(pair):
        settle(dg_in.at[pair, pl.ds(0, columns - 1)], da_recv.at[pair])
        total = dg_in[pair, 0].astype(F32)
        for e in range(1, columns):
            total = total + dg_in[pair, e].astype(F32)
        dg_sum[pair, :, rows_of(c), :] = total.astype(BF16)
        for e in range(1, columns):
            to = lax.rem(c + e, columns)
            remote(
                dg_sum.at[pair, :, rows_of(c), :], dg_sum.at[pair, :, rows_of(c), :],
                glob_send.at[3], db_recv.at[pair], (h, to),
            ).start()

    def finish(pair):
        settle(dside_in.at[pair], ds_recv.at[pair])
        settle(dg_sum.at[pair, :, pl.ds(0, rows - strip)], db_recv.at[pair])
        for i in range(groups):
            segment = lax.rem(h + i + 1, groups)
            low = lax.rem(i + at_last, groups)
            high = lax.rem(i + groups - at_first, groups)
            span = pl.ds(pl.multiple_of(segment * rows, rows), rows)
            for a, buf in enumerate((dk_out, dv_out)):
                whole = dsum[pair, a, span]
                whole += dside_in[pair, 0, a, low].astype(F32)
                whole += dside_in[pair, 1, a, high].astype(F32)
                for w in range(GLOBALS):
                    mine = (global_ref[w] == segment * columns + c).astype(F32)
                    whole += dg_sum[pair, 2 * w + a].astype(F32) * mine
                buf[pair, segment] = whole.astype(BF16)
            send_out(pair, i, 2)

    send_in(0, 0)
    for pair in range(pairs):
        if pair + 1 < pairs:
            send_in(0, pair + 1)
        forward(pair, (1, pair))
        offer(pair)
    for pair in range(pairs):
        choose(pair)
    for pair in range(pairs):
        arrive(pair)
        halves(pair, 0)
        if pair:
            gather(pair - 1)
        halves(pair, 1)
        scatter(pair)
        if pair:
            finish(pair - 1)
    gather(pairs - 1)
    finish(pairs - 1)

    shares = pl.ds(0, groups - 1)
    for n in range(2):
        settle(kv.at[:, :, shares], in_send.at[n])
        settle(kv.at[:, :, shares], out_send.at[n])
        settle(kv.at[:, :, shares], out_recv.at[n])
    settle(side, side_send.at[0])
    settle(dside, ds_send.at[0])
    for n in range(2):
        settle(piece.at[:, pl.ds(0, columns - 1)], glob_send.at[2 * n])
        settle(glob.at[:, :, pl.ds(0, rows - strip)], glob_send.at[2 * n + 1])
    settle(kv.at[:, :, pl.ds(0, 2)], keep_sem.at[0])


def fused(groups, columns, query, keys, values, d_out, rand_blocks, global_blocks):
    rows, width = query.shape
    share = width // groups
    strip = rows // columns
    half = functools.partial(pltpu.VMEM, dtype=BF16)
    full = functools.partial(pltpu.VMEM, dtype=F32)
    dma = pltpu.SemaphoreType.DMA
    pairs = share // LANES
    tile = (rows, LANES)
    scratch = [
        half((pairs, 2, groups, *tile)),
        half((pairs, 2, groups, *tile)),
        half((pairs, 2, 2, groups, *tile)),
        half((pairs, 2 * GLOBALS, *tile)),
        half((pairs, columns, 2 * GLOBALS, strip, LANES)),
        half((pairs, 2 * GLOBALS, *tile)),
        full((pairs, 2, (groups + GLOBALS) * rows, LANES)),
        half((pairs, 2, 2, groups, *tile)),
        half((pairs, 2, 2, groups, *tile)),
        half((pairs, 2 * GLOBALS, *tile)),
        half((pairs, columns, 2 * GLOBALS, strip, LANES)),
        half((pairs, 2 * GLOBALS, *tile)),
    ] + [half((pairs, groups, *tile))] * 4
    scratch += [dma((2, pairs)), dma((pairs, groups - 1))] + [dma((pairs,))] * 7
    scratch += [dma((2,)), dma((1,)), dma((4,)), dma((1,)), dma((2,)), dma((2,)), dma((1,))]
    hbm = pl.BlockSpec(memory_space=pltpu.HBM)
    return pl.pallas_call(
        functools.partial(fused_kernel, groups, columns),
        out_shape=[jax.ShapeDtypeStruct((rows, width), BF16)] * 4,
        in_specs=[pl.BlockSpec(memory_space=pltpu.SMEM)] + [hbm] * 4,
        out_specs=[hbm] * 4,
        scratch_shapes=scratch,
        compiler_params=pltpu.CompilerParams(
            collective_id=0, has_side_effects=True, vmem_limit_bytes=63 * 2**20
        ),
    )(global_blocks, query, keys, values, d_out)


CHUNKS = 4


def relay_kernel(*refs):
    count = (len(refs) - 3) // 2
    sources, targets = refs[:count], refs[count : 2 * count]
    held, in_sem, out_sem = refs[2 * count :]
    rows = held.shape[1] // CHUNKS
    for part in range(CHUNKS):
        at = pl.ds(part * rows, rows)
        for n in range(count):
            pltpu.make_async_copy(sources[n].at[at], held.at[n, at], in_sem.at[part]).start()
    for part in range(CHUNKS):
        at = pl.ds(part * rows, rows)
        pltpu.make_async_copy(held.at[:, at], held.at[:, at], in_sem.at[part]).wait()
        for n in range(count):
            pltpu.make_async_copy(held.at[n, at], targets[n].at[at], out_sem.at[0]).start()
    pltpu.make_async_copy(held, held, out_sem.at[0]).wait()


def relay(*arrays):
    hbm = pl.BlockSpec(memory_space=pltpu.HBM)
    count = len(arrays)
    return pl.pallas_call(
        relay_kernel,
        out_shape=[jax.ShapeDtypeStruct(a.shape, a.dtype) for a in arrays],
        in_specs=[hbm] * count,
        out_specs=[hbm] * count,
        scratch_shapes=[
            pltpu.VMEM((count, *arrays[0].shape), arrays[0].dtype),
            pltpu.SemaphoreType.DMA((CHUNKS,)),
            pltpu.SemaphoreType.DMA((1,)),
        ],
    )(*arrays)


def solution(mesh):
    in_specs = (
        P(("grp", "seq"), None),
        P(("grp", "seq"), None),
        P(("grp", "seq"), None),
        P(("grp", "seq"), None),
        P(),
        P(),
    )
    out_specs = (
        P(("grp", "seq"), None),
        P(("grp", "seq"), None),
        P(("grp", "seq"), None),
        P(("grp", "seq"), None),
    )
    groups, columns = mesh.shape["grp"], mesh.shape["seq"]

    def run(query, *rest):
        rows, width = query.shape
        whole_column = rows == BLOCK and groups - 1 == RANDOMS and groups % 2 == 0
        if whole_column and rows % (16 * columns) == 0 and width % (groups * LANES) == 0:
            return relay(*fused(groups, columns, query, *rest))
        return body(query, *rest)

    return jax.shard_map(run, mesh=mesh, in_specs=in_specs, out_specs=out_specs, check_vma=False)
```

```python
import functools
import math

import jax
import jax.numpy as jnp
from jax import lax
from jax.experimental import pallas as pl
from jax.experimental.pallas import tpu as pltpu
from jax.sharding import PartitionSpec as P

HEAD_DIM = 64
BLOCK = 128
GLOBALS = 2
RANDOMS = 3
KEYS = 8


def extended(block, sides, width, periodic):
    for axis, dim in sides:
        count = lax.axis_size(axis)
        forward = [(i, i + 1) for i in range(count - 1)]
        if periodic:
            forward.append((count - 1, 0))
        backward = [(target, source) for source, target in forward]
        low = lax.ppermute(
            lax.slice_in_dim(block, block.shape[dim] - width, None, axis=dim), axis, forward
        )
        high = lax.ppermute(lax.slice_in_dim(block, 0, width, axis=dim), axis, backward)
        block = jnp.concatenate([low, block, high], axis=dim)
    return block


def broadcast(block, axis, source):
    block = jnp.where(lax.axis_index(axis) == source, block, jnp.zeros_like(block))
    return lax.psum(block, axis)


def attend_blocks(queries, key_rows, value_rows, grad_rows, key_valid):
    factor = 1.0 / math.sqrt(queries.shape[-1])
    scores = (
        jnp.einsum("nqhe,njkhe->nhqjk", queries, key_rows, preferred_element_type=jnp.float32)
        * factor
    )
    scores = jnp.where(key_valid[:, None, None, :, None], scores, -1e30)
    row_max = jnp.max(scores, axis=(3, 4), keepdims=True)
    raised = jnp.exp(scores - row_max)
    attn_prob = raised / jnp.sum(raised, axis=(3, 4), keepdims=True)
    prob_half = attn_prob.astype(jnp.bfloat16)
    result = jnp.einsum(
        "nhqjk,njkhe->nqhe", prob_half, value_rows, preferred_element_type=jnp.float32
    )
    d_prob = jnp.einsum(
        "nqhe,njkhe->nhqjk", grad_rows, value_rows, preferred_element_type=jnp.float32
    )
    row_dot = jnp.sum(attn_prob * d_prob, axis=(3, 4), keepdims=True)
    d_scores = (attn_prob * (d_prob - row_dot) * factor).astype(jnp.bfloat16)
    d_query = jnp.einsum(
        "nhqjk,njkhe->nqhe", d_scores, key_rows, preferred_element_type=jnp.float32
    )
    d_keys = jnp.einsum("nhqjk,nqhe->njkhe", d_scores, queries, preferred_element_type=jnp.float32)
    d_values = jnp.einsum(
        "nhqjk,nqhe->njkhe", prob_half, grad_rows, preferred_element_type=jnp.float32
    )
    return (result, d_query, d_keys, d_values)


def body(query, keys, values, d_out, rand_blocks, global_blocks):
    group_count = lax.axis_size("grp")
    column_count = lax.axis_size("seq")
    column = lax.axis_index("seq")
    tokens_dev = query.shape[0]
    width = query.shape[1]
    local_blocks = tokens_dev // BLOCK
    head_width = width // group_count
    heads_here = head_width // HEAD_DIM
    block_total = group_count * column_count * local_blocks
    segment_span = column_count * local_blocks
    stride = local_blocks + 2
    count = group_count * local_blocks
    per_step = 4
    steps_count = count // per_step
    stacked = jnp.stack([keys, values])
    widened = extended(stacked, ((("grp", "seq"), 1),), BLOCK, False)
    key_send = widened[0][None]
    value_send = widened[1][None]
    query_heads, grad_heads, key_heads, value_heads = (
        lax.all_to_all(
            query.reshape(1, tokens_dev, width), "grp", split_axis=2, concat_axis=0, tiled=True
        ),
        lax.all_to_all(
            d_out.reshape(1, tokens_dev, width), "grp", split_axis=2, concat_axis=0, tiled=True
        ),
        lax.all_to_all(key_send, "grp", split_axis=2, concat_axis=0, tiled=True),
        lax.all_to_all(value_send, "grp", split_axis=2, concat_axis=0, tiled=True),
    )
    ext_pair = jnp.stack([key_heads, value_heads]).reshape(
        2, group_count * stride, BLOCK, head_width
    )
    global_device = global_blocks // local_blocks
    global_segment = global_device // column_count
    global_column = global_device % column_count
    global_local = global_blocks % local_blocks
    global_rows = global_segment * stride + global_local + 1
    fetched = []
    for which in range(GLOBALS):
        fetched.append(broadcast(ext_pair[:, global_rows[which]], "seq", global_column[which]))
    global_pair = jnp.stack(fetched, axis=1)
    segment_of = jnp.repeat(jnp.arange(group_count, dtype=jnp.int32), local_blocks)
    local_of = jnp.tile(jnp.arange(local_blocks, dtype=jnp.int32), group_count)
    query_ids = (segment_of * column_count + column) * local_blocks + local_of
    rand_ids = jnp.take(rand_blocks, query_ids, axis=0)
    rand_rows = rand_ids // segment_span * stride + rand_ids % local_blocks + 1
    window_rows = (segment_of * stride + local_of)[:, None] + jnp.arange(3, dtype=jnp.int32)[
        None, :
    ]
    key_table = jnp.concatenate([window_rows, rand_rows], axis=1)
    key_valid = jnp.concatenate(
        [
            (query_ids > 0)[:, None],
            jnp.ones((count, 1), dtype=jnp.bool_),
            (query_ids < block_total - 1)[:, None],
            jnp.ones((count, GLOBALS + RANDOMS), dtype=jnp.bool_),
        ],
        axis=1,
    )
    query_steps = query_heads.reshape(steps_count, per_step, BLOCK, heads_here, HEAD_DIM)
    grad_steps = grad_heads.reshape(steps_count, per_step, BLOCK, heads_here, HEAD_DIM)
    table_steps = key_table.reshape(steps_count, per_step, 3 + RANDOMS)
    valid_steps = key_valid.reshape(steps_count, per_step, KEYS)
    global_spread = jnp.broadcast_to(
        global_pair[:, None], (2, per_step, GLOBALS, BLOCK, head_width)
    )

    def advance(totals, packed):
        ext_total, global_total = totals
        query_part, grad_part, rows_part, valid_part = packed
        taken = jnp.stack(
            [
                lax.dynamic_index_in_dim(ext_pair, row, axis=1, keepdims=False)
                for row in rows_part.reshape(-1)
            ],
            axis=1,
        ).reshape(2, per_step, 3 + RANDOMS, BLOCK, head_width)
        gathered = jnp.concatenate([taken[:, :, :3], global_spread, taken[:, :, 3:]], axis=2)
        gathered = gathered.reshape(2, per_step, KEYS, BLOCK, heads_here, HEAD_DIM)
        result, d_query, d_keys, d_values = attend_blocks(
            query_part, gathered[0], gathered[1], grad_part, valid_part
        )
        d_pair = jnp.stack([d_keys, d_values]).reshape(2, per_step, KEYS, BLOCK, head_width)
        spread_back = jnp.concatenate([d_pair[:, :, :3], d_pair[:, :, 3 + GLOBALS :]], axis=2)
        spread_back = spread_back.reshape(2, per_step * (3 + RANDOMS), BLOCK, head_width)
        ext_total = ext_total.at[:, rows_part.reshape(-1)].add(spread_back)
        global_total = global_total + jnp.sum(d_pair[:, :, 3 : 3 + GLOBALS], axis=1)
        return (
            (ext_total, global_total),
            (result.astype(jnp.bfloat16), d_query.astype(jnp.bfloat16)),
        )

    start_totals = (
        jnp.zeros((2, group_count * stride, BLOCK, head_width), jnp.float32),
        jnp.zeros((2, GLOBALS, BLOCK, head_width), jnp.float32),
    )
    totals, outputs = lax.scan(
        advance, start_totals, (query_steps, grad_steps, table_steps, valid_steps)
    )
    ext_total = totals[0].reshape(2, group_count, stride, BLOCK, head_width)
    global_sum = lax.psum(totals[1], "seq")
    own_grad = ext_total[:, :, 1 : local_blocks + 1]
    for which in range(GLOBALS):
        addend = jnp.where(column == global_column[which], global_sum[:, which], 0.0)
        own_grad = own_grad.at[:, global_segment[which], global_local[which]].add(addend)
    send_left = ext_total[:, :, 0]
    send_right = ext_total[:, :, local_blocks + 1]
    empty_edge = jnp.zeros_like(send_left[:, :1])
    send_left = jnp.where(
        column == 0, jnp.concatenate([send_left[:, 1:], empty_edge], axis=1), send_left
    )
    send_right = jnp.where(
        column == column_count - 1,
        jnp.concatenate([empty_edge, send_right[:, :-1]], axis=1),
        send_right,
    )
    edges = jnp.concatenate([send_left, send_right], axis=2)
    arrived = extended(edges, (("seq", 2),), BLOCK, True)
    own_grad = own_grad.at[:, :, 0].add(arrived[:, :, :BLOCK])
    own_grad = own_grad.at[:, :, local_blocks - 1].add(arrived[:, :, 3 * BLOCK :])
    head_shape = (group_count, tokens_dev, head_width)
    attended_heads = outputs[0].reshape(head_shape)
    d_query_heads = outputs[1].reshape(head_shape)
    d_key_heads = own_grad[0].reshape(head_shape).astype(jnp.bfloat16)
    d_value_heads = own_grad[1].reshape(head_shape).astype(jnp.bfloat16)
    returned = (
        lax.all_to_all(attended_heads, "grp", split_axis=0, concat_axis=2, tiled=True),
        lax.all_to_all(d_query_heads, "grp", split_axis=0, concat_axis=2, tiled=True),
        lax.all_to_all(d_key_heads, "grp", split_axis=0, concat_axis=2, tiled=True),
        lax.all_to_all(d_value_heads, "grp", split_axis=0, concat_axis=2, tiled=True),
    )
    return (
        returned[0].reshape(tokens_dev, width),
        returned[1].reshape(tokens_dev, width),
        returned[2].reshape(tokens_dev, width),
        returned[3].reshape(tokens_dev, width),
    )


MESH = pl.DeviceIdType.MESH
F32 = jnp.float32
BF16 = jnp.bfloat16
LANES = 128


def contract(left, right, dims):
    return lax.dot_general(left, right, (dims, ((), ())), preferred_element_type=F32)


def fused_kernel(
    groups, columns, global_ref, q_ref, k_ref, v_ref, g_ref,
    att_ref, dq_ref, dk_ref, dv_ref,
    qg, kv, side, cand, piece, glob, dsum, dside, dside_in, dg_out, dg_in, dg_sum,
    att_out, dq_out, dk_out, dv_out,
    own_sem, kv_recv, qg_recv, side_recv, ga_recv, gb_recv, ds_recv, da_recv, db_recv,
    in_send, side_send, glob_send, ds_send, out_send, out_recv, keep_sem,
):
    h = lax.axis_index("grp")
    c = lax.axis_index("seq")
    rows, width = q_ref.shape
    share = width // groups
    strip = rows // columns
    pairs = share // LANES

    def rows_of(index):
        return pl.ds(pl.multiple_of(index * strip, strip), strip)

    def remote(src, dst, send, recv, device):
        return pltpu.make_async_remote_copy(
            src_ref=src, dst_ref=dst, send_sem=send, recv_sem=recv,
            device_id=device, device_id_type=MESH,
        )

    def settle(ref, sem):
        pltpu.make_async_copy(ref, ref, sem).wait()

    right = lax.rem(c + 1, columns)
    left = lax.rem(c + columns - 1, columns)

    barrier = pltpu.get_barrier_semaphore()
    for d in range(1, groups):
        pl.semaphore_signal(
            barrier, inc=1, device_id=(lax.rem(h + d, groups), c), device_id_type=MESH
        )
    for e in range(1, columns):
        pl.semaphore_signal(
            barrier, inc=1, device_id=(h, lax.rem(c + e, columns)), device_id_type=MESH
        )

    def lanes_of(index, pair):
        return pl.ds(pl.multiple_of(index * share + pair * LANES, LANES), LANES)

    own = []
    for pair in range(pairs):
        for kind, (refs, buf) in enumerate((((k_ref, v_ref), kv), ((q_ref, g_ref), qg))):
            for a, ref in enumerate(refs):
                own.append(
                    pltpu.make_async_copy(
                        ref.at[:, lanes_of(h, pair)], buf.at[pair, a, h], own_sem.at[kind, pair]
                    )
                )
    for copy in own:
        copy.start()
    pl.semaphore_wait(barrier, groups + columns - 2)

    def send_in(kind, pair):
        refs, buf = (((k_ref, v_ref), kv), ((q_ref, g_ref), qg))[kind]
        for d in range(1, groups):
            target = lax.rem(h + d, groups)
            arrival = (kv_recv, qg_recv)[kind].at[pair, d - 1]
            for a, ref in enumerate(refs):
                remote(
                    ref.at[:, lanes_of(target, pair)], buf.at[pair, a, h],
                    in_send.at[kind], arrival, (target, c),
                ).start()

    def send_sides(pair, d):
        segment = lax.rem(h + groups - d, groups)
        for way, to in ((0, right), (1, left)):
            remote(
                kv.at[pair, :, segment], side.at[pair, way, :, segment],
                side_send.at[0], side_recv.at[pair], (h, to),
            ).start()

    def forward(pair, between, held=()):
        settle(kv.at[pair, :, h], own_sem.at[0, pair])
        if 0 not in held:
            send_sides(pair, 0)
        for d in range(1, groups):
            settle(kv.at[pair, :, lax.rem(h + groups - d, groups)], kv_recv.at[pair, d - 1])
            if d not in held:
                send_sides(pair, d)
            if d in between:
                between[d]()
        offer(pair)
        for d in held:
            send_sides(pair, d)

    seg_of = [lax.div(global_ref[w], columns) for w in range(GLOBALS)]
    col_of = [lax.rem(global_ref[w], columns) for w in range(GLOBALS)]

    def offer(pair):
        for w in range(GLOBALS):
            for a in range(2):
                chosen = kv[pair, a, 0]
                for t in range(1, groups):
                    chosen = jnp.where(seg_of[w] == t, kv[pair, a, t], chosen)
                cand[pair, 2 * w + a] = chosen
        for e in range(1, columns):
            to = lax.rem(c + e, columns)
            remote(
                cand.at[pair, :, rows_of(to), :], piece.at[pair, c],
                glob_send.at[0], ga_recv.at[pair], (h, to),
            ).start()
        piece[pair, c] = cand[pair, :, rows_of(c), :]

    def choose(pair):
        settle(piece.at[pair, pl.ds(0, columns - 1)], ga_recv.at[pair])
        for w in range(GLOBALS):
            for a in range(2):
                chosen = piece[pair, 0, 2 * w + a]
                for e in range(1, columns):
                    chosen = jnp.where(col_of[w] == e, piece[pair, e, 2 * w + a], chosen)
                glob[pair, 2 * w + a, rows_of(c), :] = chosen
        for e in range(1, columns):
            to = lax.rem(c + e, columns)
            remote(
                glob.at[pair, :, rows_of(c), :], glob.at[pair, :, rows_of(c), :],
                glob_send.at[1], gb_recv.at[pair], (h, to),
            ).start()

    lane = lax.broadcasted_iota(jnp.int32, (rows, LANES), 1)
    factor = 1.0 / math.sqrt(HEAD_DIM)
    last = groups * columns - 1

    def stacked(block):
        zero = jnp.zeros_like(block)
        low = jnp.where(lane < HEAD_DIM, block, zero)
        high = jnp.where(lane < HEAD_DIM, zero, block)
        return jnp.concatenate([low, high], axis=0)

    def picked(wide):
        return jnp.concatenate(
            [wide[:HEAD_DIM, :rows], wide[HEAD_DIM:, rows:]], axis=0
        ).T

    outgoing = ((att_out, att_ref), (dq_out, dq_ref), (dk_out, dk_ref), (dv_out, dv_ref))

    def send_out(pair, i, first):
        segment = lax.rem(h + i + 1, groups)
        for buf, ref in outgoing[first : first + 2]:
            if i < groups - 1:
                remote(
                    buf.at[pair, segment], ref.at[:, lanes_of(h, pair)],
                    out_send.at[first // 2], out_recv.at[first // 2], (segment, c),
                ).start()
            else:
                pltpu.make_async_copy(
                    buf.at[pair, h], ref.at[:, lanes_of(h, pair)], keep_sem.at[0]
                ).start()

    def send_dsides(pair, i):
        for way, to in ((0, left), (1, right)):
            remote(
                dside.at[pair, way, :, i], dside_in.at[pair, way, :, i],
                ds_send.at[0], ds_recv.at[pair], (h, to),
            ).start()

    at_first = jnp.where(c == 0, 1, 0)
    at_last = jnp.where(c == columns - 1, 1, 0)
    dense = (groups + GLOBALS) * rows

    def unit(pair, i):
        segment = lax.rem(h + i + 1, groups)
        block = segment * columns + c
        before = lax.rem(segment + groups - at_first, groups)
        after = lax.rem(segment + at_last, groups)

        def listed(a):
            return jnp.concatenate(
                [kv[pair, a, t] for t in range(groups)]
                + [glob[pair, 2 * w + a] for w in range(GLOBALS)]
                + [side[pair, 0, a, before], side[pair, 1, a, after]],
                axis=0,
            )

        key = listed(0)
        value = listed(1)
        query = stacked(qg[pair, 0, segment] * jnp.asarray(factor, BF16))
        grad = stacked(qg[pair, 1, segment])
        scores = contract(key, query, ((1,), (1,)))
        scores = jnp.concatenate(
            [
                scores[:dense],
                jnp.where(block > 0, scores[dense : dense + rows], -1e30),
                jnp.where(block < last, scores[dense + rows :], -1e30),
            ],
            axis=0,
        )
        raised = jnp.exp(scores - jnp.max(scores, axis=0, keepdims=True))
        prob = raised * (1.0 / jnp.sum(raised, axis=0, keepdims=True))
        half = prob.astype(BF16)
        d_prob = contract(value, grad, ((1,), (1,)))
        result = contract(value, half, ((0,), (0,)))
        row_dot = jnp.sum(prob * d_prob, axis=0, keepdims=True)
        d_scores = (prob * (d_prob - row_dot)).astype(BF16)
        d_query = contract(key, d_scores, ((0,), (0,))) * factor
        d_value = contract(half, grad, ((1,), (0,)))
        d_key = contract(d_scores, query, ((1,), (0,)))
        att_out[pair, segment] = picked(result).astype(BF16)
        dq_out[pair, segment] = picked(d_query).astype(BF16)
        return d_key, d_value

    def ready(pair):
        settle(side.at[pair], side_recv.at[pair])
        settle(glob.at[pair, :, pl.ds(0, rows - strip)], gb_recv.at[pair])
        settle(qg.at[pair, :, h], own_sem.at[1, pair])

    def run(pair, i, closing=False):
        segment = lax.rem(h + i + 1, groups)
        if i < groups - 1:
            settle(qg.at[pair, :, segment], qg_recv.at[pair, groups - 2 - i])
        grads = unit(pair, i)
        for a in range(2):
            if i == groups - 1:
                dsum[pair, a] = grads[a][:dense]
            else:
                dsum[pair, a] += grads[a][:dense]
            dside[pair, 0, a, i] = grads[a][dense : dense + rows].astype(BF16)
            dside[pair, 1, a, i] = grads[a][dense + rows :].astype(BF16)
        if closing:
            scatter(pair)
        send_dsides(pair, i)
        send_out(pair, i, 0)

    def scatter(pair):
        for w in range(GLOBALS):
            for a in range(2):
                start = (groups + w) * rows
                dg_out[pair, 2 * w + a] = dsum[pair, a, start : start + rows].astype(BF16)
        for e in range(1, columns):
            to = lax.rem(c + e, columns)
            remote(
                dg_out.at[pair, :, rows_of(to), :], dg_in.at[pair, c],
                glob_send.at[2], da_recv.at[pair], (h, to),
            ).start()
        dg_in[pair, c] = dg_out[pair, :, rows_of(c), :]

    def gather(pair):
        settle(dg_in.at[pair, pl.ds(0, columns - 1)], da_recv.at[pair])
        total = dg_in[pair, 0].astype(F32)
        for e in range(1, columns):
            total = total + dg_in[pair, e].astype(F32)
        dg_sum[pair, :, rows_of(c), :] = total.astype(BF16)
        for e in range(1, columns):
            to = lax.rem(c + e, columns)
            remote(
                dg_sum.at[pair, :, rows_of(c), :], dg_sum.at[pair, :, rows_of(c), :],
                glob_send.at[3], db_recv.at[pair], (h, to),
            ).start()

    def finish(pair):
        settle(dside_in.at[pair], ds_recv.at[pair])
        settle(dg_sum.at[pair, :, pl.ds(0, rows - strip)], db_recv.at[pair])
        for i in range(groups):
            segment = lax.rem(h + i + 1, groups)
            low = lax.rem(i + at_last, groups)
            high = lax.rem(i + groups - at_first, groups)
            span = pl.ds(pl.multiple_of(segment * rows, rows), rows)
            for a, buf in enumerate((dk_out, dv_out)):
                whole = dsum[pair, a, span]
                whole += dside_in[pair, 0, a, low].astype(F32)
                whole += dside_in[pair, 1, a, high].astype(F32)
                for w in range(GLOBALS):
                    mine = (global_ref[w] == segment * columns + c).astype(F32)
                    whole += dg_sum[pair, 2 * w + a].astype(F32) * mine
                buf[pair, segment] = whole.astype(BF16)
            send_out(pair, i, 2)

    def then(step, *rest):
        return functools.partial(step, *rest)

    send_in(0, 0)
    forward(0, {2: then(send_in, 0, 1)}, (2, 3))
    send_in(1, 0)
    choose(0)
    forward(1, {1: then(send_in, 1, 1)}, range(groups))
    ready(0)
    run(0, 3)
    run(0, 2)
    choose(1)
    run(0, 1)
    run(0, 0, True)
    ready(1)
    run(1, 3)
    run(1, 2)
    gather(0)
    run(1, 1)
    run(1, 0, True)
    finish(0)
    gather(1)
    finish(1)

    shares = pl.ds(0, groups - 1)
    for n in range(2):
        settle(kv.at[:, :, shares], in_send.at[n])
        settle(kv.at[:, :, shares], out_send.at[n])
        settle(kv.at[:, :, shares], out_recv.at[n])
    settle(side, side_send.at[0])
    settle(dside, ds_send.at[0])
    for n in range(2):
        settle(piece.at[:, pl.ds(0, columns - 1)], glob_send.at[2 * n])
        settle(glob.at[:, :, pl.ds(0, rows - strip)], glob_send.at[2 * n + 1])
    settle(kv.at[:, :, pl.ds(0, 2)], keep_sem.at[0])


def fused(groups, columns, query, keys, values, d_out, rand_blocks, global_blocks):
    rows, width = query.shape
    share = width // groups
    strip = rows // columns
    half = functools.partial(pltpu.VMEM, dtype=BF16)
    full = functools.partial(pltpu.VMEM, dtype=F32)
    dma = pltpu.SemaphoreType.DMA
    pairs = share // LANES
    tile = (rows, LANES)
    scratch = [
        half((pairs, 2, groups, *tile)),
        half((pairs, 2, groups, *tile)),
        half((pairs, 2, 2, groups, *tile)),
        half((pairs, 2 * GLOBALS, *tile)),
        half((pairs, columns, 2 * GLOBALS, strip, LANES)),
        half((pairs, 2 * GLOBALS, *tile)),
        full((pairs, 2, (groups + GLOBALS) * rows, LANES)),
        half((pairs, 2, 2, groups, *tile)),
        half((pairs, 2, 2, groups, *tile)),
        half((pairs, 2 * GLOBALS, *tile)),
        half((pairs, columns, 2 * GLOBALS, strip, LANES)),
        half((pairs, 2 * GLOBALS, *tile)),
    ] + [half((pairs, groups, *tile))] * 4
    scratch += [dma((2, pairs))] + [dma((pairs, groups - 1))] * 2 + [dma((pairs,))] * 6
    scratch += [dma((2,)), dma((1,)), dma((4,)), dma((1,)), dma((2,)), dma((2,)), dma((1,))]
    hbm = pl.BlockSpec(memory_space=pltpu.HBM)
    return pl.pallas_call(
        functools.partial(fused_kernel, groups, columns),
        out_shape=[jax.ShapeDtypeStruct((rows, width), BF16)] * 4,
        in_specs=[pl.BlockSpec(memory_space=pltpu.SMEM)] + [hbm] * 4,
        out_specs=[hbm] * 4,
        scratch_shapes=scratch,
        compiler_params=pltpu.CompilerParams(
            collective_id=0, has_side_effects=True, vmem_limit_bytes=63 * 2**20
        ),
    )(global_blocks, query, keys, values, d_out)


CHUNKS = 4


def relay_kernel(*refs):
    count = (len(refs) - 3) // 2
    sources, targets = refs[:count], refs[count : 2 * count]
    held, in_sem, out_sem = refs[2 * count :]
    rows = held.shape[1] // CHUNKS
    for part in range(CHUNKS):
        at = pl.ds(part * rows, rows)
        for n in range(count):
            pltpu.make_async_copy(sources[n].at[at], held.at[n, at], in_sem.at[part]).start()
    for part in range(CHUNKS):
        at = pl.ds(part * rows, rows)
        pltpu.make_async_copy(held.at[:, at], held.at[:, at], in_sem.at[part]).wait()
        for n in range(count):
            pltpu.make_async_copy(held.at[n, at], targets[n].at[at], out_sem.at[0]).start()
    pltpu.make_async_copy(held, held, out_sem.at[0]).wait()


def relay(*arrays):
    hbm = pl.BlockSpec(memory_space=pltpu.HBM)
    count = len(arrays)
    return pl.pallas_call(
        relay_kernel,
        out_shape=[jax.ShapeDtypeStruct(a.shape, a.dtype) for a in arrays],
        in_specs=[hbm] * count,
        out_specs=[hbm] * count,
        scratch_shapes=[
            pltpu.VMEM((count, *arrays[0].shape), arrays[0].dtype),
            pltpu.SemaphoreType.DMA((CHUNKS,)),
            pltpu.SemaphoreType.DMA((1,)),
        ],
    )(*arrays)


def solution(mesh):
    in_specs = (
        P(("grp", "seq"), None),
        P(("grp", "seq"), None),
        P(("grp", "seq"), None),
        P(("grp", "seq"), None),
        P(),
        P(),
    )
    out_specs = (
        P(("grp", "seq"), None),
        P(("grp", "seq"), None),
        P(("grp", "seq"), None),
        P(("grp", "seq"), None),
    )
    groups, columns = mesh.shape["grp"], mesh.shape["seq"]

    def run(query, *rest):
        rows, width = query.shape
        whole_column = rows == BLOCK and groups - 1 == RANDOMS and groups % 2 == 0
        if whole_column and rows % (16 * columns) == 0 and width == 2 * groups * LANES:
            return relay(*fused(groups, columns, query, *rest))
        return body(query, *rest)

    return jax.shard_map(run, mesh=mesh, in_specs=in_specs, out_specs=out_specs, check_vma=False)
```

```python
import functools
import math

import jax
import jax.numpy as jnp
from jax import lax
from jax.experimental import pallas as pl
from jax.experimental.pallas import tpu as pltpu
from jax.sharding import PartitionSpec as P

HEAD_DIM = 64
BLOCK = 128
GLOBALS = 2
RANDOMS = 3
KEYS = 8


def extended(block, sides, width, periodic):
    for axis, dim in sides:
        count = lax.axis_size(axis)
        forward = [(i, i + 1) for i in range(count - 1)]
        if periodic:
            forward.append((count - 1, 0))
        backward = [(target, source) for source, target in forward]
        low = lax.ppermute(
            lax.slice_in_dim(block, block.shape[dim] - width, None, axis=dim), axis, forward
        )
        high = lax.ppermute(lax.slice_in_dim(block, 0, width, axis=dim), axis, backward)
        block = jnp.concatenate([low, block, high], axis=dim)
    return block


def broadcast(block, axis, source):
    block = jnp.where(lax.axis_index(axis) == source, block, jnp.zeros_like(block))
    return lax.psum(block, axis)


def attend_blocks(queries, key_rows, value_rows, grad_rows, key_valid):
    factor = 1.0 / math.sqrt(queries.shape[-1])
    scores = (
        jnp.einsum("nqhe,njkhe->nhqjk", queries, key_rows, preferred_element_type=jnp.float32)
        * factor
    )
    scores = jnp.where(key_valid[:, None, None, :, None], scores, -1e30)
    row_max = jnp.max(scores, axis=(3, 4), keepdims=True)
    raised = jnp.exp(scores - row_max)
    attn_prob = raised / jnp.sum(raised, axis=(3, 4), keepdims=True)
    prob_half = attn_prob.astype(jnp.bfloat16)
    result = jnp.einsum(
        "nhqjk,njkhe->nqhe", prob_half, value_rows, preferred_element_type=jnp.float32
    )
    d_prob = jnp.einsum(
        "nqhe,njkhe->nhqjk", grad_rows, value_rows, preferred_element_type=jnp.float32
    )
    row_dot = jnp.sum(attn_prob * d_prob, axis=(3, 4), keepdims=True)
    d_scores = (attn_prob * (d_prob - row_dot) * factor).astype(jnp.bfloat16)
    d_query = jnp.einsum(
        "nhqjk,njkhe->nqhe", d_scores, key_rows, preferred_element_type=jnp.float32
    )
    d_keys = jnp.einsum("nhqjk,nqhe->njkhe", d_scores, queries, preferred_element_type=jnp.float32)
    d_values = jnp.einsum(
        "nhqjk,nqhe->njkhe", prob_half, grad_rows, preferred_element_type=jnp.float32
    )
    return (result, d_query, d_keys, d_values)


def body(query, keys, values, d_out, rand_blocks, global_blocks):
    group_count = lax.axis_size("grp")
    column_count = lax.axis_size("seq")
    column = lax.axis_index("seq")
    tokens_dev = query.shape[0]
    width = query.shape[1]
    local_blocks = tokens_dev // BLOCK
    head_width = width // group_count
    heads_here = head_width // HEAD_DIM
    block_total = group_count * column_count * local_blocks
    segment_span = column_count * local_blocks
    stride = local_blocks + 2
    count = group_count * local_blocks
    per_step = 4
    steps_count = count // per_step
    stacked = jnp.stack([keys, values])
    widened = extended(stacked, ((("grp", "seq"), 1),), BLOCK, False)
    key_send = widened[0][None]
    value_send = widened[1][None]
    query_heads, grad_heads, key_heads, value_heads = (
        lax.all_to_all(
            query.reshape(1, tokens_dev, width), "grp", split_axis=2, concat_axis=0, tiled=True
        ),
        lax.all_to_all(
            d_out.reshape(1, tokens_dev, width), "grp", split_axis=2, concat_axis=0, tiled=True
        ),
        lax.all_to_all(key_send, "grp", split_axis=2, concat_axis=0, tiled=True),
        lax.all_to_all(value_send, "grp", split_axis=2, concat_axis=0, tiled=True),
    )
    ext_pair = jnp.stack([key_heads, value_heads]).reshape(
        2, group_count * stride, BLOCK, head_width
    )
    global_device = global_blocks // local_blocks
    global_segment = global_device // column_count
    global_column = global_device % column_count
    global_local = global_blocks % local_blocks
    global_rows = global_segment * stride + global_local + 1
    fetched = []
    for which in range(GLOBALS):
        fetched.append(broadcast(ext_pair[:, global_rows[which]], "seq", global_column[which]))
    global_pair = jnp.stack(fetched, axis=1)
    segment_of = jnp.repeat(jnp.arange(group_count, dtype=jnp.int32), local_blocks)
    local_of = jnp.tile(jnp.arange(local_blocks, dtype=jnp.int32), group_count)
    query_ids = (segment_of * column_count + column) * local_blocks + local_of
    rand_ids = jnp.take(rand_blocks, query_ids, axis=0)
    rand_rows = rand_ids // segment_span * stride + rand_ids % local_blocks + 1
    window_rows = (segment_of * stride + local_of)[:, None] + jnp.arange(3, dtype=jnp.int32)[
        None, :
    ]
    key_table = jnp.concatenate([window_rows, rand_rows], axis=1)
    key_valid = jnp.concatenate(
        [
            (query_ids > 0)[:, None],
            jnp.ones((count, 1), dtype=jnp.bool_),
            (query_ids < block_total - 1)[:, None],
            jnp.ones((count, GLOBALS + RANDOMS), dtype=jnp.bool_),
        ],
        axis=1,
    )
    query_steps = query_heads.reshape(steps_count, per_step, BLOCK, heads_here, HEAD_DIM)
    grad_steps = grad_heads.reshape(steps_count, per_step, BLOCK, heads_here, HEAD_DIM)
    table_steps = key_table.reshape(steps_count, per_step, 3 + RANDOMS)
    valid_steps = key_valid.reshape(steps_count, per_step, KEYS)
    global_spread = jnp.broadcast_to(
        global_pair[:, None], (2, per_step, GLOBALS, BLOCK, head_width)
    )

    def advance(totals, packed):
        ext_total, global_total = totals
        query_part, grad_part, rows_part, valid_part = packed
        taken = jnp.stack(
            [
                lax.dynamic_index_in_dim(ext_pair, row, axis=1, keepdims=False)
                for row in rows_part.reshape(-1)
            ],
            axis=1,
        ).reshape(2, per_step, 3 + RANDOMS, BLOCK, head_width)
        gathered = jnp.concatenate([taken[:, :, :3], global_spread, taken[:, :, 3:]], axis=2)
        gathered = gathered.reshape(2, per_step, KEYS, BLOCK, heads_here, HEAD_DIM)
        result, d_query, d_keys, d_values = attend_blocks(
            query_part, gathered[0], gathered[1], grad_part, valid_part
        )
        d_pair = jnp.stack([d_keys, d_values]).reshape(2, per_step, KEYS, BLOCK, head_width)
        spread_back = jnp.concatenate([d_pair[:, :, :3], d_pair[:, :, 3 + GLOBALS :]], axis=2)
        spread_back = spread_back.reshape(2, per_step * (3 + RANDOMS), BLOCK, head_width)
        ext_total = ext_total.at[:, rows_part.reshape(-1)].add(spread_back)
        global_total = global_total + jnp.sum(d_pair[:, :, 3 : 3 + GLOBALS], axis=1)
        return (
            (ext_total, global_total),
            (result.astype(jnp.bfloat16), d_query.astype(jnp.bfloat16)),
        )

    start_totals = (
        jnp.zeros((2, group_count * stride, BLOCK, head_width), jnp.float32),
        jnp.zeros((2, GLOBALS, BLOCK, head_width), jnp.float32),
    )
    totals, outputs = lax.scan(
        advance, start_totals, (query_steps, grad_steps, table_steps, valid_steps)
    )
    ext_total = totals[0].reshape(2, group_count, stride, BLOCK, head_width)
    global_sum = lax.psum(totals[1], "seq")
    own_grad = ext_total[:, :, 1 : local_blocks + 1]
    for which in range(GLOBALS):
        addend = jnp.where(column == global_column[which], global_sum[:, which], 0.0)
        own_grad = own_grad.at[:, global_segment[which], global_local[which]].add(addend)
    send_left = ext_total[:, :, 0]
    send_right = ext_total[:, :, local_blocks + 1]
    empty_edge = jnp.zeros_like(send_left[:, :1])
    send_left = jnp.where(
        column == 0, jnp.concatenate([send_left[:, 1:], empty_edge], axis=1), send_left
    )
    send_right = jnp.where(
        column == column_count - 1,
        jnp.concatenate([empty_edge, send_right[:, :-1]], axis=1),
        send_right,
    )
    edges = jnp.concatenate([send_left, send_right], axis=2)
    arrived = extended(edges, (("seq", 2),), BLOCK, True)
    own_grad = own_grad.at[:, :, 0].add(arrived[:, :, :BLOCK])
    own_grad = own_grad.at[:, :, local_blocks - 1].add(arrived[:, :, 3 * BLOCK :])
    head_shape = (group_count, tokens_dev, head_width)
    attended_heads = outputs[0].reshape(head_shape)
    d_query_heads = outputs[1].reshape(head_shape)
    d_key_heads = own_grad[0].reshape(head_shape).astype(jnp.bfloat16)
    d_value_heads = own_grad[1].reshape(head_shape).astype(jnp.bfloat16)
    returned = (
        lax.all_to_all(attended_heads, "grp", split_axis=0, concat_axis=2, tiled=True),
        lax.all_to_all(d_query_heads, "grp", split_axis=0, concat_axis=2, tiled=True),
        lax.all_to_all(d_key_heads, "grp", split_axis=0, concat_axis=2, tiled=True),
        lax.all_to_all(d_value_heads, "grp", split_axis=0, concat_axis=2, tiled=True),
    )
    return (
        returned[0].reshape(tokens_dev, width),
        returned[1].reshape(tokens_dev, width),
        returned[2].reshape(tokens_dev, width),
        returned[3].reshape(tokens_dev, width),
    )


MESH = pl.DeviceIdType.MESH
F32 = jnp.float32
BF16 = jnp.bfloat16
LANES = 128


def contract(left, right, dims):
    return lax.dot_general(left, right, (dims, ((), ())), preferred_element_type=F32)


def fused_kernel(
    groups, columns, global_ref, q_ref, k_ref, v_ref, g_ref,
    att_ref, dq_ref, dk_ref, dv_ref,
    qg, kv, side, cand, piece, glob, dsum, dside, dside_in, dg_out, dg_in, dg_sum,
    att_out, dq_out, dk_out, dv_out,
    own_sem, kv_recv, qg_recv, side_recv, ga_recv, gb_recv, ds_recv, da_recv, db_recv,
    in_send, side_send, glob_send, ds_send, out_send, out_recv, keep_sem,
):
    h = lax.axis_index("grp")
    c = lax.axis_index("seq")
    rows, width = q_ref.shape
    share = width // groups
    strip = rows // columns
    pairs = share // LANES

    def rows_of(index):
        return pl.ds(pl.multiple_of(index * strip, strip), strip)

    def remote(src, dst, send, recv, device):
        return pltpu.make_async_remote_copy(
            src_ref=src, dst_ref=dst, send_sem=send, recv_sem=recv,
            device_id=device, device_id_type=MESH,
        )

    def settle(ref, sem):
        pltpu.make_async_copy(ref, ref, sem).wait()

    right = lax.rem(c + 1, columns)
    left = lax.rem(c + columns - 1, columns)

    barrier = pltpu.get_barrier_semaphore()
    for d in range(1, groups):
        pl.semaphore_signal(
            barrier, inc=1, device_id=(lax.rem(h + d, groups), c), device_id_type=MESH
        )
    for e in range(1, columns):
        pl.semaphore_signal(
            barrier, inc=1, device_id=(h, lax.rem(c + e, columns)), device_id_type=MESH
        )

    def lanes_of(index, pair):
        return pl.ds(pl.multiple_of(index * share + pair * LANES, LANES), LANES)

    own = []
    for pair in range(pairs):
        for kind, (refs, buf) in enumerate((((k_ref, v_ref), kv), ((q_ref, g_ref), qg))):
            for a, ref in enumerate(refs):
                own.append(
                    pltpu.make_async_copy(
                        ref.at[:, lanes_of(h, pair)], buf.at[pair, a, h], own_sem.at[kind, pair]
                    )
                )
    for copy in own:
        copy.start()
    pl.semaphore_wait(barrier, groups + columns - 2)

    def send_in(kind, pair):
        refs, buf = (((k_ref, v_ref), kv), ((q_ref, g_ref), qg))[kind]
        for d in range(1, groups):
            target = lax.rem(h + d, groups)
            arrival = (kv_recv, qg_recv)[kind].at[pair, d - 1]
            for a, ref in enumerate(refs):
                remote(
                    ref.at[:, lanes_of(target, pair)], buf.at[pair, a, h],
                    in_send.at[kind], arrival, (target, c),
                ).start()

    def send_sides(pair, d):
        segment = lax.rem(h + groups - d, groups)
        for way, to in ((0, right), (1, left)):
            remote(
                kv.at[pair, :, segment], side.at[pair, way, :, segment],
                side_send.at[0], side_recv.at[pair], (h, to),
            ).start()

    def forward(pair, between, held=()):
        settle(kv.at[pair, :, h], own_sem.at[0, pair])
        if 0 not in held:
            send_sides(pair, 0)
        for d in range(1, groups):
            settle(kv.at[pair, :, lax.rem(h + groups - d, groups)], kv_recv.at[pair, d - 1])
            if d not in held:
                send_sides(pair, d)
            if d in between:
                between[d]()
        offer(pair)
        for d in held:
            send_sides(pair, d)

    seg_of = [lax.div(global_ref[w], columns) for w in range(GLOBALS)]
    col_of = [lax.rem(global_ref[w], columns) for w in range(GLOBALS)]

    def offer(pair):
        for w in range(GLOBALS):
            for a in range(2):
                chosen = kv[pair, a, 0]
                for t in range(1, groups):
                    chosen = jnp.where(seg_of[w] == t, kv[pair, a, t], chosen)
                cand[pair, 2 * w + a] = chosen
        for e in range(1, columns):
            to = lax.rem(c + e, columns)
            remote(
                cand.at[pair, :, rows_of(to), :], piece.at[pair, c],
                glob_send.at[0], ga_recv.at[pair], (h, to),
            ).start()
        piece[pair, c] = cand[pair, :, rows_of(c), :]

    def choose(pair):
        settle(piece.at[pair, pl.ds(0, columns - 1)], ga_recv.at[pair])
        for w in range(GLOBALS):
            for a in range(2):
                chosen = piece[pair, 0, 2 * w + a]
                for e in range(1, columns):
                    chosen = jnp.where(col_of[w] == e, piece[pair, e, 2 * w + a], chosen)
                glob[pair, 2 * w + a, rows_of(c), :] = chosen
        for e in range(1, columns):
            to = lax.rem(c + e, columns)
            remote(
                glob.at[pair, :, rows_of(c), :], glob.at[pair, :, rows_of(c), :],
                glob_send.at[1], gb_recv.at[pair], (h, to),
            ).start()

    lane = lax.broadcasted_iota(jnp.int32, (rows, LANES), 1)
    factor = 1.0 / math.sqrt(HEAD_DIM)
    last = groups * columns - 1

    def stacked(block):
        zero = jnp.zeros_like(block)
        low = jnp.where(lane < HEAD_DIM, block, zero)
        high = jnp.where(lane < HEAD_DIM, zero, block)
        return jnp.concatenate([low, high], axis=0)

    def picked(wide):
        return jnp.concatenate(
            [wide[:HEAD_DIM, :rows], wide[HEAD_DIM:, rows:]], axis=0
        ).T

    outgoing = ((att_out, att_ref), (dq_out, dq_ref), (dk_out, dk_ref), (dv_out, dv_ref))

    def send_out(pair, i, first):
        segment = lax.rem(h + i + 1, groups)
        for buf, ref in outgoing[first : first + 2]:
            if i < groups - 1:
                remote(
                    buf.at[pair, segment], ref.at[:, lanes_of(h, pair)],
                    out_send.at[first // 2], out_recv.at[first // 2], (segment, c),
                ).start()
            else:
                pltpu.make_async_copy(
                    buf.at[pair, h], ref.at[:, lanes_of(h, pair)], keep_sem.at[0]
                ).start()

    def send_dsides(pair, i):
        for way, to in ((0, left), (1, right)):
            remote(
                dside.at[pair, way, :, i], dside_in.at[pair, way, :, i],
                ds_send.at[0], ds_recv.at[pair], (h, to),
            ).start()

    at_first = jnp.where(c == 0, 1, 0)
    at_last = jnp.where(c == columns - 1, 1, 0)
    dense = (groups + GLOBALS) * rows

    def unit(pair, i):
        segment = lax.rem(h + i + 1, groups)
        block = segment * columns + c
        before = lax.rem(segment + groups - at_first, groups)
        after = lax.rem(segment + at_last, groups)

        def listed(a):
            return jnp.concatenate(
                [kv[pair, a, t] for t in range(groups)]
                + [glob[pair, 2 * w + a] for w in range(GLOBALS)]
                + [side[pair, 0, a, before], side[pair, 1, a, after]],
                axis=0,
            )

        key = listed(0)
        value = listed(1)
        query = stacked(qg[pair, 0, segment] * jnp.asarray(factor, BF16))
        grad = stacked(qg[pair, 1, segment])
        scores = contract(key, query, ((1,), (1,)))
        scores = jnp.concatenate(
            [
                scores[:dense],
                jnp.where(block > 0, scores[dense : dense + rows], -1e30),
                jnp.where(block < last, scores[dense + rows :], -1e30),
            ],
            axis=0,
        )
        raised = jnp.exp(scores - jnp.max(scores, axis=0, keepdims=True))
        prob = raised * (1.0 / jnp.sum(raised, axis=0, keepdims=True))
        half = prob.astype(BF16)
        d_prob = contract(value, grad, ((1,), (1,)))
        result = contract(value, half, ((0,), (0,)))
        row_dot = jnp.sum(prob * d_prob, axis=0, keepdims=True)
        d_scores = (prob * (d_prob - row_dot)).astype(BF16)
        d_query = contract(key, d_scores, ((0,), (0,))) * factor
        d_value = contract(half, grad, ((1,), (0,)))
        d_key = contract(d_scores, query, ((1,), (0,)))
        att_out[pair, segment] = picked(result).astype(BF16)
        dq_out[pair, segment] = picked(d_query).astype(BF16)
        return d_key, d_value

    def ready(pair):
        settle(side.at[pair], side_recv.at[pair])
        settle(glob.at[pair, :, pl.ds(0, rows - strip)], gb_recv.at[pair])
        settle(qg.at[pair, :, h], own_sem.at[1, pair])

    def run(pair, i, closing=False, share_now=True):
        segment = lax.rem(h + i + 1, groups)
        if i < groups - 1:
            settle(qg.at[pair, :, segment], qg_recv.at[pair, groups - 2 - i])
        grads = unit(pair, i)
        for a in range(2):
            if i == groups - 1:
                dsum[pair, a] = grads[a][:dense]
            else:
                dsum[pair, a] += grads[a][:dense]
            dside[pair, 0, a, i] = grads[a][dense : dense + rows].astype(BF16)
            dside[pair, 1, a, i] = grads[a][dense + rows :].astype(BF16)
        if closing:
            scatter(pair)
        if share_now:
            send_dsides(pair, i)
        send_out(pair, i, 0)

    def scatter(pair):
        for w in range(GLOBALS):
            for a in range(2):
                start = (groups + w) * rows
                dg_out[pair, 2 * w + a] = dsum[pair, a, start : start + rows].astype(BF16)
        for e in range(1, columns):
            to = lax.rem(c + e, columns)
            remote(
                dg_out.at[pair, :, rows_of(to), :], dg_in.at[pair, c],
                glob_send.at[2], da_recv.at[pair], (h, to),
            ).start()
        dg_in[pair, c] = dg_out[pair, :, rows_of(c), :]

    def gather(pair):
        settle(dg_in.at[pair, pl.ds(0, columns - 1)], da_recv.at[pair])
        total = dg_in[pair, 0].astype(F32)
        for e in range(1, columns):
            total = total + dg_in[pair, e].astype(F32)
        dg_sum[pair, :, rows_of(c), :] = total.astype(BF16)
        for e in range(1, columns):
            to = lax.rem(c + e, columns)
            remote(
                dg_sum.at[pair, :, rows_of(c), :], dg_sum.at[pair, :, rows_of(c), :],
                glob_send.at[3], db_recv.at[pair], (h, to),
            ).start()

    def finish(pair):
        settle(dside_in.at[pair], ds_recv.at[pair])
        settle(dg_sum.at[pair, :, pl.ds(0, rows - strip)], db_recv.at[pair])
        for i in range(groups):
            segment = lax.rem(h + i + 1, groups)
            low = lax.rem(i + at_last, groups)
            high = lax.rem(i + groups - at_first, groups)
            span = pl.ds(pl.multiple_of(segment * rows, rows), rows)
            for a, buf in enumerate((dk_out, dv_out)):
                whole = dsum[pair, a, span]
                whole += dside_in[pair, 0, a, low].astype(F32)
                whole += dside_in[pair, 1, a, high].astype(F32)
                for w in range(GLOBALS):
                    mine = (global_ref[w] == segment * columns + c).astype(F32)
                    whole += dg_sum[pair, 2 * w + a].astype(F32) * mine
                buf[pair, segment] = whole.astype(BF16)
            send_out(pair, i, 2)

    def then(step, *rest):
        return functools.partial(step, *rest)

    send_in(0, 0)
    forward(0, {2: then(send_in, 0, 1)}, (2, 3))
    send_in(1, 0)
    choose(0)
    forward(1, {1: then(send_in, 1, 1)}, range(groups))
    ready(0)
    run(0, 3, False, False)
    choose(1)
    run(0, 2, False, False)
    send_dsides(0, 3)
    run(0, 1, False, False)
    send_dsides(0, 2)
    run(0, 0, True, False)
    ready(1)
    send_dsides(0, 1)
    run(1, 3, False, False)
    send_dsides(0, 0)
    run(1, 2, False, False)
    gather(0)
    send_dsides(1, 3)
    run(1, 1, False, False)
    send_dsides(1, 2)
    run(1, 0, True, False)
    send_dsides(1, 1)
    send_dsides(1, 0)
    finish(0)
    gather(1)
    finish(1)

    shares = pl.ds(0, groups - 1)
    for n in range(2):
        settle(kv.at[:, :, shares], in_send.at[n])
        settle(kv.at[:, :, shares], out_send.at[n])
        settle(kv.at[:, :, shares], out_recv.at[n])
    settle(side, side_send.at[0])
    settle(dside, ds_send.at[0])
    for n in range(2):
        settle(piece.at[:, pl.ds(0, columns - 1)], glob_send.at[2 * n])
        settle(glob.at[:, :, pl.ds(0, rows - strip)], glob_send.at[2 * n + 1])
    settle(kv.at[:, :, pl.ds(0, 2)], keep_sem.at[0])


def fused(groups, columns, query, keys, values, d_out, rand_blocks, global_blocks):
    rows, width = query.shape
    share = width // groups
    strip = rows // columns
    half = functools.partial(pltpu.VMEM, dtype=BF16)
    full = functools.partial(pltpu.VMEM, dtype=F32)
    dma = pltpu.SemaphoreType.DMA
    pairs = share // LANES
    tile = (rows, LANES)
    scratch = [
        half((pairs, 2, groups, *tile)),
        half((pairs, 2, groups, *tile)),
        half((pairs, 2, 2, groups, *tile)),
        half((pairs, 2 * GLOBALS, *tile)),
        half((pairs, columns, 2 * GLOBALS, strip, LANES)),
        half((pairs, 2 * GLOBALS, *tile)),
        full((pairs, 2, (groups + GLOBALS) * rows, LANES)),
        half((pairs, 2, 2, groups, *tile)),
        half((pairs, 2, 2, groups, *tile)),
        half((pairs, 2 * GLOBALS, *tile)),
        half((pairs, columns, 2 * GLOBALS, strip, LANES)),
        half((pairs, 2 * GLOBALS, *tile)),
    ] + [half((pairs, groups, *tile))] * 4
    scratch += [dma((2, pairs))] + [dma((pairs, groups - 1))] * 2 + [dma((pairs,))] * 6
    scratch += [dma((2,)), dma((1,)), dma((4,)), dma((1,)), dma((2,)), dma((2,)), dma((1,))]
    hbm = pl.BlockSpec(memory_space=pltpu.HBM)
    return pl.pallas_call(
        functools.partial(fused_kernel, groups, columns),
        out_shape=[jax.ShapeDtypeStruct((rows, width), BF16)] * 4,
        in_specs=[pl.BlockSpec(memory_space=pltpu.SMEM)] + [hbm] * 4,
        out_specs=[hbm] * 4,
        scratch_shapes=scratch,
        compiler_params=pltpu.CompilerParams(
            collective_id=0, has_side_effects=True, vmem_limit_bytes=63 * 2**20
        ),
    )(global_blocks, query, keys, values, d_out)


CHUNKS = 4


def relay_kernel(*refs):
    count = (len(refs) - 3) // 2
    sources, targets = refs[:count], refs[count : 2 * count]
    held, in_sem, out_sem = refs[2 * count :]
    rows = held.shape[1] // CHUNKS
    for part in range(CHUNKS):
        at = pl.ds(part * rows, rows)
        for n in range(count):
            pltpu.make_async_copy(sources[n].at[at], held.at[n, at], in_sem.at[part]).start()
    for part in range(CHUNKS):
        at = pl.ds(part * rows, rows)
        pltpu.make_async_copy(held.at[:, at], held.at[:, at], in_sem.at[part]).wait()
        for n in range(count):
            pltpu.make_async_copy(held.at[n, at], targets[n].at[at], out_sem.at[0]).start()
    pltpu.make_async_copy(held, held, out_sem.at[0]).wait()


def relay(*arrays):
    hbm = pl.BlockSpec(memory_space=pltpu.HBM)
    count = len(arrays)
    return pl.pallas_call(
        relay_kernel,
        out_shape=[jax.ShapeDtypeStruct(a.shape, a.dtype) for a in arrays],
        in_specs=[hbm] * count,
        out_specs=[hbm] * count,
        scratch_shapes=[
            pltpu.VMEM((count, *arrays[0].shape), arrays[0].dtype),
            pltpu.SemaphoreType.DMA((CHUNKS,)),
            pltpu.SemaphoreType.DMA((1,)),
        ],
    )(*arrays)


def solution(mesh):
    in_specs = (
        P(("grp", "seq"), None),
        P(("grp", "seq"), None),
        P(("grp", "seq"), None),
        P(("grp", "seq"), None),
        P(),
        P(),
    )
    out_specs = (
        P(("grp", "seq"), None),
        P(("grp", "seq"), None),
        P(("grp", "seq"), None),
        P(("grp", "seq"), None),
    )
    groups, columns = mesh.shape["grp"], mesh.shape["seq"]

    def run(query, *rest):
        rows, width = query.shape
        whole_column = rows == BLOCK and groups - 1 == RANDOMS and groups % 2 == 0
        if whole_column and rows % (16 * columns) == 0 and width == 2 * groups * LANES:
            return relay(*fused(groups, columns, query, *rest))
        return body(query, *rest)

    return jax.shard_map(run, mesh=mesh, in_specs=in_specs, out_specs=out_specs, check_vma=False)
```

```python
import functools
import math

import jax
import jax.numpy as jnp
from jax import lax
from jax.experimental import pallas as pl
from jax.experimental.pallas import tpu as pltpu
from jax.sharding import PartitionSpec as P

HEAD_DIM = 64
BLOCK = 128
GLOBALS = 2
RANDOMS = 3
KEYS = 8


def extended(block, sides, width, periodic):
    for axis, dim in sides:
        count = lax.axis_size(axis)
        forward = [(i, i + 1) for i in range(count - 1)]
        if periodic:
            forward.append((count - 1, 0))
        backward = [(target, source) for source, target in forward]
        low = lax.ppermute(
            lax.slice_in_dim(block, block.shape[dim] - width, None, axis=dim), axis, forward
        )
        high = lax.ppermute(lax.slice_in_dim(block, 0, width, axis=dim), axis, backward)
        block = jnp.concatenate([low, block, high], axis=dim)
    return block


def broadcast(block, axis, source):
    block = jnp.where(lax.axis_index(axis) == source, block, jnp.zeros_like(block))
    return lax.psum(block, axis)


def attend_blocks(queries, key_rows, value_rows, grad_rows, key_valid):
    factor = 1.0 / math.sqrt(queries.shape[-1])
    scores = (
        jnp.einsum("nqhe,njkhe->nhqjk", queries, key_rows, preferred_element_type=jnp.float32)
        * factor
    )
    scores = jnp.where(key_valid[:, None, None, :, None], scores, -1e30)
    row_max = jnp.max(scores, axis=(3, 4), keepdims=True)
    raised = jnp.exp(scores - row_max)
    attn_prob = raised / jnp.sum(raised, axis=(3, 4), keepdims=True)
    prob_half = attn_prob.astype(jnp.bfloat16)
    result = jnp.einsum(
        "nhqjk,njkhe->nqhe", prob_half, value_rows, preferred_element_type=jnp.float32
    )
    d_prob = jnp.einsum(
        "nqhe,njkhe->nhqjk", grad_rows, value_rows, preferred_element_type=jnp.float32
    )
    row_dot = jnp.sum(attn_prob * d_prob, axis=(3, 4), keepdims=True)
    d_scores = (attn_prob * (d_prob - row_dot) * factor).astype(jnp.bfloat16)
    d_query = jnp.einsum(
        "nhqjk,njkhe->nqhe", d_scores, key_rows, preferred_element_type=jnp.float32
    )
    d_keys = jnp.einsum("nhqjk,nqhe->njkhe", d_scores, queries, preferred_element_type=jnp.float32)
    d_values = jnp.einsum(
        "nhqjk,nqhe->njkhe", prob_half, grad_rows, preferred_element_type=jnp.float32
    )
    return (result, d_query, d_keys, d_values)


def body(query, keys, values, d_out, rand_blocks, global_blocks):
    group_count = lax.axis_size("grp")
    column_count = lax.axis_size("seq")
    column = lax.axis_index("seq")
    tokens_dev = query.shape[0]
    width = query.shape[1]
    local_blocks = tokens_dev // BLOCK
    head_width = width // group_count
    heads_here = head_width // HEAD_DIM
    block_total = group_count * column_count * local_blocks
    segment_span = column_count * local_blocks
    stride = local_blocks + 2
    count = group_count * local_blocks
    per_step = 4
    steps_count = count // per_step
    stacked = jnp.stack([keys, values])
    widened = extended(stacked, ((("grp", "seq"), 1),), BLOCK, False)
    key_send = widened[0][None]
    value_send = widened[1][None]
    query_heads, grad_heads, key_heads, value_heads = (
        lax.all_to_all(
            query.reshape(1, tokens_dev, width), "grp", split_axis=2, concat_axis=0, tiled=True
        ),
        lax.all_to_all(
            d_out.reshape(1, tokens_dev, width), "grp", split_axis=2, concat_axis=0, tiled=True
        ),
        lax.all_to_all(key_send, "grp", split_axis=2, concat_axis=0, tiled=True),
        lax.all_to_all(value_send, "grp", split_axis=2, concat_axis=0, tiled=True),
    )
    ext_pair = jnp.stack([key_heads, value_heads]).reshape(
        2, group_count * stride, BLOCK, head_width
    )
    global_device = global_blocks // local_blocks
    global_segment = global_device // column_count
    global_column = global_device % column_count
    global_local = global_blocks % local_blocks
    global_rows = global_segment * stride + global_local + 1
    fetched = []
    for which in range(GLOBALS):
        fetched.append(broadcast(ext_pair[:, global_rows[which]], "seq", global_column[which]))
    global_pair = jnp.stack(fetched, axis=1)
    segment_of = jnp.repeat(jnp.arange(group_count, dtype=jnp.int32), local_blocks)
    local_of = jnp.tile(jnp.arange(local_blocks, dtype=jnp.int32), group_count)
    query_ids = (segment_of * column_count + column) * local_blocks + local_of
    rand_ids = jnp.take(rand_blocks, query_ids, axis=0)
    rand_rows = rand_ids // segment_span * stride + rand_ids % local_blocks + 1
    window_rows = (segment_of * stride + local_of)[:, None] + jnp.arange(3, dtype=jnp.int32)[
        None, :
    ]
    key_table = jnp.concatenate([window_rows, rand_rows], axis=1)
    key_valid = jnp.concatenate(
        [
            (query_ids > 0)[:, None],
            jnp.ones((count, 1), dtype=jnp.bool_),
            (query_ids < block_total - 1)[:, None],
            jnp.ones((count, GLOBALS + RANDOMS), dtype=jnp.bool_),
        ],
        axis=1,
    )
    query_steps = query_heads.reshape(steps_count, per_step, BLOCK, heads_here, HEAD_DIM)
    grad_steps = grad_heads.reshape(steps_count, per_step, BLOCK, heads_here, HEAD_DIM)
    table_steps = key_table.reshape(steps_count, per_step, 3 + RANDOMS)
    valid_steps = key_valid.reshape(steps_count, per_step, KEYS)
    global_spread = jnp.broadcast_to(
        global_pair[:, None], (2, per_step, GLOBALS, BLOCK, head_width)
    )

    def advance(totals, packed):
        ext_total, global_total = totals
        query_part, grad_part, rows_part, valid_part = packed
        taken = jnp.stack(
            [
                lax.dynamic_index_in_dim(ext_pair, row, axis=1, keepdims=False)
                for row in rows_part.reshape(-1)
            ],
            axis=1,
        ).reshape(2, per_step, 3 + RANDOMS, BLOCK, head_width)
        gathered = jnp.concatenate([taken[:, :, :3], global_spread, taken[:, :, 3:]], axis=2)
        gathered = gathered.reshape(2, per_step, KEYS, BLOCK, heads_here, HEAD_DIM)
        result, d_query, d_keys, d_values = attend_blocks(
            query_part, gathered[0], gathered[1], grad_part, valid_part
        )
        d_pair = jnp.stack([d_keys, d_values]).reshape(2, per_step, KEYS, BLOCK, head_width)
        spread_back = jnp.concatenate([d_pair[:, :, :3], d_pair[:, :, 3 + GLOBALS :]], axis=2)
        spread_back = spread_back.reshape(2, per_step * (3 + RANDOMS), BLOCK, head_width)
        ext_total = ext_total.at[:, rows_part.reshape(-1)].add(spread_back)
        global_total = global_total + jnp.sum(d_pair[:, :, 3 : 3 + GLOBALS], axis=1)
        return (
            (ext_total, global_total),
            (result.astype(jnp.bfloat16), d_query.astype(jnp.bfloat16)),
        )

    start_totals = (
        jnp.zeros((2, group_count * stride, BLOCK, head_width), jnp.float32),
        jnp.zeros((2, GLOBALS, BLOCK, head_width), jnp.float32),
    )
    totals, outputs = lax.scan(
        advance, start_totals, (query_steps, grad_steps, table_steps, valid_steps)
    )
    ext_total = totals[0].reshape(2, group_count, stride, BLOCK, head_width)
    global_sum = lax.psum(totals[1], "seq")
    own_grad = ext_total[:, :, 1 : local_blocks + 1]
    for which in range(GLOBALS):
        addend = jnp.where(column == global_column[which], global_sum[:, which], 0.0)
        own_grad = own_grad.at[:, global_segment[which], global_local[which]].add(addend)
    send_left = ext_total[:, :, 0]
    send_right = ext_total[:, :, local_blocks + 1]
    empty_edge = jnp.zeros_like(send_left[:, :1])
    send_left = jnp.where(
        column == 0, jnp.concatenate([send_left[:, 1:], empty_edge], axis=1), send_left
    )
    send_right = jnp.where(
        column == column_count - 1,
        jnp.concatenate([empty_edge, send_right[:, :-1]], axis=1),
        send_right,
    )
    edges = jnp.concatenate([send_left, send_right], axis=2)
    arrived = extended(edges, (("seq", 2),), BLOCK, True)
    own_grad = own_grad.at[:, :, 0].add(arrived[:, :, :BLOCK])
    own_grad = own_grad.at[:, :, local_blocks - 1].add(arrived[:, :, 3 * BLOCK :])
    head_shape = (group_count, tokens_dev, head_width)
    attended_heads = outputs[0].reshape(head_shape)
    d_query_heads = outputs[1].reshape(head_shape)
    d_key_heads = own_grad[0].reshape(head_shape).astype(jnp.bfloat16)
    d_value_heads = own_grad[1].reshape(head_shape).astype(jnp.bfloat16)
    returned = (
        lax.all_to_all(attended_heads, "grp", split_axis=0, concat_axis=2, tiled=True),
        lax.all_to_all(d_query_heads, "grp", split_axis=0, concat_axis=2, tiled=True),
        lax.all_to_all(d_key_heads, "grp", split_axis=0, concat_axis=2, tiled=True),
        lax.all_to_all(d_value_heads, "grp", split_axis=0, concat_axis=2, tiled=True),
    )
    return (
        returned[0].reshape(tokens_dev, width),
        returned[1].reshape(tokens_dev, width),
        returned[2].reshape(tokens_dev, width),
        returned[3].reshape(tokens_dev, width),
    )


MESH = pl.DeviceIdType.MESH
F32 = jnp.float32
BF16 = jnp.bfloat16
LANES = 128


def contract(left, right, dims):
    return lax.dot_general(left, right, (dims, ((), ())), preferred_element_type=F32)


def fused_kernel(
    groups, columns, global_ref, q_ref, k_ref, v_ref, g_ref,
    att_ref, dq_ref, dk_ref, dv_ref,
    qg, kv, side, cand, piece, glob, dsum, dside, dside_in, dg_out, dg_in, dg_sum,
    att_out, dq_out, dk_out, dv_out,
    own_sem, kv_recv, qg_recv, side_recv, ga_recv, gb_recv, ds_recv, da_recv, db_recv,
    gs_recv, dt_recv, in_send, side_send, glob_send, ds_send, out_send, out_recv,
    keep_sem, fixed_send,
):
    h = lax.axis_index("grp")
    c = lax.axis_index("seq")
    rows, width = q_ref.shape
    share = width // groups
    strip = rows // columns
    pairs = share // LANES

    def rows_of(index):
        return pl.ds(pl.multiple_of(index * strip, strip), strip)

    def remote(src, dst, send, recv, device):
        return pltpu.make_async_remote_copy(
            src_ref=src, dst_ref=dst, send_sem=send, recv_sem=recv,
            device_id=device, device_id_type=MESH,
        )

    def settle(ref, sem):
        pltpu.make_async_copy(ref, ref, sem).wait()

    right = lax.rem(c + 1, columns)
    left = lax.rem(c + columns - 1, columns)

    barrier = pltpu.get_barrier_semaphore()
    for d in range(1, groups):
        pl.semaphore_signal(
            barrier, inc=1, device_id=(lax.rem(h + d, groups), c), device_id_type=MESH
        )
    for e in range(1, columns):
        pl.semaphore_signal(
            barrier, inc=1, device_id=(h, lax.rem(c + e, columns)), device_id_type=MESH
        )

    def lanes_of(index, pair):
        return pl.ds(pl.multiple_of(index * share + pair * LANES, LANES), LANES)

    own = []
    for pair in range(pairs):
        for kind, (refs, buf) in enumerate((((k_ref, v_ref), kv), ((q_ref, g_ref), qg))):
            for a, ref in enumerate(refs):
                own.append(
                    pltpu.make_async_copy(
                        ref.at[:, lanes_of(h, pair)], buf.at[pair, a, h], own_sem.at[kind, pair]
                    )
                )
    for copy in own:
        copy.start()
    pl.semaphore_wait(barrier, groups + columns - 2)

    def send_in(kind, pair):
        refs, buf = (((k_ref, v_ref), kv), ((q_ref, g_ref), qg))[kind]
        for d in range(1, groups):
            target = lax.rem(h + d, groups)
            arrival = (kv_recv, qg_recv)[kind].at[pair, d - 1]
            for a, ref in enumerate(refs):
                remote(
                    ref.at[:, lanes_of(target, pair)], buf.at[pair, a, h],
                    in_send.at[kind], arrival, (target, c),
                ).start()

    def send_sides(pair, d):
        segment = lax.rem(h + groups - d, groups)
        for way, to in ((0, right), (1, left)):
            remote(
                kv.at[pair, :, segment], side.at[pair, way, :, segment],
                side_send.at[0], side_recv.at[pair], (h, to),
            ).start()

    def forward(pair, between, held=()):
        settle(kv.at[pair, :, h], own_sem.at[0, pair])
        if 0 not in held:
            send_sides(pair, 0)
        for d in range(1, groups):
            settle(kv.at[pair, :, lax.rem(h + groups - d, groups)], kv_recv.at[pair, d - 1])
            if d not in held:
                send_sides(pair, d)
            if d in between:
                between[d]()
        offer(pair)
        for d in held:
            send_sides(pair, d)

    last = groups * columns - 1
    other = global_ref[0] + global_ref[1] - last
    seg_of = lax.div(other, columns)
    col_of = lax.rem(other, columns)
    moving, fixed = pl.ds(0, 2), pl.ds(2, 2)

    def offer(pair):
        for a in range(2):
            chosen = kv[pair, a, 0]
            for t in range(1, groups):
                chosen = jnp.where(seg_of == t, kv[pair, a, t], chosen)
            cand[pair, a] = chosen
        for e in range(1, columns):
            to = lax.rem(c + e, columns)
            remote(
                cand.at[pair, :, rows_of(to), :], piece.at[pair, c],
                glob_send.at[0], ga_recv.at[pair], (h, to),
            ).start()
        piece[pair, c] = cand[pair, :, rows_of(c), :]

        @pl.when(c == columns - 1)
        def _():
            for to in range(columns - 1):
                remote(
                    kv.at[pair, :, groups - 1, rows_of(to), :],
                    glob.at[pair, fixed, rows_of(to), :],
                    fixed_send.at[0], gs_recv.at[pair], (h, to),
                ).start()
            for a in range(2):
                glob[pair, 2 + a, rows_of(c), :] = kv[pair, a, groups - 1, rows_of(c), :]

    def choose(pair):
        settle(piece.at[pair, pl.ds(0, columns - 1)], ga_recv.at[pair])
        for a in range(2):
            chosen = piece[pair, 0, a]
            for e in range(1, columns):
                chosen = jnp.where(col_of == e, piece[pair, e, a], chosen)
            glob[pair, a, rows_of(c), :] = chosen

        @pl.when(c < columns - 1)
        def _():
            settle(glob.at[pair, fixed, rows_of(c), :], gs_recv.at[pair])

        for e in range(1, columns):
            to = lax.rem(c + e, columns)
            remote(
                glob.at[pair, :, rows_of(c), :], glob.at[pair, :, rows_of(c), :],
                glob_send.at[1], gb_recv.at[pair], (h, to),
            ).start()

    lane = lax.broadcasted_iota(jnp.int32, (rows, LANES), 1)
    factor = 1.0 / math.sqrt(HEAD_DIM)

    def stacked(block):
        zero = jnp.zeros_like(block)
        low = jnp.where(lane < HEAD_DIM, block, zero)
        high = jnp.where(lane < HEAD_DIM, zero, block)
        return jnp.concatenate([low, high], axis=0)

    def picked(wide):
        return jnp.concatenate(
            [wide[:HEAD_DIM, :rows], wide[HEAD_DIM:, rows:]], axis=0
        ).T

    outgoing = ((att_out, att_ref), (dq_out, dq_ref), (dk_out, dk_ref), (dv_out, dv_ref))

    def send_out(pair, i, first):
        segment = lax.rem(h + i + 1, groups)
        for buf, ref in outgoing[first : first + 2]:
            if i < groups - 1:
                remote(
                    buf.at[pair, segment], ref.at[:, lanes_of(h, pair)],
                    out_send.at[first // 2], out_recv.at[first // 2], (segment, c),
                ).start()
            else:
                pltpu.make_async_copy(
                    buf.at[pair, h], ref.at[:, lanes_of(h, pair)], keep_sem.at[0]
                ).start()

    def send_dsides(pair, i):
        for way, to in ((0, left), (1, right)):
            remote(
                dside.at[pair, way, :, i], dside_in.at[pair, way, :, i],
                ds_send.at[0], ds_recv.at[pair], (h, to),
            ).start()

    at_first = jnp.where(c == 0, 1, 0)
    at_last = jnp.where(c == columns - 1, 1, 0)
    dense = (groups + GLOBALS) * rows

    def unit(pair, i):
        segment = lax.rem(h + i + 1, groups)
        block = segment * columns + c
        before = lax.rem(segment + groups - at_first, groups)
        after = lax.rem(segment + at_last, groups)

        def listed(a):
            return jnp.concatenate(
                [kv[pair, a, t] for t in range(groups)]
                + [glob[pair, 2 * w + a] for w in range(GLOBALS)]
                + [side[pair, 0, a, before], side[pair, 1, a, after]],
                axis=0,
            )

        key = listed(0)
        value = listed(1)
        query = stacked(qg[pair, 0, segment] * jnp.asarray(factor, BF16))
        grad = stacked(qg[pair, 1, segment])
        scores = contract(key, query, ((1,), (1,)))
        scores = jnp.concatenate(
            [
                scores[:dense],
                jnp.where(block > 0, scores[dense : dense + rows], -1e30),
                jnp.where(block < last, scores[dense + rows :], -1e30),
            ],
            axis=0,
        )
        raised = jnp.exp(scores - jnp.max(scores, axis=0, keepdims=True))
        prob = raised * (1.0 / jnp.sum(raised, axis=0, keepdims=True))
        half = prob.astype(BF16)
        d_prob = contract(value, grad, ((1,), (1,)))
        result = contract(value, half, ((0,), (0,)))
        row_dot = jnp.sum(prob * d_prob, axis=0, keepdims=True)
        d_scores = (prob * (d_prob - row_dot)).astype(BF16)
        d_query = contract(key, d_scores, ((0,), (0,))) * factor
        d_value = contract(half, grad, ((1,), (0,)))
        d_key = contract(d_scores, query, ((1,), (0,)))
        att_out[pair, segment] = picked(result).astype(BF16)
        dq_out[pair, segment] = picked(d_query).astype(BF16)
        return d_key, d_value

    def ready(pair):
        settle(side.at[pair], side_recv.at[pair])
        settle(glob.at[pair, :, pl.ds(0, rows - strip)], gb_recv.at[pair])
        settle(qg.at[pair, :, h], own_sem.at[1, pair])

    def run(pair, i, closing=False, share_now=True):
        segment = lax.rem(h + i + 1, groups)
        if i < groups - 1:
            settle(qg.at[pair, :, segment], qg_recv.at[pair, groups - 2 - i])
        grads = unit(pair, i)
        for a in range(2):
            if i == groups - 1:
                dsum[pair, a] = grads[a][:dense]
            else:
                dsum[pair, a] += grads[a][:dense]
            dside[pair, 0, a, i] = grads[a][dense : dense + rows].astype(BF16)
            dside[pair, 1, a, i] = grads[a][dense + rows :].astype(BF16)
        if closing:
            scatter(pair)
        if share_now:
            send_dsides(pair, i)
        send_out(pair, i, 0)

    def scatter(pair):
        for w in range(GLOBALS):
            for a in range(2):
                start = (groups + w) * rows
                dg_out[pair, 2 * w + a] = dsum[pair, a, start : start + rows].astype(BF16)
        for e in range(1, columns):
            to = lax.rem(c + e, columns)
            remote(
                dg_out.at[pair, :, rows_of(to), :], dg_in.at[pair, c],
                glob_send.at[2], da_recv.at[pair], (h, to),
            ).start()
        dg_in[pair, c] = dg_out[pair, :, rows_of(c), :]

    def gather(pair):
        settle(dg_in.at[pair, pl.ds(0, columns - 1)], da_recv.at[pair])
        total = dg_in[pair, 0].astype(F32)
        for e in range(1, columns):
            total = total + dg_in[pair, e].astype(F32)
        dg_sum[pair, :, rows_of(c), :] = total.astype(BF16)
        for e in range(1, columns):
            to = lax.rem(c + e, columns)
            remote(
                dg_sum.at[pair, moving, rows_of(c), :], dg_sum.at[pair, moving, rows_of(c), :],
                glob_send.at[3], db_recv.at[pair], (h, to),
            ).start()

        @pl.when(c < columns - 1)
        def _():
            remote(
                dg_sum.at[pair, fixed, rows_of(c), :], dg_sum.at[pair, fixed, rows_of(c), :],
                fixed_send.at[1], dt_recv.at[pair], (h, columns - 1),
            ).start()

    def finish(pair):
        settle(dside_in.at[pair], ds_recv.at[pair])
        settle(dg_sum.at[pair, moving, pl.ds(0, rows - strip)], db_recv.at[pair])

        @pl.when(c == columns - 1)
        def _():
            settle(dg_sum.at[pair, fixed, pl.ds(0, rows - strip)], dt_recv.at[pair])
            span = pl.ds((groups - 1) * rows, rows)
            for a in range(2):
                dsum[pair, a, span] += dg_sum[pair, 2 + a].astype(F32)

        for i in range(groups):
            segment = lax.rem(h + i + 1, groups)
            low = lax.rem(i + at_last, groups)
            high = lax.rem(i + groups - at_first, groups)
            span = pl.ds(pl.multiple_of(segment * rows, rows), rows)
            mine = (other == segment * columns + c).astype(F32)
            for a, buf in enumerate((dk_out, dv_out)):
                whole = dsum[pair, a, span]
                whole += dside_in[pair, 0, a, low].astype(F32)
                whole += dside_in[pair, 1, a, high].astype(F32)
                whole += dg_sum[pair, a].astype(F32) * mine
                buf[pair, segment] = whole.astype(BF16)
            send_out(pair, i, 2)

    def then(step, *rest):
        return functools.partial(step, *rest)

    send_in(0, 0)
    forward(0, {2: then(send_in, 0, 1)}, (2, 3))
    send_in(1, 0)
    choose(0)
    forward(1, {1: then(send_in, 1, 1)}, range(groups))
    ready(0)
    run(0, 3, False, False)
    choose(1)
    run(0, 2, False, False)
    send_dsides(0, 3)
    run(0, 1, False, False)
    send_dsides(0, 2)
    run(0, 0, True, False)
    ready(1)
    send_dsides(0, 1)
    run(1, 3, False, False)
    send_dsides(0, 0)
    run(1, 2, False, False)
    gather(0)
    send_dsides(1, 3)
    run(1, 1, False, False)
    send_dsides(1, 2)
    run(1, 0, True, False)
    send_dsides(1, 1)
    send_dsides(1, 0)
    finish(0)
    gather(1)
    finish(1)

    shares = pl.ds(0, groups - 1)
    for n in range(2):
        settle(kv.at[:, :, shares], in_send.at[n])
        settle(kv.at[:, :, shares], out_send.at[n])
        settle(kv.at[:, :, shares], out_recv.at[n])
    settle(side, side_send.at[0])
    settle(dside, ds_send.at[0])
    settle(piece.at[:, pl.ds(0, columns - 1)], glob_send.at[0])
    settle(glob.at[:, :, pl.ds(0, rows - strip)], glob_send.at[1])
    settle(dg_in.at[:, pl.ds(0, columns - 1)], glob_send.at[2])
    settle(dg_sum.at[:, moving, pl.ds(0, rows - strip)], glob_send.at[3])

    @pl.when(c == columns - 1)
    def _():
        settle(glob.at[:, fixed, pl.ds(0, rows - strip)], fixed_send.at[0])

    @pl.when(c < columns - 1)
    def _():
        settle(glob.at[:, fixed, pl.ds(0, strip)], fixed_send.at[1])

    settle(kv.at[:, :, pl.ds(0, 2)], keep_sem.at[0])


def fused(groups, columns, query, keys, values, d_out, rand_blocks, global_blocks):
    rows, width = query.shape
    share = width // groups
    strip = rows // columns
    half = functools.partial(pltpu.VMEM, dtype=BF16)
    full = functools.partial(pltpu.VMEM, dtype=F32)
    dma = pltpu.SemaphoreType.DMA
    pairs = share // LANES
    tile = (rows, LANES)
    scratch = [
        half((pairs, 2, groups, *tile)),
        half((pairs, 2, groups, *tile)),
        half((pairs, 2, 2, groups, *tile)),
        half((pairs, 2, *tile)),
        half((pairs, columns, 2, strip, LANES)),
        half((pairs, 2 * GLOBALS, *tile)),
        full((pairs, 2, (groups + GLOBALS) * rows, LANES)),
        half((pairs, 2, 2, groups, *tile)),
        half((pairs, 2, 2, groups, *tile)),
        half((pairs, 2 * GLOBALS, *tile)),
        half((pairs, columns, 2 * GLOBALS, strip, LANES)),
        half((pairs, 2 * GLOBALS, *tile)),
    ] + [half((pairs, groups, *tile))] * 4
    scratch += [dma((2, pairs))] + [dma((pairs, groups - 1))] * 2 + [dma((pairs,))] * 8
    scratch += [dma((2,)), dma((1,)), dma((4,)), dma((1,)), dma((2,)), dma((2,)), dma((1,)), dma((2,))]
    hbm = pl.BlockSpec(memory_space=pltpu.HBM)
    return pl.pallas_call(
        functools.partial(fused_kernel, groups, columns),
        out_shape=[jax.ShapeDtypeStruct((rows, width), BF16)] * 4,
        in_specs=[pl.BlockSpec(memory_space=pltpu.SMEM)] + [hbm] * 4,
        out_specs=[hbm] * 4,
        scratch_shapes=scratch,
        compiler_params=pltpu.CompilerParams(
            collective_id=0, has_side_effects=True, vmem_limit_bytes=63 * 2**20
        ),
    )(global_blocks, query, keys, values, d_out)


CHUNKS = 4


def relay_kernel(*refs):
    count = (len(refs) - 3) // 2
    sources, targets = refs[:count], refs[count : 2 * count]
    held, in_sem, out_sem = refs[2 * count :]
    rows = held.shape[1] // CHUNKS
    for part in range(CHUNKS):
        at = pl.ds(part * rows, rows)
        for n in range(count):
            pltpu.make_async_copy(sources[n].at[at], held.at[n, at], in_sem.at[part]).start()
    for part in range(CHUNKS):
        at = pl.ds(part * rows, rows)
        pltpu.make_async_copy(held.at[:, at], held.at[:, at], in_sem.at[part]).wait()
        for n in range(count):
            pltpu.make_async_copy(held.at[n, at], targets[n].at[at], out_sem.at[0]).start()
    pltpu.make_async_copy(held, held, out_sem.at[0]).wait()


def relay(*arrays):
    hbm = pl.BlockSpec(memory_space=pltpu.HBM)
    count = len(arrays)
    return pl.pallas_call(
        relay_kernel,
        out_shape=[jax.ShapeDtypeStruct(a.shape, a.dtype) for a in arrays],
        in_specs=[hbm] * count,
        out_specs=[hbm] * count,
        scratch_shapes=[
            pltpu.VMEM((count, *arrays[0].shape), arrays[0].dtype),
            pltpu.SemaphoreType.DMA((CHUNKS,)),
            pltpu.SemaphoreType.DMA((1,)),
        ],
    )(*arrays)


def solution(mesh):
    in_specs = (
        P(("grp", "seq"), None),
        P(("grp", "seq"), None),
        P(("grp", "seq"), None),
        P(("grp", "seq"), None),
        P(),
        P(),
    )
    out_specs = (
        P(("grp", "seq"), None),
        P(("grp", "seq"), None),
        P(("grp", "seq"), None),
        P(("grp", "seq"), None),
    )
    groups, columns = mesh.shape["grp"], mesh.shape["seq"]

    def run(query, *rest):
        rows, width = query.shape
        whole_column = rows == BLOCK and groups - 1 == RANDOMS and groups % 2 == 0
        if whole_column and rows % (16 * columns) == 0 and width == 2 * groups * LANES:
            return relay(*fused(groups, columns, query, *rest))
        return body(query, *rest)

    return jax.shard_map(run, mesh=mesh, in_specs=in_specs, out_specs=out_specs, check_vma=False)
```

```python
import functools
import math

import jax
import jax.numpy as jnp
from jax import lax
from jax.experimental import pallas as pl
from jax.experimental.pallas import tpu as pltpu
from jax.sharding import PartitionSpec as P

HEAD_DIM = 64
BLOCK = 128
GLOBALS = 2
RANDOMS = 3
KEYS = 8


def extended(block, sides, width, periodic):
    for axis, dim in sides:
        count = lax.axis_size(axis)
        forward = [(i, i + 1) for i in range(count - 1)]
        if periodic:
            forward.append((count - 1, 0))
        backward = [(target, source) for source, target in forward]
        low = lax.ppermute(
            lax.slice_in_dim(block, block.shape[dim] - width, None, axis=dim), axis, forward
        )
        high = lax.ppermute(lax.slice_in_dim(block, 0, width, axis=dim), axis, backward)
        block = jnp.concatenate([low, block, high], axis=dim)
    return block


def broadcast(block, axis, source):
    block = jnp.where(lax.axis_index(axis) == source, block, jnp.zeros_like(block))
    return lax.psum(block, axis)


def attend_blocks(queries, key_rows, value_rows, grad_rows, key_valid):
    factor = 1.0 / math.sqrt(queries.shape[-1])
    scores = (
        jnp.einsum("nqhe,njkhe->nhqjk", queries, key_rows, preferred_element_type=jnp.float32)
        * factor
    )
    scores = jnp.where(key_valid[:, None, None, :, None], scores, -1e30)
    row_max = jnp.max(scores, axis=(3, 4), keepdims=True)
    raised = jnp.exp(scores - row_max)
    attn_prob = raised / jnp.sum(raised, axis=(3, 4), keepdims=True)
    prob_half = attn_prob.astype(jnp.bfloat16)
    result = jnp.einsum(
        "nhqjk,njkhe->nqhe", prob_half, value_rows, preferred_element_type=jnp.float32
    )
    d_prob = jnp.einsum(
        "nqhe,njkhe->nhqjk", grad_rows, value_rows, preferred_element_type=jnp.float32
    )
    row_dot = jnp.sum(attn_prob * d_prob, axis=(3, 4), keepdims=True)
    d_scores = (attn_prob * (d_prob - row_dot) * factor).astype(jnp.bfloat16)
    d_query = jnp.einsum(
        "nhqjk,njkhe->nqhe", d_scores, key_rows, preferred_element_type=jnp.float32
    )
    d_keys = jnp.einsum("nhqjk,nqhe->njkhe", d_scores, queries, preferred_element_type=jnp.float32)
    d_values = jnp.einsum(
        "nhqjk,nqhe->njkhe", prob_half, grad_rows, preferred_element_type=jnp.float32
    )
    return (result, d_query, d_keys, d_values)


def body(query, keys, values, d_out, rand_blocks, global_blocks):
    group_count = lax.axis_size("grp")
    column_count = lax.axis_size("seq")
    column = lax.axis_index("seq")
    tokens_dev = query.shape[0]
    width = query.shape[1]
    local_blocks = tokens_dev // BLOCK
    head_width = width // group_count
    heads_here = head_width // HEAD_DIM
    block_total = group_count * column_count * local_blocks
    segment_span = column_count * local_blocks
    stride = local_blocks + 2
    count = group_count * local_blocks
    per_step = 4
    steps_count = count // per_step
    stacked = jnp.stack([keys, values])
    widened = extended(stacked, ((("grp", "seq"), 1),), BLOCK, False)
    key_send = widened[0][None]
    value_send = widened[1][None]
    query_heads, grad_heads, key_heads, value_heads = (
        lax.all_to_all(
            query.reshape(1, tokens_dev, width), "grp", split_axis=2, concat_axis=0, tiled=True
        ),
        lax.all_to_all(
            d_out.reshape(1, tokens_dev, width), "grp", split_axis=2, concat_axis=0, tiled=True
        ),
        lax.all_to_all(key_send, "grp", split_axis=2, concat_axis=0, tiled=True),
        lax.all_to_all(value_send, "grp", split_axis=2, concat_axis=0, tiled=True),
    )
    ext_pair = jnp.stack([key_heads, value_heads]).reshape(
        2, group_count * stride, BLOCK, head_width
    )
    global_device = global_blocks // local_blocks
    global_segment = global_device // column_count
    global_column = global_device % column_count
    global_local = global_blocks % local_blocks
    global_rows = global_segment * stride + global_local + 1
    fetched = []
    for which in range(GLOBALS):
        fetched.append(broadcast(ext_pair[:, global_rows[which]], "seq", global_column[which]))
    global_pair = jnp.stack(fetched, axis=1)
    segment_of = jnp.repeat(jnp.arange(group_count, dtype=jnp.int32), local_blocks)
    local_of = jnp.tile(jnp.arange(local_blocks, dtype=jnp.int32), group_count)
    query_ids = (segment_of * column_count + column) * local_blocks + local_of
    rand_ids = jnp.take(rand_blocks, query_ids, axis=0)
    rand_rows = rand_ids // segment_span * stride + rand_ids % local_blocks + 1
    window_rows = (segment_of * stride + local_of)[:, None] + jnp.arange(3, dtype=jnp.int32)[
        None, :
    ]
    key_table = jnp.concatenate([window_rows, rand_rows], axis=1)
    key_valid = jnp.concatenate(
        [
            (query_ids > 0)[:, None],
            jnp.ones((count, 1), dtype=jnp.bool_),
            (query_ids < block_total - 1)[:, None],
            jnp.ones((count, GLOBALS + RANDOMS), dtype=jnp.bool_),
        ],
        axis=1,
    )
    query_steps = query_heads.reshape(steps_count, per_step, BLOCK, heads_here, HEAD_DIM)
    grad_steps = grad_heads.reshape(steps_count, per_step, BLOCK, heads_here, HEAD_DIM)
    table_steps = key_table.reshape(steps_count, per_step, 3 + RANDOMS)
    valid_steps = key_valid.reshape(steps_count, per_step, KEYS)
    global_spread = jnp.broadcast_to(
        global_pair[:, None], (2, per_step, GLOBALS, BLOCK, head_width)
    )

    def advance(totals, packed):
        ext_total, global_total = totals
        query_part, grad_part, rows_part, valid_part = packed
        taken = jnp.stack(
            [
                lax.dynamic_index_in_dim(ext_pair, row, axis=1, keepdims=False)
                for row in rows_part.reshape(-1)
            ],
            axis=1,
        ).reshape(2, per_step, 3 + RANDOMS, BLOCK, head_width)
        gathered = jnp.concatenate([taken[:, :, :3], global_spread, taken[:, :, 3:]], axis=2)
        gathered = gathered.reshape(2, per_step, KEYS, BLOCK, heads_here, HEAD_DIM)
        result, d_query, d_keys, d_values = attend_blocks(
            query_part, gathered[0], gathered[1], grad_part, valid_part
        )
        d_pair = jnp.stack([d_keys, d_values]).reshape(2, per_step, KEYS, BLOCK, head_width)
        spread_back = jnp.concatenate([d_pair[:, :, :3], d_pair[:, :, 3 + GLOBALS :]], axis=2)
        spread_back = spread_back.reshape(2, per_step * (3 + RANDOMS), BLOCK, head_width)
        ext_total = ext_total.at[:, rows_part.reshape(-1)].add(spread_back)
        global_total = global_total + jnp.sum(d_pair[:, :, 3 : 3 + GLOBALS], axis=1)
        return (
            (ext_total, global_total),
            (result.astype(jnp.bfloat16), d_query.astype(jnp.bfloat16)),
        )

    start_totals = (
        jnp.zeros((2, group_count * stride, BLOCK, head_width), jnp.float32),
        jnp.zeros((2, GLOBALS, BLOCK, head_width), jnp.float32),
    )
    totals, outputs = lax.scan(
        advance, start_totals, (query_steps, grad_steps, table_steps, valid_steps)
    )
    ext_total = totals[0].reshape(2, group_count, stride, BLOCK, head_width)
    global_sum = lax.psum(totals[1], "seq")
    own_grad = ext_total[:, :, 1 : local_blocks + 1]
    for which in range(GLOBALS):
        addend = jnp.where(column == global_column[which], global_sum[:, which], 0.0)
        own_grad = own_grad.at[:, global_segment[which], global_local[which]].add(addend)
    send_left = ext_total[:, :, 0]
    send_right = ext_total[:, :, local_blocks + 1]
    empty_edge = jnp.zeros_like(send_left[:, :1])
    send_left = jnp.where(
        column == 0, jnp.concatenate([send_left[:, 1:], empty_edge], axis=1), send_left
    )
    send_right = jnp.where(
        column == column_count - 1,
        jnp.concatenate([empty_edge, send_right[:, :-1]], axis=1),
        send_right,
    )
    edges = jnp.concatenate([send_left, send_right], axis=2)
    arrived = extended(edges, (("seq", 2),), BLOCK, True)
    own_grad = own_grad.at[:, :, 0].add(arrived[:, :, :BLOCK])
    own_grad = own_grad.at[:, :, local_blocks - 1].add(arrived[:, :, 3 * BLOCK :])
    head_shape = (group_count, tokens_dev, head_width)
    attended_heads = outputs[0].reshape(head_shape)
    d_query_heads = outputs[1].reshape(head_shape)
    d_key_heads = own_grad[0].reshape(head_shape).astype(jnp.bfloat16)
    d_value_heads = own_grad[1].reshape(head_shape).astype(jnp.bfloat16)
    returned = (
        lax.all_to_all(attended_heads, "grp", split_axis=0, concat_axis=2, tiled=True),
        lax.all_to_all(d_query_heads, "grp", split_axis=0, concat_axis=2, tiled=True),
        lax.all_to_all(d_key_heads, "grp", split_axis=0, concat_axis=2, tiled=True),
        lax.all_to_all(d_value_heads, "grp", split_axis=0, concat_axis=2, tiled=True),
    )
    return (
        returned[0].reshape(tokens_dev, width),
        returned[1].reshape(tokens_dev, width),
        returned[2].reshape(tokens_dev, width),
        returned[3].reshape(tokens_dev, width),
    )


MESH = pl.DeviceIdType.MESH
F32 = jnp.float32
BF16 = jnp.bfloat16
LANES = 128


def contract(left, right, dims):
    return lax.dot_general(left, right, (dims, ((), ())), preferred_element_type=F32)


def fused_kernel(
    groups, columns, global_ref, q_ref, k_ref, v_ref, g_ref,
    out_ref,
    qg, kv, side, cand, piece, glob, dsum, dside, dside_in, dg_out, dg_in, dg_sum,
    row_parts, key_parts,
    own_sem, kv_recv, qg_recv, side_recv, ga_recv, gb_recv, ds_recv, da_recv, db_recv,
    gs_recv, dt_recv, in_send, side_send, glob_send, ds_send, out_send, out_recv,
    keep_sem, fixed_send,
):
    h = lax.axis_index("grp")
    c = lax.axis_index("seq")
    rows, width = q_ref.shape
    share = width // groups
    strip = rows // columns
    pairs = share // LANES

    def rows_of(index):
        return pl.ds(pl.multiple_of(index * strip, strip), strip)

    def remote(src, dst, send, recv, device):
        return pltpu.make_async_remote_copy(
            src_ref=src, dst_ref=dst, send_sem=send, recv_sem=recv,
            device_id=device, device_id_type=MESH,
        )

    def settle(ref, sem):
        pltpu.make_async_copy(ref, ref, sem).wait()

    right = lax.rem(c + 1, columns)
    left = lax.rem(c + columns - 1, columns)

    barrier = pltpu.get_barrier_semaphore()
    for d in range(1, groups):
        pl.semaphore_signal(
            barrier, inc=1, device_id=(lax.rem(h + d, groups), c), device_id_type=MESH
        )
    for e in range(1, columns):
        pl.semaphore_signal(
            barrier, inc=1, device_id=(h, lax.rem(c + e, columns)), device_id_type=MESH
        )

    def lanes_of(index, pair):
        return pl.ds(pl.multiple_of(index * share + pair * LANES, LANES), LANES)

    own = []
    for pair in range(pairs):
        for kind, (refs, buf) in enumerate((((k_ref, v_ref), kv), ((q_ref, g_ref), qg))):
            for a, ref in enumerate(refs):
                own.append(
                    pltpu.make_async_copy(
                        ref.at[:, lanes_of(h, pair)], buf.at[pair, a, h], own_sem.at[kind, pair]
                    )
                )
    for copy in own:
        copy.start()
    pl.semaphore_wait(barrier, groups + columns - 2)

    def send_in(kind, pair):
        refs, buf = (((k_ref, v_ref), kv), ((q_ref, g_ref), qg))[kind]
        for d in range(1, groups):
            target = lax.rem(h + d, groups)
            arrival = (kv_recv, qg_recv)[kind].at[pair, d - 1]
            for a, ref in enumerate(refs):
                remote(
                    ref.at[:, lanes_of(target, pair)], buf.at[pair, a, h],
                    in_send.at[kind], arrival, (target, c),
                ).start()

    def send_sides(pair, d):
        segment = lax.rem(h + groups - d, groups)
        for way, to in ((0, right), (1, left)):
            remote(
                kv.at[pair, :, segment], side.at[pair, way, :, segment],
                side_send.at[0], side_recv.at[pair], (h, to),
            ).start()

    def forward(pair, between, held=()):
        settle(kv.at[pair, :, h], own_sem.at[0, pair])
        if 0 not in held:
            send_sides(pair, 0)
        for d in range(1, groups):
            settle(kv.at[pair, :, lax.rem(h + groups - d, groups)], kv_recv.at[pair, d - 1])
            if d not in held:
                send_sides(pair, d)
            if d in between:
                between[d]()
        offer(pair)
        for d in held:
            send_sides(pair, d)

    last = groups * columns - 1
    other = global_ref[0] + global_ref[1] - last
    seg_of = lax.div(other, columns)
    col_of = lax.rem(other, columns)
    moving, fixed = pl.ds(0, 2), pl.ds(2, 2)

    def offer(pair):
        for a in range(2):
            chosen = kv[pair, a, 0]
            for t in range(1, groups):
                chosen = jnp.where(seg_of == t, kv[pair, a, t], chosen)
            cand[pair, a] = chosen
        for e in range(1, columns):
            to = lax.rem(c + e, columns)
            remote(
                cand.at[pair, :, rows_of(to), :], piece.at[pair, c],
                glob_send.at[0], ga_recv.at[pair], (h, to),
            ).start()
        piece[pair, c] = cand[pair, :, rows_of(c), :]

        @pl.when(c == columns - 1)
        def _():
            for to in range(columns - 1):
                remote(
                    kv.at[pair, :, groups - 1, rows_of(to), :],
                    glob.at[pair, fixed, rows_of(to), :],
                    fixed_send.at[0], gs_recv.at[pair], (h, to),
                ).start()
            for a in range(2):
                glob[pair, 2 + a, rows_of(c), :] = kv[pair, a, groups - 1, rows_of(c), :]

    def choose(pair):
        settle(piece.at[pair, pl.ds(0, columns - 1)], ga_recv.at[pair])
        for a in range(2):
            chosen = piece[pair, 0, a]
            for e in range(1, columns):
                chosen = jnp.where(col_of == e, piece[pair, e, a], chosen)
            glob[pair, a, rows_of(c), :] = chosen

        @pl.when(c < columns - 1)
        def _():
            settle(glob.at[pair, fixed, rows_of(c), :], gs_recv.at[pair])

        for e in range(1, columns):
            to = lax.rem(c + e, columns)
            remote(
                glob.at[pair, :, rows_of(c), :], glob.at[pair, :, rows_of(c), :],
                glob_send.at[1], gb_recv.at[pair], (h, to),
            ).start()

    lane = lax.broadcasted_iota(jnp.int32, (rows, LANES), 1)
    factor = 1.0 / math.sqrt(HEAD_DIM)

    def stacked(block):
        zero = jnp.zeros_like(block)
        low = jnp.where(lane < HEAD_DIM, block, zero)
        high = jnp.where(lane < HEAD_DIM, zero, block)
        return jnp.concatenate([low, high], axis=0)

    def picked(wide):
        return jnp.concatenate(
            [wide[:HEAD_DIM, :rows], wide[HEAD_DIM:, rows:]], axis=0
        ).T

    def send_out(pair, segment, away, first):
        buf = (row_parts, key_parts)[first // 2]
        target = out_ref.at[pl.ds(first, 2), :, lanes_of(h, pair)]
        if away:
            remote(
                buf.at[pair, segment], target,
                out_send.at[first // 2], out_recv.at[first // 2], (segment, c),
            ).start()
        else:
            pltpu.make_async_copy(buf.at[pair, h], target, keep_sem.at[0]).start()

    def send_dsides(pair, i):
        for way, to in ((0, left), (1, right)):
            remote(
                dside.at[pair, way, :, i], dside_in.at[pair, way, :, i],
                ds_send.at[0], ds_recv.at[pair], (h, to),
            ).start()

    at_first = jnp.where(c == 0, 1, 0)
    at_last = jnp.where(c == columns - 1, 1, 0)
    dense = (groups + GLOBALS) * rows

    def unit(pair, i):
        segment = lax.rem(h + i + 1, groups)
        block = segment * columns + c
        before = lax.rem(segment + groups - at_first, groups)
        after = lax.rem(segment + at_last, groups)

        def listed(a):
            return jnp.concatenate(
                [kv[pair, a, t] for t in range(groups)]
                + [glob[pair, 2 * w + a] for w in range(GLOBALS)]
                + [side[pair, 0, a, before], side[pair, 1, a, after]],
                axis=0,
            )

        key = listed(0)
        value = listed(1)
        query = stacked(qg[pair, 0, segment] * jnp.asarray(factor, BF16))
        grad = stacked(qg[pair, 1, segment])
        scores = contract(key, query, ((1,), (1,)))
        scores = jnp.concatenate(
            [
                scores[:dense],
                jnp.where(block > 0, scores[dense : dense + rows], -1e30),
                jnp.where(block < last, scores[dense + rows :], -1e30),
            ],
            axis=0,
        )
        raised = jnp.exp(scores - jnp.max(scores, axis=0, keepdims=True))
        prob = raised * (1.0 / jnp.sum(raised, axis=0, keepdims=True))
        half = prob.astype(BF16)
        d_prob = contract(value, grad, ((1,), (1,)))
        row_dot = jnp.sum(prob * d_prob, axis=0, keepdims=True)
        d_scores = (prob * (d_prob - row_dot)).astype(BF16)

        def part(start, stop):
            return (
                contract(d_scores[start:stop], query, ((1,), (0,))),
                contract(half[start:stop], grad, ((1,), (0,))),
            )

        def rows_out():
            result = contract(value, half, ((0,), (0,)))
            d_query = contract(key, d_scores, ((0,), (0,))) * factor
            row_parts[pair, segment, 0] = picked(result).astype(BF16)
            row_parts[pair, segment, 1] = picked(d_query).astype(BF16)

        return part, rows_out

    def ready(pair):
        settle(side.at[pair], side_recv.at[pair])
        settle(glob.at[pair, :, pl.ds(0, rows - strip)], gb_recv.at[pair])
        settle(qg.at[pair, :, h], own_sem.at[1, pair])

    def run(pair, i, closing=(), share_now=True):
        segment = lax.rem(h + i + 1, groups)
        if i < groups - 1:
            settle(qg.at[pair, :, segment], qg_recv.at[pair, groups - 2 - i])
        part, rows_out = unit(pair, i)

        def summed(start, stop):
            grads = part(start, stop)
            for a in range(2):
                if i == groups - 1:
                    dsum[pair, a, start:stop] = grads[a]
                else:
                    dsum[pair, a, start:stop] += grads[a]

        def sides_out():
            grads = part(dense, dense + 2 * rows)
            for a in range(2):
                dside[pair, 0, a, i] = grads[a][:rows].astype(BF16)
                dside[pair, 1, a, i] = grads[a][rows:].astype(BF16)

        if closing:
            summed(groups * rows, dense)
            scatter(pair)
            sides_out()
            for late in closing:
                send_dsides(pair, late)
            rows_out()
            summed(0, groups * rows)
        else:
            rows_out()
            summed(0, dense)
            sides_out()
            if share_now:
                send_dsides(pair, i)
        send_out(pair, segment, i < groups - 1, 0)

    def scatter(pair):
        for w in range(GLOBALS):
            for a in range(2):
                start = (groups + w) * rows
                dg_out[pair, 2 * w + a] = dsum[pair, a, start : start + rows].astype(BF16)
        for e in range(1, columns):
            to = lax.rem(c + e, columns)
            remote(
                dg_out.at[pair, :, rows_of(to), :], dg_in.at[pair, c],
                glob_send.at[2], da_recv.at[pair], (h, to),
            ).start()
        dg_in[pair, c] = dg_out[pair, :, rows_of(c), :]

    def gather(pair):
        settle(dg_in.at[pair, pl.ds(0, columns - 1)], da_recv.at[pair])
        total = dg_in[pair, 0].astype(F32)
        for e in range(1, columns):
            total = total + dg_in[pair, e].astype(F32)
        dg_sum[pair, :, rows_of(c), :] = total.astype(BF16)
        for e in range(1, columns):
            to = lax.rem(c + e, columns)
            remote(
                dg_sum.at[pair, moving, rows_of(c), :], dg_sum.at[pair, moving, rows_of(c), :],
                glob_send.at[3], db_recv.at[pair], (h, to),
            ).start()

        @pl.when(c < columns - 1)
        def _():
            remote(
                dg_sum.at[pair, fixed, rows_of(c), :], dg_sum.at[pair, fixed, rows_of(c), :],
                fixed_send.at[1], dt_recv.at[pair], (h, columns - 1),
            ).start()

    def finish(pair):
        settle(dside_in.at[pair], ds_recv.at[pair])
        settle(dg_sum.at[pair, moving, pl.ds(0, rows - strip)], db_recv.at[pair])

        @pl.when(c == columns - 1)
        def _():
            settle(dg_sum.at[pair, fixed, pl.ds(0, rows - strip)], dt_recv.at[pair])
            span = pl.ds((groups - 1) * rows, rows)
            for a in range(2):
                dsum[pair, a, span] += dg_sum[pair, 2 + a].astype(F32)

        for n in range(groups):
            segment = n + jnp.where(h <= n, 1, 0) if n < groups - 1 else h
            place = lax.rem(segment + 2 * groups - 1 - h, groups)
            low = lax.rem(place + at_last, groups)
            high = lax.rem(place + groups - at_first, groups)
            span = pl.ds(pl.multiple_of(segment * rows, rows), rows)
            mine = (other == segment * columns + c).astype(F32)
            for a in range(2):
                whole = dsum[pair, a, span]
                whole += dside_in[pair, 0, a, low].astype(F32)
                whole += dside_in[pair, 1, a, high].astype(F32)
                whole += dg_sum[pair, a].astype(F32) * mine
                key_parts[pair, segment, a] = whole.astype(BF16)
            send_out(pair, segment, n < groups - 1, 2)

    def then(step, *rest):
        return functools.partial(step, *rest)

    send_in(0, 0)
    forward(0, {2: then(send_in, 0, 1)}, (2, 3))
    send_in(1, 0)
    choose(0)
    forward(1, {1: then(send_in, 1, 1)}, range(groups))
    ready(0)
    run(0, 3, False, False)
    choose(1)
    run(0, 2, False, False)
    send_dsides(0, 3)
    run(0, 1, False, False)
    send_dsides(0, 2)
    run(0, 0, (1,))
    ready(1)
    run(1, 3, False, False)
    send_dsides(0, 0)
    run(1, 2, False, False)
    gather(0)
    send_dsides(1, 3)
    run(1, 1, False, False)
    send_dsides(1, 2)
    run(1, 0, (1, 0))
    finish(0)
    gather(1)
    finish(1)

    shares = pl.ds(0, groups - 1)
    for n in range(2):
        settle(kv.at[:, :, shares], in_send.at[n])
        settle(kv.at[:, :, shares], out_send.at[n])
        settle(kv.at[:, :, shares], out_recv.at[n])
    settle(side, side_send.at[0])
    settle(dside, ds_send.at[0])
    settle(piece.at[:, pl.ds(0, columns - 1)], glob_send.at[0])
    settle(glob.at[:, :, pl.ds(0, rows - strip)], glob_send.at[1])
    settle(dg_in.at[:, pl.ds(0, columns - 1)], glob_send.at[2])
    settle(dg_sum.at[:, moving, pl.ds(0, rows - strip)], glob_send.at[3])

    @pl.when(c == columns - 1)
    def _():
        settle(glob.at[:, fixed, pl.ds(0, rows - strip)], fixed_send.at[0])

    @pl.when(c < columns - 1)
    def _():
        settle(glob.at[:, fixed, pl.ds(0, strip)], fixed_send.at[1])

    settle(kv.at[:, :, pl.ds(0, 2)], keep_sem.at[0])


def fused(groups, columns, query, keys, values, d_out, rand_blocks, global_blocks):
    rows, width = query.shape
    share = width // groups
    strip = rows // columns
    half = functools.partial(pltpu.VMEM, dtype=BF16)
    full = functools.partial(pltpu.VMEM, dtype=F32)
    dma = pltpu.SemaphoreType.DMA
    pairs = share // LANES
    tile = (rows, LANES)
    scratch = [
        half((pairs, 2, groups, *tile)),
        half((pairs, 2, groups, *tile)),
        half((pairs, 2, 2, groups, *tile)),
        half((pairs, 2, *tile)),
        half((pairs, columns, 2, strip, LANES)),
        half((pairs, 2 * GLOBALS, *tile)),
        full((pairs, 2, (groups + GLOBALS) * rows, LANES)),
        half((pairs, 2, 2, groups, *tile)),
        half((pairs, 2, 2, groups, *tile)),
        half((pairs, 2 * GLOBALS, *tile)),
        half((pairs, columns, 2 * GLOBALS, strip, LANES)),
        half((pairs, 2 * GLOBALS, *tile)),
    ] + [half((pairs, groups, 2, *tile))] * 2
    scratch += [dma((2, pairs))] + [dma((pairs, groups - 1))] * 2 + [dma((pairs,))] * 8
    scratch += [dma((2,)), dma((1,)), dma((4,)), dma((1,)), dma((2,)), dma((2,)), dma((1,)), dma((2,))]
    hbm = pl.BlockSpec(memory_space=pltpu.HBM)
    return pl.pallas_call(
        functools.partial(fused_kernel, groups, columns),
        out_shape=jax.ShapeDtypeStruct((4, rows, width), BF16),
        in_specs=[pl.BlockSpec(memory_space=pltpu.SMEM)] + [hbm] * 4,
        out_specs=hbm,
        scratch_shapes=scratch,
        compiler_params=pltpu.CompilerParams(
            collective_id=0, has_side_effects=True, vmem_limit_bytes=63 * 2**20
        ),
    )(global_blocks, query, keys, values, d_out)


CHUNKS = 4


def relay_kernel(source, *refs):
    targets, (held, in_sem, out_sem) = refs[:-3], refs[-3:]
    rows = held.shape[1] // CHUNKS
    parts = [pl.ds(part * rows, rows) for part in range(CHUNKS)]
    arrivals = [
        pltpu.make_async_copy(source.at[:, at], held.at[:, at], in_sem.at[part])
        for part, at in enumerate(parts)
    ]
    for copy in arrivals:
        copy.start()
    for copy, at in zip(arrivals, parts):
        copy.wait()
        for n, target in enumerate(targets):
            pltpu.make_async_copy(held.at[n, at], target.at[at], out_sem.at[0]).start()
    pltpu.make_async_copy(held, held, out_sem.at[0]).wait()


def relay(stacked):
    hbm = pl.BlockSpec(memory_space=pltpu.HBM)
    count, *shape = stacked.shape
    return pl.pallas_call(
        relay_kernel,
        out_shape=[jax.ShapeDtypeStruct(tuple(shape), stacked.dtype)] * count,
        in_specs=[hbm],
        out_specs=[hbm] * count,
        scratch_shapes=[
            pltpu.VMEM(stacked.shape, stacked.dtype),
            pltpu.SemaphoreType.DMA((CHUNKS,)),
            pltpu.SemaphoreType.DMA((1,)),
        ],
    )(stacked)


def solution(mesh):
    in_specs = (
        P(("grp", "seq"), None),
        P(("grp", "seq"), None),
        P(("grp", "seq"), None),
        P(("grp", "seq"), None),
        P(),
        P(),
    )
    out_specs = (
        P(("grp", "seq"), None),
        P(("grp", "seq"), None),
        P(("grp", "seq"), None),
        P(("grp", "seq"), None),
    )
    groups, columns = mesh.shape["grp"], mesh.shape["seq"]

    def run(query, *rest):
        rows, width = query.shape
        whole_column = rows == BLOCK and groups - 1 == RANDOMS and groups % 2 == 0
        if whole_column and rows % (16 * columns) == 0 and width == 2 * groups * LANES:
            return relay(fused(groups, columns, query, *rest))
        return body(query, *rest)

    return jax.shard_map(run, mesh=mesh, in_specs=in_specs, out_specs=out_specs, check_vma=False)
```

```python
import functools
import math

import jax
import jax.numpy as jnp
from jax import lax
from jax.experimental import pallas as pl
from jax.experimental.pallas import tpu as pltpu
from jax.sharding import PartitionSpec as P

HEAD_DIM = 64
BLOCK = 128
GLOBALS = 2
RANDOMS = 3
KEYS = 8


def extended(block, sides, width, periodic):
    for axis, dim in sides:
        count = lax.axis_size(axis)
        forward = [(i, i + 1) for i in range(count - 1)]
        if periodic:
            forward.append((count - 1, 0))
        backward = [(target, source) for source, target in forward]
        low = lax.ppermute(
            lax.slice_in_dim(block, block.shape[dim] - width, None, axis=dim), axis, forward
        )
        high = lax.ppermute(lax.slice_in_dim(block, 0, width, axis=dim), axis, backward)
        block = jnp.concatenate([low, block, high], axis=dim)
    return block


def broadcast(block, axis, source):
    block = jnp.where(lax.axis_index(axis) == source, block, jnp.zeros_like(block))
    return lax.psum(block, axis)


def attend_blocks(queries, key_rows, value_rows, grad_rows, key_valid):
    factor = 1.0 / math.sqrt(queries.shape[-1])
    scores = (
        jnp.einsum("nqhe,njkhe->nhqjk", queries, key_rows, preferred_element_type=jnp.float32)
        * factor
    )
    scores = jnp.where(key_valid[:, None, None, :, None], scores, -1e30)
    row_max = jnp.max(scores, axis=(3, 4), keepdims=True)
    raised = jnp.exp(scores - row_max)
    attn_prob = raised / jnp.sum(raised, axis=(3, 4), keepdims=True)
    prob_half = attn_prob.astype(jnp.bfloat16)
    result = jnp.einsum(
        "nhqjk,njkhe->nqhe", prob_half, value_rows, preferred_element_type=jnp.float32
    )
    d_prob = jnp.einsum(
        "nqhe,njkhe->nhqjk", grad_rows, value_rows, preferred_element_type=jnp.float32
    )
    row_dot = jnp.sum(attn_prob * d_prob, axis=(3, 4), keepdims=True)
    d_scores = (attn_prob * (d_prob - row_dot) * factor).astype(jnp.bfloat16)
    d_query = jnp.einsum(
        "nhqjk,njkhe->nqhe", d_scores, key_rows, preferred_element_type=jnp.float32
    )
    d_keys = jnp.einsum("nhqjk,nqhe->njkhe", d_scores, queries, preferred_element_type=jnp.float32)
    d_values = jnp.einsum(
        "nhqjk,nqhe->njkhe", prob_half, grad_rows, preferred_element_type=jnp.float32
    )
    return (result, d_query, d_keys, d_values)


def body(query, keys, values, d_out, rand_blocks, global_blocks):
    group_count = lax.axis_size("grp")
    column_count = lax.axis_size("seq")
    column = lax.axis_index("seq")
    tokens_dev = query.shape[0]
    width = query.shape[1]
    local_blocks = tokens_dev // BLOCK
    head_width = width // group_count
    heads_here = head_width // HEAD_DIM
    block_total = group_count * column_count * local_blocks
    segment_span = column_count * local_blocks
    stride = local_blocks + 2
    count = group_count * local_blocks
    per_step = 4
    steps_count = count // per_step
    stacked = jnp.stack([keys, values])
    widened = extended(stacked, ((("grp", "seq"), 1),), BLOCK, False)
    key_send = widened[0][None]
    value_send = widened[1][None]
    query_heads, grad_heads, key_heads, value_heads = (
        lax.all_to_all(
            query.reshape(1, tokens_dev, width), "grp", split_axis=2, concat_axis=0, tiled=True
        ),
        lax.all_to_all(
            d_out.reshape(1, tokens_dev, width), "grp", split_axis=2, concat_axis=0, tiled=True
        ),
        lax.all_to_all(key_send, "grp", split_axis=2, concat_axis=0, tiled=True),
        lax.all_to_all(value_send, "grp", split_axis=2, concat_axis=0, tiled=True),
    )
    ext_pair = jnp.stack([key_heads, value_heads]).reshape(
        2, group_count * stride, BLOCK, head_width
    )
    global_device = global_blocks // local_blocks
    global_segment = global_device // column_count
    global_column = global_device % column_count
    global_local = global_blocks % local_blocks
    global_rows = global_segment * stride + global_local + 1
    fetched = []
    for which in range(GLOBALS):
        fetched.append(broadcast(ext_pair[:, global_rows[which]], "seq", global_column[which]))
    global_pair = jnp.stack(fetched, axis=1)
    segment_of = jnp.repeat(jnp.arange(group_count, dtype=jnp.int32), local_blocks)
    local_of = jnp.tile(jnp.arange(local_blocks, dtype=jnp.int32), group_count)
    query_ids = (segment_of * column_count + column) * local_blocks + local_of
    rand_ids = jnp.take(rand_blocks, query_ids, axis=0)
    rand_rows = rand_ids // segment_span * stride + rand_ids % local_blocks + 1
    window_rows = (segment_of * stride + local_of)[:, None] + jnp.arange(3, dtype=jnp.int32)[
        None, :
    ]
    key_table = jnp.concatenate([window_rows, rand_rows], axis=1)
    key_valid = jnp.concatenate(
        [
            (query_ids > 0)[:, None],
            jnp.ones((count, 1), dtype=jnp.bool_),
            (query_ids < block_total - 1)[:, None],
            jnp.ones((count, GLOBALS + RANDOMS), dtype=jnp.bool_),
        ],
        axis=1,
    )
    query_steps = query_heads.reshape(steps_count, per_step, BLOCK, heads_here, HEAD_DIM)
    grad_steps = grad_heads.reshape(steps_count, per_step, BLOCK, heads_here, HEAD_DIM)
    table_steps = key_table.reshape(steps_count, per_step, 3 + RANDOMS)
    valid_steps = key_valid.reshape(steps_count, per_step, KEYS)
    global_spread = jnp.broadcast_to(
        global_pair[:, None], (2, per_step, GLOBALS, BLOCK, head_width)
    )

    def advance(totals, packed):
        ext_total, global_total = totals
        query_part, grad_part, rows_part, valid_part = packed
        taken = jnp.stack(
            [
                lax.dynamic_index_in_dim(ext_pair, row, axis=1, keepdims=False)
                for row in rows_part.reshape(-1)
            ],
            axis=1,
        ).reshape(2, per_step, 3 + RANDOMS, BLOCK, head_width)
        gathered = jnp.concatenate([taken[:, :, :3], global_spread, taken[:, :, 3:]], axis=2)
        gathered = gathered.reshape(2, per_step, KEYS, BLOCK, heads_here, HEAD_DIM)
        result, d_query, d_keys, d_values = attend_blocks(
            query_part, gathered[0], gathered[1], grad_part, valid_part
        )
        d_pair = jnp.stack([d_keys, d_values]).reshape(2, per_step, KEYS, BLOCK, head_width)
        spread_back = jnp.concatenate([d_pair[:, :, :3], d_pair[:, :, 3 + GLOBALS :]], axis=2)
        spread_back = spread_back.reshape(2, per_step * (3 + RANDOMS), BLOCK, head_width)
        ext_total = ext_total.at[:, rows_part.reshape(-1)].add(spread_back)
        global_total = global_total + jnp.sum(d_pair[:, :, 3 : 3 + GLOBALS], axis=1)
        return (
            (ext_total, global_total),
            (result.astype(jnp.bfloat16), d_query.astype(jnp.bfloat16)),
        )

    start_totals = (
        jnp.zeros((2, group_count * stride, BLOCK, head_width), jnp.float32),
        jnp.zeros((2, GLOBALS, BLOCK, head_width), jnp.float32),
    )
    totals, outputs = lax.scan(
        advance, start_totals, (query_steps, grad_steps, table_steps, valid_steps)
    )
    ext_total = totals[0].reshape(2, group_count, stride, BLOCK, head_width)
    global_sum = lax.psum(totals[1], "seq")
    own_grad = ext_total[:, :, 1 : local_blocks + 1]
    for which in range(GLOBALS):
        addend = jnp.where(column == global_column[which], global_sum[:, which], 0.0)
        own_grad = own_grad.at[:, global_segment[which], global_local[which]].add(addend)
    send_left = ext_total[:, :, 0]
    send_right = ext_total[:, :, local_blocks + 1]
    empty_edge = jnp.zeros_like(send_left[:, :1])
    send_left = jnp.where(
        column == 0, jnp.concatenate([send_left[:, 1:], empty_edge], axis=1), send_left
    )
    send_right = jnp.where(
        column == column_count - 1,
        jnp.concatenate([empty_edge, send_right[:, :-1]], axis=1),
        send_right,
    )
    edges = jnp.concatenate([send_left, send_right], axis=2)
    arrived = extended(edges, (("seq", 2),), BLOCK, True)
    own_grad = own_grad.at[:, :, 0].add(arrived[:, :, :BLOCK])
    own_grad = own_grad.at[:, :, local_blocks - 1].add(arrived[:, :, 3 * BLOCK :])
    head_shape = (group_count, tokens_dev, head_width)
    attended_heads = outputs[0].reshape(head_shape)
    d_query_heads = outputs[1].reshape(head_shape)
    d_key_heads = own_grad[0].reshape(head_shape).astype(jnp.bfloat16)
    d_value_heads = own_grad[1].reshape(head_shape).astype(jnp.bfloat16)
    returned = (
        lax.all_to_all(attended_heads, "grp", split_axis=0, concat_axis=2, tiled=True),
        lax.all_to_all(d_query_heads, "grp", split_axis=0, concat_axis=2, tiled=True),
        lax.all_to_all(d_key_heads, "grp", split_axis=0, concat_axis=2, tiled=True),
        lax.all_to_all(d_value_heads, "grp", split_axis=0, concat_axis=2, tiled=True),
    )
    return (
        returned[0].reshape(tokens_dev, width),
        returned[1].reshape(tokens_dev, width),
        returned[2].reshape(tokens_dev, width),
        returned[3].reshape(tokens_dev, width),
    )


MESH = pl.DeviceIdType.MESH
F32 = jnp.float32
BF16 = jnp.bfloat16
LANES = 128


def contract(left, right, dims):
    return lax.dot_general(left, right, (dims, ((), ())), preferred_element_type=F32)


def fused_kernel(
    groups, columns, global_ref, q_ref, k_ref, v_ref, g_ref,
    out_ref,
    qg, kv, side, cand, piece, glob, dsum, dside, dside_in, dg_out, dg_in, dg_sum,
    row_parts, key_parts,
    own_sem, kv_recv, qg_recv, side_recv, ga_recv, gb_recv, ds_recv, da_recv, db_recv,
    gs_recv, dt_recv, in_send, side_send, glob_send, ds_send, out_send, out_recv,
    keep_sem, fixed_send,
):
    h = lax.axis_index("grp")
    c = lax.axis_index("seq")
    rows, width = q_ref.shape
    share = width // groups
    strip = rows // columns
    pairs = share // LANES

    def rows_of(index):
        return pl.ds(pl.multiple_of(index * strip, strip), strip)

    def remote(src, dst, send, recv, device):
        return pltpu.make_async_remote_copy(
            src_ref=src, dst_ref=dst, send_sem=send, recv_sem=recv,
            device_id=device, device_id_type=MESH,
        )

    def settle(ref, sem):
        pltpu.make_async_copy(ref, ref, sem).wait()

    right = lax.rem(c + 1, columns)
    left = lax.rem(c + columns - 1, columns)

    barrier = pltpu.get_barrier_semaphore()
    for d in range(1, groups):
        pl.semaphore_signal(
            barrier, inc=1, device_id=(lax.rem(h + d, groups), c), device_id_type=MESH
        )
    for e in range(1, columns):
        pl.semaphore_signal(
            barrier, inc=1, device_id=(h, lax.rem(c + e, columns)), device_id_type=MESH
        )

    def lanes_of(index, pair):
        return pl.ds(pl.multiple_of(index * share + pair * LANES, LANES), LANES)

    own = []
    for pair in range(pairs):
        for kind, (refs, buf) in enumerate((((k_ref, v_ref), kv), ((q_ref, g_ref), qg))):
            for a, ref in enumerate(refs):
                own.append(
                    pltpu.make_async_copy(
                        ref.at[:, lanes_of(h, pair)], buf.at[pair, a, h], own_sem.at[kind, pair]
                    )
                )
    for copy in own:
        copy.start()
    pl.semaphore_wait(barrier, groups + columns - 2)

    def send_in(kind, pair):
        refs, buf = (((k_ref, v_ref), kv), ((q_ref, g_ref), qg))[kind]
        for d in range(1, groups):
            target = lax.rem(h + d, groups)
            arrival = (kv_recv, qg_recv)[kind].at[pair, d - 1]
            for a, ref in enumerate(refs):
                remote(
                    ref.at[:, lanes_of(target, pair)], buf.at[pair, a, h],
                    in_send.at[kind], arrival, (target, c),
                ).start()

    def send_sides(pair, d):
        segment = lax.rem(h + groups - d, groups)
        for way, to in ((0, right), (1, left)):
            remote(
                kv.at[pair, :, segment], side.at[pair, way, :, segment],
                side_send.at[0], side_recv.at[pair], (h, to),
            ).start()

    def forward(pair, between, held=()):
        settle(kv.at[pair, :, h], own_sem.at[0, pair])
        if 0 not in held:
            send_sides(pair, 0)
        for d in range(1, groups):
            settle(kv.at[pair, :, lax.rem(h + groups - d, groups)], kv_recv.at[pair, d - 1])
            if d not in held:
                send_sides(pair, d)
            if d in between:
                between[d]()
        offer(pair)
        for d in held:
            send_sides(pair, d)

    last = groups * columns - 1
    other = global_ref[0] + global_ref[1] - last
    seg_of = lax.div(other, columns)
    col_of = lax.rem(other, columns)
    moving, fixed = pl.ds(0, 2), pl.ds(2, 2)

    def offer(pair):
        for a in range(2):
            chosen = kv[pair, a, 0]
            for t in range(1, groups):
                chosen = jnp.where(seg_of == t, kv[pair, a, t], chosen)
            cand[pair, a] = chosen
        for e in range(1, columns):
            to = lax.rem(c + e, columns)
            remote(
                cand.at[pair, :, rows_of(to), :], piece.at[pair, c],
                glob_send.at[0], ga_recv.at[pair], (h, to),
            ).start()
        piece[pair, c] = cand[pair, :, rows_of(c), :]

        @pl.when(c == columns - 1)
        def _():
            for to in range(columns - 1):
                remote(
                    kv.at[pair, :, groups - 1, rows_of(to), :],
                    glob.at[pair, fixed, rows_of(to), :],
                    fixed_send.at[0], gs_recv.at[pair], (h, to),
                ).start()
            for a in range(2):
                glob[pair, 2 + a, rows_of(c), :] = kv[pair, a, groups - 1, rows_of(c), :]

    def choose(pair):
        settle(piece.at[pair, pl.ds(0, columns - 1)], ga_recv.at[pair])
        for a in range(2):
            chosen = piece[pair, 0, a]
            for e in range(1, columns):
                chosen = jnp.where(col_of == e, piece[pair, e, a], chosen)
            glob[pair, a, rows_of(c), :] = chosen

        @pl.when(c < columns - 1)
        def _():
            settle(glob.at[pair, fixed, rows_of(c), :], gs_recv.at[pair])

        for e in range(1, columns):
            to = lax.rem(c + e, columns)
            remote(
                glob.at[pair, :, rows_of(c), :], glob.at[pair, :, rows_of(c), :],
                glob_send.at[1], gb_recv.at[pair], (h, to),
            ).start()

    lane = lax.broadcasted_iota(jnp.int32, (rows, LANES), 1)
    factor = 1.0 / math.sqrt(HEAD_DIM)

    def stacked(block):
        zero = jnp.zeros_like(block)
        low = jnp.where(lane < HEAD_DIM, block, zero)
        high = jnp.where(lane < HEAD_DIM, zero, block)
        return jnp.concatenate([low, high], axis=0)

    def picked(wide):
        return jnp.concatenate(
            [wide[:HEAD_DIM, :rows], wide[HEAD_DIM:, rows:]], axis=0
        ).T

    def send_out(pair, segment, away, first):
        buf = (row_parts, key_parts)[first // 2]
        target = out_ref.at[pl.ds(first, 2), :, lanes_of(h, pair)]
        if away:
            remote(
                buf.at[pair, segment], target,
                out_send.at[first // 2], out_recv.at[first // 2], (segment, c),
            ).start()
        else:
            pltpu.make_async_copy(buf.at[pair, h], target, keep_sem.at[0]).start()

    def send_dsides(pair, i):
        for way, to in ((0, left), (1, right)):
            remote(
                dside.at[pair, way, :, i], dside_in.at[pair, way, :, i],
                ds_send.at[0], ds_recv.at[pair], (h, to),
            ).start()

    at_first = jnp.where(c == 0, 1, 0)
    at_last = jnp.where(c == columns - 1, 1, 0)
    dense = (groups + GLOBALS) * rows

    def unit(pair, i):
        segment = lax.rem(h + i + 1, groups)
        block = segment * columns + c
        before = lax.rem(segment + groups - at_first, groups)
        after = lax.rem(segment + at_last, groups)

        def listed(a):
            return jnp.concatenate(
                [kv[pair, a, t] for t in range(groups)]
                + [glob[pair, 2 * w + a] for w in range(GLOBALS)]
                + [side[pair, 0, a, before], side[pair, 1, a, after]],
                axis=0,
            )

        key = listed(0)
        value = listed(1)
        query = stacked(qg[pair, 0, segment] * jnp.asarray(factor, BF16))
        grad = stacked(qg[pair, 1, segment])
        scores = contract(key, query, ((1,), (1,)))
        scores = jnp.concatenate(
            [
                scores[:dense],
                jnp.where(block > 0, scores[dense : dense + rows], -1e30),
                jnp.where(block < last, scores[dense + rows :], -1e30),
            ],
            axis=0,
        )
        raised = jnp.exp(scores - jnp.max(scores, axis=0, keepdims=True))
        prob = raised * (1.0 / jnp.sum(raised, axis=0, keepdims=True))
        half = prob.astype(BF16)
        d_prob = contract(value, grad, ((1,), (1,)))
        row_dot = jnp.sum(prob * d_prob, axis=0, keepdims=True)
        d_scores = (prob * (d_prob - row_dot)).astype(BF16)

        def part(start, stop):
            return (
                contract(d_scores[start:stop], query, ((1,), (0,))),
                contract(half[start:stop], grad, ((1,), (0,))),
            )

        def rows_out():
            result = contract(value, half, ((0,), (0,)))
            d_query = contract(key, d_scores, ((0,), (0,))) * factor
            row_parts[pair, segment, 0] = picked(result).astype(BF16)
            row_parts[pair, segment, 1] = picked(d_query).astype(BF16)

        return part, rows_out

    def ready(pair):
        settle(side.at[pair], side_recv.at[pair])
        settle(glob.at[pair, :, pl.ds(0, rows - strip)], gb_recv.at[pair])
        settle(qg.at[pair, :, h], own_sem.at[1, pair])

    def run(pair, i, closing=(), share_now=True):
        segment = lax.rem(h + i + 1, groups)
        if i < groups - 1:
            settle(qg.at[pair, :, segment], qg_recv.at[pair, groups - 2 - i])
        part, rows_out = unit(pair, i)

        def summed(start, stop):
            grads = part(start, stop)
            for a in range(2):
                if i == groups - 1:
                    dsum[pair, a, start:stop] = grads[a]
                else:
                    dsum[pair, a, start:stop] += grads[a]

        def sides_out():
            grads = part(dense, dense + 2 * rows)
            for a in range(2):
                dside[pair, 0, a, i] = grads[a][:rows].astype(BF16)
                dside[pair, 1, a, i] = grads[a][rows:].astype(BF16)

        if closing:
            summed(groups * rows, dense)
            scatter(pair)
            sides_out()
            for late in closing:
                send_dsides(pair, late)
            rows_out()
            send_out(pair, segment, i < groups - 1, 0)
            summed(0, groups * rows)
        else:
            rows_out()
            send_out(pair, segment, i < groups - 1, 0)
            summed(0, dense)
            sides_out()
            if share_now:
                send_dsides(pair, i)

    def scatter(pair):
        for w in range(GLOBALS):
            for a in range(2):
                start = (groups + w) * rows
                dg_out[pair, 2 * w + a] = dsum[pair, a, start : start + rows].astype(BF16)
        for e in range(1, columns):
            to = lax.rem(c + e, columns)
            remote(
                dg_out.at[pair, :, rows_of(to), :], dg_in.at[pair, c],
                glob_send.at[2], da_recv.at[pair], (h, to),
            ).start()
        dg_in[pair, c] = dg_out[pair, :, rows_of(c), :]

    def gather(pair):
        settle(dg_in.at[pair, pl.ds(0, columns - 1)], da_recv.at[pair])
        total = dg_in[pair, 0].astype(F32)
        for e in range(1, columns):
            total = total + dg_in[pair, e].astype(F32)
        dg_sum[pair, :, rows_of(c), :] = total.astype(BF16)
        for e in range(1, columns):
            to = lax.rem(c + e, columns)
            remote(
                dg_sum.at[pair, moving, rows_of(c), :], dg_sum.at[pair, moving, rows_of(c), :],
                glob_send.at[3], db_recv.at[pair], (h, to),
            ).start()

        @pl.when(c < columns - 1)
        def _():
            remote(
                dg_sum.at[pair, fixed, rows_of(c), :], dg_sum.at[pair, fixed, rows_of(c), :],
                fixed_send.at[1], dt_recv.at[pair], (h, columns - 1),
            ).start()

    def finish(pair):
        settle(dside_in.at[pair], ds_recv.at[pair])
        settle(dg_sum.at[pair, moving, pl.ds(0, rows - strip)], db_recv.at[pair])

        @pl.when(c == columns - 1)
        def _():
            settle(dg_sum.at[pair, fixed, pl.ds(0, rows - strip)], dt_recv.at[pair])
            span = pl.ds((groups - 1) * rows, rows)
            for a in range(2):
                dsum[pair, a, span] += dg_sum[pair, 2 + a].astype(F32)

        for n in range(groups):
            segment = n + jnp.where(h <= n, 1, 0) if n < groups - 1 else h
            place = lax.rem(segment + 2 * groups - 1 - h, groups)
            low = lax.rem(place + at_last, groups)
            high = lax.rem(place + groups - at_first, groups)
            span = pl.ds(pl.multiple_of(segment * rows, rows), rows)
            mine = (other == segment * columns + c).astype(F32)
            for a in range(2):
                whole = dsum[pair, a, span]
                whole += dside_in[pair, 0, a, low].astype(F32)
                whole += dside_in[pair, 1, a, high].astype(F32)
                whole += dg_sum[pair, a].astype(F32) * mine
                key_parts[pair, segment, a] = whole.astype(BF16)
            send_out(pair, segment, n < groups - 1, 2)

    def then(step, *rest):
        return functools.partial(step, *rest)

    send_in(0, 0)
    forward(0, {2: then(send_in, 0, 1)}, (2, 3))
    send_in(1, 0)
    choose(0)
    forward(1, {1: then(send_in, 1, 1)}, range(groups))
    ready(0)
    run(0, 3, False, False)
    choose(1)
    run(0, 2, False, False)
    send_dsides(0, 3)
    run(0, 1, False, False)
    send_dsides(0, 2)
    run(0, 0, (1,))
    ready(1)
    run(1, 3, False, False)
    send_dsides(0, 0)
    run(1, 2, False, False)
    gather(0)
    send_dsides(1, 3)
    run(1, 1, False, False)
    send_dsides(1, 2)
    run(1, 0, (1, 0))
    finish(0)
    gather(1)
    finish(1)

    shares = pl.ds(0, groups - 1)
    for n in range(2):
        settle(kv.at[:, :, shares], in_send.at[n])
        settle(kv.at[:, :, shares], out_send.at[n])
        settle(kv.at[:, :, shares], out_recv.at[n])
    settle(side, side_send.at[0])
    settle(dside, ds_send.at[0])
    settle(piece.at[:, pl.ds(0, columns - 1)], glob_send.at[0])
    settle(glob.at[:, :, pl.ds(0, rows - strip)], glob_send.at[1])
    settle(dg_in.at[:, pl.ds(0, columns - 1)], glob_send.at[2])
    settle(dg_sum.at[:, moving, pl.ds(0, rows - strip)], glob_send.at[3])

    @pl.when(c == columns - 1)
    def _():
        settle(glob.at[:, fixed, pl.ds(0, rows - strip)], fixed_send.at[0])

    @pl.when(c < columns - 1)
    def _():
        settle(glob.at[:, fixed, pl.ds(0, strip)], fixed_send.at[1])

    settle(kv.at[:, :, pl.ds(0, 2)], keep_sem.at[0])


def fused(groups, columns, query, keys, values, d_out, rand_blocks, global_blocks):
    rows, width = query.shape
    share = width // groups
    strip = rows // columns
    half = functools.partial(pltpu.VMEM, dtype=BF16)
    full = functools.partial(pltpu.VMEM, dtype=F32)
    dma = pltpu.SemaphoreType.DMA
    pairs = share // LANES
    tile = (rows, LANES)
    scratch = [
        half((pairs, 2, groups, *tile)),
        half((pairs, 2, groups, *tile)),
        half((pairs, 2, 2, groups, *tile)),
        half((pairs, 2, *tile)),
        half((pairs, columns, 2, strip, LANES)),
        half((pairs, 2 * GLOBALS, *tile)),
        full((pairs, 2, (groups + GLOBALS) * rows, LANES)),
        half((pairs, 2, 2, groups, *tile)),
        half((pairs, 2, 2, groups, *tile)),
        half((pairs, 2 * GLOBALS, *tile)),
        half((pairs, columns, 2 * GLOBALS, strip, LANES)),
        half((pairs, 2 * GLOBALS, *tile)),
    ] + [half((pairs, groups, 2, *tile))] * 2
    scratch += [dma((2, pairs))] + [dma((pairs, groups - 1))] * 2 + [dma((pairs,))] * 8
    scratch += [dma((2,)), dma((1,)), dma((4,)), dma((1,)), dma((2,)), dma((2,)), dma((1,)), dma((2,))]
    hbm = pl.BlockSpec(memory_space=pltpu.HBM)
    return pl.pallas_call(
        functools.partial(fused_kernel, groups, columns),
        out_shape=jax.ShapeDtypeStruct((4, rows, width), BF16),
        in_specs=[pl.BlockSpec(memory_space=pltpu.SMEM)] + [hbm] * 4,
        out_specs=hbm,
        scratch_shapes=scratch,
        compiler_params=pltpu.CompilerParams(
            collective_id=0, has_side_effects=True, vmem_limit_bytes=63 * 2**20
        ),
    )(global_blocks, query, keys, values, d_out)


CHUNKS = 4


def relay_kernel(source, *refs):
    targets, (held, in_sem, out_sem) = refs[:-3], refs[-3:]
    rows = held.shape[1] // CHUNKS
    parts = [pl.ds(part * rows, rows) for part in range(CHUNKS)]
    arrivals = [
        pltpu.make_async_copy(source.at[:, at], held.at[:, at], in_sem.at[part])
        for part, at in enumerate(parts)
    ]
    for copy in arrivals:
        copy.start()
    for copy, at in zip(arrivals, parts):
        copy.wait()
        for n, target in enumerate(targets):
            pltpu.make_async_copy(held.at[n, at], target.at[at], out_sem.at[0]).start()
    pltpu.make_async_copy(held, held, out_sem.at[0]).wait()


def relay(stacked):
    hbm = pl.BlockSpec(memory_space=pltpu.HBM)
    count, *shape = stacked.shape
    return pl.pallas_call(
        relay_kernel,
        out_shape=[jax.ShapeDtypeStruct(tuple(shape), stacked.dtype)] * count,
        in_specs=[hbm],
        out_specs=[hbm] * count,
        scratch_shapes=[
            pltpu.VMEM(stacked.shape, stacked.dtype),
            pltpu.SemaphoreType.DMA((CHUNKS,)),
            pltpu.SemaphoreType.DMA((1,)),
        ],
    )(stacked)


def solution(mesh):
    in_specs = (
        P(("grp", "seq"), None),
        P(("grp", "seq"), None),
        P(("grp", "seq"), None),
        P(("grp", "seq"), None),
        P(),
        P(),
    )
    out_specs = (
        P(("grp", "seq"), None),
        P(("grp", "seq"), None),
        P(("grp", "seq"), None),
        P(("grp", "seq"), None),
    )
    groups, columns = mesh.shape["grp"], mesh.shape["seq"]

    def run(query, *rest):
        rows, width = query.shape
        whole_column = rows == BLOCK and groups - 1 == RANDOMS and groups % 2 == 0
        if whole_column and rows % (16 * columns) == 0 and width == 2 * groups * LANES:
            return relay(fused(groups, columns, query, *rest))
        return body(query, *rest)

    return jax.shard_map(run, mesh=mesh, in_specs=in_specs, out_specs=out_specs, check_vma=False)
```

```python
import functools
import math

import jax
import jax.numpy as jnp
from jax import lax
from jax.experimental import pallas as pl
from jax.experimental.pallas import tpu as pltpu
from jax.sharding import PartitionSpec as P

HEAD_DIM = 64
BLOCK = 128
GLOBALS = 2
RANDOMS = 3
KEYS = 8


def extended(block, sides, width, periodic):
    for axis, dim in sides:
        count = lax.axis_size(axis)
        forward = [(i, i + 1) for i in range(count - 1)]
        if periodic:
            forward.append((count - 1, 0))
        backward = [(target, source) for source, target in forward]
        low = lax.ppermute(
            lax.slice_in_dim(block, block.shape[dim] - width, None, axis=dim), axis, forward
        )
        high = lax.ppermute(lax.slice_in_dim(block, 0, width, axis=dim), axis, backward)
        block = jnp.concatenate([low, block, high], axis=dim)
    return block


def broadcast(block, axis, source):
    block = jnp.where(lax.axis_index(axis) == source, block, jnp.zeros_like(block))
    return lax.psum(block, axis)


def attend_blocks(queries, key_rows, value_rows, grad_rows, key_valid):
    factor = 1.0 / math.sqrt(queries.shape[-1])
    scores = (
        jnp.einsum("nqhe,njkhe->nhqjk", queries, key_rows, preferred_element_type=jnp.float32)
        * factor
    )
    scores = jnp.where(key_valid[:, None, None, :, None], scores, -1e30)
    row_max = jnp.max(scores, axis=(3, 4), keepdims=True)
    raised = jnp.exp(scores - row_max)
    attn_prob = raised / jnp.sum(raised, axis=(3, 4), keepdims=True)
    prob_half = attn_prob.astype(jnp.bfloat16)
    result = jnp.einsum(
        "nhqjk,njkhe->nqhe", prob_half, value_rows, preferred_element_type=jnp.float32
    )
    d_prob = jnp.einsum(
        "nqhe,njkhe->nhqjk", grad_rows, value_rows, preferred_element_type=jnp.float32
    )
    row_dot = jnp.sum(attn_prob * d_prob, axis=(3, 4), keepdims=True)
    d_scores = (attn_prob * (d_prob - row_dot) * factor).astype(jnp.bfloat16)
    d_query = jnp.einsum(
        "nhqjk,njkhe->nqhe", d_scores, key_rows, preferred_element_type=jnp.float32
    )
    d_keys = jnp.einsum("nhqjk,nqhe->njkhe", d_scores, queries, preferred_element_type=jnp.float32)
    d_values = jnp.einsum(
        "nhqjk,nqhe->njkhe", prob_half, grad_rows, preferred_element_type=jnp.float32
    )
    return (result, d_query, d_keys, d_values)


def body(query, keys, values, d_out, rand_blocks, global_blocks):
    group_count = lax.axis_size("grp")
    column_count = lax.axis_size("seq")
    column = lax.axis_index("seq")
    tokens_dev = query.shape[0]
    width = query.shape[1]
    local_blocks = tokens_dev // BLOCK
    head_width = width // group_count
    heads_here = head_width // HEAD_DIM
    block_total = group_count * column_count * local_blocks
    segment_span = column_count * local_blocks
    stride = local_blocks + 2
    count = group_count * local_blocks
    per_step = 4
    steps_count = count // per_step
    stacked = jnp.stack([keys, values])
    widened = extended(stacked, ((("grp", "seq"), 1),), BLOCK, False)
    key_send = widened[0][None]
    value_send = widened[1][None]
    query_heads, grad_heads, key_heads, value_heads = (
        lax.all_to_all(
            query.reshape(1, tokens_dev, width), "grp", split_axis=2, concat_axis=0, tiled=True
        ),
        lax.all_to_all(
            d_out.reshape(1, tokens_dev, width), "grp", split_axis=2, concat_axis=0, tiled=True
        ),
        lax.all_to_all(key_send, "grp", split_axis=2, concat_axis=0, tiled=True),
        lax.all_to_all(value_send, "grp", split_axis=2, concat_axis=0, tiled=True),
    )
    ext_pair = jnp.stack([key_heads, value_heads]).reshape(
        2, group_count * stride, BLOCK, head_width
    )
    global_device = global_blocks // local_blocks
    global_segment = global_device // column_count
    global_column = global_device % column_count
    global_local = global_blocks % local_blocks
    global_rows = global_segment * stride + global_local + 1
    fetched = []
    for which in range(GLOBALS):
        fetched.append(broadcast(ext_pair[:, global_rows[which]], "seq", global_column[which]))
    global_pair = jnp.stack(fetched, axis=1)
    segment_of = jnp.repeat(jnp.arange(group_count, dtype=jnp.int32), local_blocks)
    local_of = jnp.tile(jnp.arange(local_blocks, dtype=jnp.int32), group_count)
    query_ids = (segment_of * column_count + column) * local_blocks + local_of
    rand_ids = jnp.take(rand_blocks, query_ids, axis=0)
    rand_rows = rand_ids // segment_span * stride + rand_ids % local_blocks + 1
    window_rows = (segment_of * stride + local_of)[:, None] + jnp.arange(3, dtype=jnp.int32)[
        None, :
    ]
    key_table = jnp.concatenate([window_rows, rand_rows], axis=1)
    key_valid = jnp.concatenate(
        [
            (query_ids > 0)[:, None],
            jnp.ones((count, 1), dtype=jnp.bool_),
            (query_ids < block_total - 1)[:, None],
            jnp.ones((count, GLOBALS + RANDOMS), dtype=jnp.bool_),
        ],
        axis=1,
    )
    query_steps = query_heads.reshape(steps_count, per_step, BLOCK, heads_here, HEAD_DIM)
    grad_steps = grad_heads.reshape(steps_count, per_step, BLOCK, heads_here, HEAD_DIM)
    table_steps = key_table.reshape(steps_count, per_step, 3 + RANDOMS)
    valid_steps = key_valid.reshape(steps_count, per_step, KEYS)
    global_spread = jnp.broadcast_to(
        global_pair[:, None], (2, per_step, GLOBALS, BLOCK, head_width)
    )

    def advance(totals, packed):
        ext_total, global_total = totals
        query_part, grad_part, rows_part, valid_part = packed
        taken = jnp.stack(
            [
                lax.dynamic_index_in_dim(ext_pair, row, axis=1, keepdims=False)
                for row in rows_part.reshape(-1)
            ],
            axis=1,
        ).reshape(2, per_step, 3 + RANDOMS, BLOCK, head_width)
        gathered = jnp.concatenate([taken[:, :, :3], global_spread, taken[:, :, 3:]], axis=2)
        gathered = gathered.reshape(2, per_step, KEYS, BLOCK, heads_here, HEAD_DIM)
        result, d_query, d_keys, d_values = attend_blocks(
            query_part, gathered[0], gathered[1], grad_part, valid_part
        )
        d_pair = jnp.stack([d_keys, d_values]).reshape(2, per_step, KEYS, BLOCK, head_width)
        spread_back = jnp.concatenate([d_pair[:, :, :3], d_pair[:, :, 3 + GLOBALS :]], axis=2)
        spread_back = spread_back.reshape(2, per_step * (3 + RANDOMS), BLOCK, head_width)
        ext_total = ext_total.at[:, rows_part.reshape(-1)].add(spread_back)
        global_total = global_total + jnp.sum(d_pair[:, :, 3 : 3 + GLOBALS], axis=1)
        return (
            (ext_total, global_total),
            (result.astype(jnp.bfloat16), d_query.astype(jnp.bfloat16)),
        )

    start_totals = (
        jnp.zeros((2, group_count * stride, BLOCK, head_width), jnp.float32),
        jnp.zeros((2, GLOBALS, BLOCK, head_width), jnp.float32),
    )
    totals, outputs = lax.scan(
        advance, start_totals, (query_steps, grad_steps, table_steps, valid_steps)
    )
    ext_total = totals[0].reshape(2, group_count, stride, BLOCK, head_width)
    global_sum = lax.psum(totals[1], "seq")
    own_grad = ext_total[:, :, 1 : local_blocks + 1]
    for which in range(GLOBALS):
        addend = jnp.where(column == global_column[which], global_sum[:, which], 0.0)
        own_grad = own_grad.at[:, global_segment[which], global_local[which]].add(addend)
    send_left = ext_total[:, :, 0]
    send_right = ext_total[:, :, local_blocks + 1]
    empty_edge = jnp.zeros_like(send_left[:, :1])
    send_left = jnp.where(
        column == 0, jnp.concatenate([send_left[:, 1:], empty_edge], axis=1), send_left
    )
    send_right = jnp.where(
        column == column_count - 1,
        jnp.concatenate([empty_edge, send_right[:, :-1]], axis=1),
        send_right,
    )
    edges = jnp.concatenate([send_left, send_right], axis=2)
    arrived = extended(edges, (("seq", 2),), BLOCK, True)
    own_grad = own_grad.at[:, :, 0].add(arrived[:, :, :BLOCK])
    own_grad = own_grad.at[:, :, local_blocks - 1].add(arrived[:, :, 3 * BLOCK :])
    head_shape = (group_count, tokens_dev, head_width)
    attended_heads = outputs[0].reshape(head_shape)
    d_query_heads = outputs[1].reshape(head_shape)
    d_key_heads = own_grad[0].reshape(head_shape).astype(jnp.bfloat16)
    d_value_heads = own_grad[1].reshape(head_shape).astype(jnp.bfloat16)
    returned = (
        lax.all_to_all(attended_heads, "grp", split_axis=0, concat_axis=2, tiled=True),
        lax.all_to_all(d_query_heads, "grp", split_axis=0, concat_axis=2, tiled=True),
        lax.all_to_all(d_key_heads, "grp", split_axis=0, concat_axis=2, tiled=True),
        lax.all_to_all(d_value_heads, "grp", split_axis=0, concat_axis=2, tiled=True),
    )
    return (
        returned[0].reshape(tokens_dev, width),
        returned[1].reshape(tokens_dev, width),
        returned[2].reshape(tokens_dev, width),
        returned[3].reshape(tokens_dev, width),
    )


MESH = pl.DeviceIdType.MESH
F32 = jnp.float32
BF16 = jnp.bfloat16
LANES = 128


def contract(left, right, dims):
    return lax.dot_general(left, right, (dims, ((), ())), preferred_element_type=F32)


def fused_kernel(
    groups, columns, global_ref, q_ref, k_ref, v_ref, g_ref,
    out_ref,
    qg, kv, side, cand, piece, glob, dsum, dside, dside_in, dg_out, dg_in, dg_sum,
    row_parts, key_parts,
    own_sem, kv_recv, qg_recv, side_recv, ga_recv, gb_recv, ds_recv, da_recv, db_recv,
    gs_recv, dt_recv, in_send, side_send, glob_send, ds_send, out_send, out_recv,
    keep_sem, fixed_send,
):
    h = lax.axis_index("grp")
    c = lax.axis_index("seq")
    rows, width = q_ref.shape
    share = width // groups
    strip = rows // columns
    pairs = share // LANES

    def rows_of(index):
        return pl.ds(pl.multiple_of(index * strip, strip), strip)

    def remote(src, dst, send, recv, device):
        return pltpu.make_async_remote_copy(
            src_ref=src, dst_ref=dst, send_sem=send, recv_sem=recv,
            device_id=device, device_id_type=MESH,
        )

    def settle(ref, sem):
        pltpu.make_async_copy(ref, ref, sem).wait()

    right = lax.rem(c + 1, columns)
    left = lax.rem(c + columns - 1, columns)

    barrier = pltpu.get_barrier_semaphore()
    for d in range(1, groups):
        pl.semaphore_signal(
            barrier, inc=1, device_id=(lax.rem(h + d, groups), c), device_id_type=MESH
        )
    for e in range(1, columns):
        pl.semaphore_signal(
            barrier, inc=1, device_id=(h, lax.rem(c + e, columns)), device_id_type=MESH
        )

    def lanes_of(index, pair):
        return pl.ds(pl.multiple_of(index * share + pair * LANES, LANES), LANES)

    own = []
    for pair in range(pairs):
        for kind, (refs, buf) in enumerate((((k_ref, v_ref), kv), ((q_ref, g_ref), qg))):
            for a, ref in enumerate(refs):
                own.append(
                    pltpu.make_async_copy(
                        ref.at[:, lanes_of(h, pair)], buf.at[pair, a, h], own_sem.at[kind, pair]
                    )
                )
    for copy in own:
        copy.start()
    pl.semaphore_wait(barrier, groups + columns - 2)

    def send_in(kind, pair):
        refs, buf = (((k_ref, v_ref), kv), ((q_ref, g_ref), qg))[kind]
        for d in range(1, groups):
            target = lax.rem(h + d, groups)
            arrival = (kv_recv, qg_recv)[kind].at[pair, d - 1]
            for a, ref in enumerate(refs):
                remote(
                    ref.at[:, lanes_of(target, pair)], buf.at[pair, a, h],
                    in_send.at[kind], arrival, (target, c),
                ).start()

    def send_sides(pair, d):
        segment = lax.rem(h + groups - d, groups)
        for way, to in ((0, right), (1, left)):
            remote(
                kv.at[pair, :, segment], side.at[pair, way, :, segment],
                side_send.at[0], side_recv.at[pair], (h, to),
            ).start()

    def forward(pair, between, held=()):
        settle(kv.at[pair, :, h], own_sem.at[0, pair])
        if 0 not in held:
            send_sides(pair, 0)
        for d in range(1, groups):
            settle(kv.at[pair, :, lax.rem(h + groups - d, groups)], kv_recv.at[pair, d - 1])
            if d not in held:
                send_sides(pair, d)
            if d in between:
                between[d]()
        offer(pair)
        for d in held:
            send_sides(pair, d)

    last = groups * columns - 1
    other = global_ref[0] + global_ref[1] - last
    seg_of = lax.div(other, columns)
    col_of = lax.rem(other, columns)
    moving, fixed = pl.ds(0, 2), pl.ds(2, 2)

    def offer(pair):
        for a in range(2):
            chosen = kv[pair, a, 0]
            for t in range(1, groups):
                chosen = jnp.where(seg_of == t, kv[pair, a, t], chosen)
            cand[pair, a] = chosen
        for e in range(1, columns):
            to = lax.rem(c + e, columns)
            remote(
                cand.at[pair, :, rows_of(to), :], piece.at[pair, c],
                glob_send.at[0], ga_recv.at[pair], (h, to),
            ).start()
        piece[pair, c] = cand[pair, :, rows_of(c), :]

        @pl.when(c == columns - 1)
        def _():
            for to in range(columns - 1):
                remote(
                    kv.at[pair, :, groups - 1, rows_of(to), :],
                    glob.at[pair, fixed, rows_of(to), :],
                    fixed_send.at[0], gs_recv.at[pair], (h, to),
                ).start()
            for a in range(2):
                glob[pair, 2 + a, rows_of(c), :] = kv[pair, a, groups - 1, rows_of(c), :]

    def choose(pair):
        settle(piece.at[pair, pl.ds(0, columns - 1)], ga_recv.at[pair])
        for a in range(2):
            chosen = piece[pair, 0, a]
            for e in range(1, columns):
                chosen = jnp.where(col_of == e, piece[pair, e, a], chosen)
            glob[pair, a, rows_of(c), :] = chosen

        @pl.when(c < columns - 1)
        def _():
            settle(glob.at[pair, fixed, rows_of(c), :], gs_recv.at[pair])

        for e in range(1, columns):
            to = lax.rem(c + e, columns)
            remote(
                glob.at[pair, :, rows_of(c), :], glob.at[pair, :, rows_of(c), :],
                glob_send.at[1], gb_recv.at[pair], (h, to),
            ).start()

    lane = lax.broadcasted_iota(jnp.int32, (rows, LANES), 1)
    factor = 1.0 / math.sqrt(HEAD_DIM)

    def stacked(block):
        zero = jnp.zeros_like(block)
        low = jnp.where(lane < HEAD_DIM, block, zero)
        high = jnp.where(lane < HEAD_DIM, zero, block)
        return jnp.concatenate([low, high], axis=0)

    def picked(wide):
        return jnp.concatenate(
            [wide[:HEAD_DIM, :rows], wide[HEAD_DIM:, rows:]], axis=0
        ).T

    def send_out(pair, segment, away, first):
        buf = (row_parts, key_parts)[first // 2]
        target = out_ref.at[pl.ds(first, 2), :, lanes_of(h, pair)]
        if away:
            remote(
                buf.at[pair, segment], target,
                out_send.at[first // 2], out_recv.at[first // 2], (segment, c),
            ).start()
        else:
            pltpu.make_async_copy(buf.at[pair, h], target, keep_sem.at[0]).start()

    def send_dsides(pair, i):
        for way, to in ((0, left), (1, right)):
            remote(
                dside.at[pair, way, :, i], dside_in.at[pair, way, :, i],
                ds_send.at[0], ds_recv.at[pair], (h, to),
            ).start()

    at_first = jnp.where(c == 0, 1, 0)
    at_last = jnp.where(c == columns - 1, 1, 0)
    dense = (groups + GLOBALS) * rows

    def unit(pair, i):
        segment = lax.rem(h + i + 1, groups)
        block = segment * columns + c
        before = lax.rem(segment + groups - at_first, groups)
        after = lax.rem(segment + at_last, groups)

        def listed(a):
            return jnp.concatenate(
                [kv[pair, a, t] for t in range(groups)]
                + [glob[pair, 2 * w + a] for w in range(GLOBALS)]
                + [side[pair, 0, a, before], side[pair, 1, a, after]],
                axis=0,
            )

        key = listed(0)
        value = listed(1)
        query = stacked(qg[pair, 0, segment] * jnp.asarray(factor, BF16))
        grad = stacked(qg[pair, 1, segment])
        scores = contract(key, query, ((1,), (1,)))
        scores = jnp.concatenate(
            [
                scores[:dense],
                jnp.where(block > 0, scores[dense : dense + rows], -1e30),
                jnp.where(block < last, scores[dense + rows :], -1e30),
            ],
            axis=0,
        )
        raised = jnp.exp(scores - jnp.max(scores, axis=0, keepdims=True))
        prob = raised * (1.0 / jnp.sum(raised, axis=0, keepdims=True))
        half = prob.astype(BF16)
        d_prob = contract(value, grad, ((1,), (1,)))
        row_dot = jnp.sum(prob * d_prob, axis=0, keepdims=True)
        d_scores = (prob * (d_prob - row_dot)).astype(BF16)

        def part(start, stop):
            return (
                contract(d_scores[start:stop], query, ((1,), (0,))),
                contract(half[start:stop], grad, ((1,), (0,))),
            )

        def rows_out():
            result = contract(value, half, ((0,), (0,)))
            d_query = contract(key, d_scores, ((0,), (0,))) * factor
            row_parts[pair, segment, 0] = picked(result).astype(BF16)
            row_parts[pair, segment, 1] = picked(d_query).astype(BF16)

        return part, rows_out

    def ready(pair):
        settle(side.at[pair], side_recv.at[pair])
        settle(glob.at[pair, :, pl.ds(0, rows - strip)], gb_recv.at[pair])
        settle(qg.at[pair, :, h], own_sem.at[1, pair])

    def run(pair, i, closing=(), share_now=True):
        segment = lax.rem(h + i + 1, groups)
        if i < groups - 1:
            settle(qg.at[pair, :, segment], qg_recv.at[pair, groups - 2 - i])
        part, rows_out = unit(pair, i)

        def summed(start, stop):
            grads = part(start, stop)
            for a in range(2):
                if i == groups - 1:
                    dsum[pair, a, start:stop] = grads[a]
                else:
                    dsum[pair, a, start:stop] += grads[a]

        def sides_out():
            grads = part(dense, dense + 2 * rows)
            for a in range(2):
                dside[pair, 0, a, i] = grads[a][:rows].astype(BF16)
                dside[pair, 1, a, i] = grads[a][rows:].astype(BF16)

        if closing:
            summed(groups * rows, dense)
            scatter(pair)
            sides_out()
            for late in closing:
                send_dsides(pair, late)
            rows_out()
            summed(0, groups * rows)
        else:
            rows_out()
            summed(0, dense)
            sides_out()
            if share_now:
                send_dsides(pair, i)
        send_out(pair, segment, i < groups - 1, 0)

    def scatter(pair):
        for w in range(GLOBALS):
            for a in range(2):
                start = (groups + w) * rows
                dg_out[pair, 2 * w + a] = dsum[pair, a, start : start + rows].astype(BF16)
        for e in range(1, columns):
            to = lax.rem(c + e, columns)
            remote(
                dg_out.at[pair, :, rows_of(to), :], dg_in.at[pair, c],
                glob_send.at[2], da_recv.at[pair], (h, to),
            ).start()
        dg_in[pair, c] = dg_out[pair, :, rows_of(c), :]

    def gather(pair):
        settle(dg_in.at[pair, pl.ds(0, columns - 1)], da_recv.at[pair])
        total = dg_in[pair, 0].astype(F32)
        for e in range(1, columns):
            total = total + dg_in[pair, e].astype(F32)
        dg_sum[pair, :, rows_of(c), :] = total.astype(BF16)
        for e in range(1, columns):
            to = lax.rem(c + e, columns)
            remote(
                dg_sum.at[pair, moving, rows_of(c), :], dg_sum.at[pair, moving, rows_of(c), :],
                glob_send.at[3], db_recv.at[pair], (h, to),
            ).start()

        @pl.when(c < columns - 1)
        def _():
            remote(
                dg_sum.at[pair, fixed, rows_of(c), :], dg_sum.at[pair, fixed, rows_of(c), :],
                fixed_send.at[1], dt_recv.at[pair], (h, columns - 1),
            ).start()

    def finish(pair):
        settle(dside_in.at[pair], ds_recv.at[pair])
        settle(dg_sum.at[pair, moving, pl.ds(0, rows - strip)], db_recv.at[pair])

        @pl.when(c == columns - 1)
        def _():
            settle(dg_sum.at[pair, fixed, pl.ds(0, rows - strip)], dt_recv.at[pair])
            span = pl.ds((groups - 1) * rows, rows)
            for a in range(2):
                dsum[pair, a, span] += dg_sum[pair, 2 + a].astype(F32)

        for n in range(groups):
            segment = n + jnp.where(h <= n, 1, 0) if n < groups - 1 else h
            place = lax.rem(segment + 2 * groups - 1 - h, groups)
            low = lax.rem(place + at_last, groups)
            high = lax.rem(place + groups - at_first, groups)
            span = pl.ds(pl.multiple_of(segment * rows, rows), rows)
            mine = (other == segment * columns + c).astype(F32)
            for a in range(2):
                whole = dsum[pair, a, span]
                whole += dside_in[pair, 0, a, low].astype(F32)
                whole += dside_in[pair, 1, a, high].astype(F32)
                whole += dg_sum[pair, a].astype(F32) * mine
                key_parts[pair, segment, a] = whole.astype(BF16)
            send_out(pair, segment, n < groups - 1, 2)

    def then(step, *rest):
        return functools.partial(step, *rest)

    send_in(0, 0)
    forward(0, {2: then(send_in, 0, 1)}, (2, 3))
    send_in(1, 0)
    choose(0)
    forward(1, {1: then(send_in, 1, 1)}, range(groups))
    ready(0)
    run(0, 3, False, False)
    choose(1)
    run(0, 2, False, False)
    send_dsides(0, 3)
    run(0, 1, False, False)
    send_dsides(0, 2)
    run(0, 0, (1,))
    ready(1)
    run(1, 3, False, False)
    send_dsides(0, 0)
    run(1, 2, False, False)
    send_dsides(1, 3)
    run(1, 1, False, False)
    gather(0)
    send_dsides(1, 2)
    run(1, 0, (1, 0))
    finish(0)
    gather(1)
    finish(1)

    shares = pl.ds(0, groups - 1)
    for n in range(2):
        settle(kv.at[:, :, shares], in_send.at[n])
        settle(kv.at[:, :, shares], out_send.at[n])
        settle(kv.at[:, :, shares], out_recv.at[n])
    settle(side, side_send.at[0])
    settle(dside, ds_send.at[0])
    settle(piece.at[:, pl.ds(0, columns - 1)], glob_send.at[0])
    settle(glob.at[:, :, pl.ds(0, rows - strip)], glob_send.at[1])
    settle(dg_in.at[:, pl.ds(0, columns - 1)], glob_send.at[2])
    settle(dg_sum.at[:, moving, pl.ds(0, rows - strip)], glob_send.at[3])

    @pl.when(c == columns - 1)
    def _():
        settle(glob.at[:, fixed, pl.ds(0, rows - strip)], fixed_send.at[0])

    @pl.when(c < columns - 1)
    def _():
        settle(glob.at[:, fixed, pl.ds(0, strip)], fixed_send.at[1])

    settle(kv.at[:, :, pl.ds(0, 2)], keep_sem.at[0])


def fused(groups, columns, query, keys, values, d_out, rand_blocks, global_blocks):
    rows, width = query.shape
    share = width // groups
    strip = rows // columns
    half = functools.partial(pltpu.VMEM, dtype=BF16)
    full = functools.partial(pltpu.VMEM, dtype=F32)
    dma = pltpu.SemaphoreType.DMA
    pairs = share // LANES
    tile = (rows, LANES)
    scratch = [
        half((pairs, 2, groups, *tile)),
        half((pairs, 2, groups, *tile)),
        half((pairs, 2, 2, groups, *tile)),
        half((pairs, 2, *tile)),
        half((pairs, columns, 2, strip, LANES)),
        half((pairs, 2 * GLOBALS, *tile)),
        full((pairs, 2, (groups + GLOBALS) * rows, LANES)),
        half((pairs, 2, 2, groups, *tile)),
        half((pairs, 2, 2, groups, *tile)),
        half((pairs, 2 * GLOBALS, *tile)),
        half((pairs, columns, 2 * GLOBALS, strip, LANES)),
        half((pairs, 2 * GLOBALS, *tile)),
    ] + [half((pairs, groups, 2, *tile))] * 2
    scratch += [dma((2, pairs))] + [dma((pairs, groups - 1))] * 2 + [dma((pairs,))] * 8
    scratch += [dma((2,)), dma((1,)), dma((4,)), dma((1,)), dma((2,)), dma((2,)), dma((1,)), dma((2,))]
    hbm = pl.BlockSpec(memory_space=pltpu.HBM)
    return pl.pallas_call(
        functools.partial(fused_kernel, groups, columns),
        out_shape=jax.ShapeDtypeStruct((4, rows, width), BF16),
        in_specs=[pl.BlockSpec(memory_space=pltpu.SMEM)] + [hbm] * 4,
        out_specs=hbm,
        scratch_shapes=scratch,
        compiler_params=pltpu.CompilerParams(
            collective_id=0, has_side_effects=True, vmem_limit_bytes=63 * 2**20
        ),
    )(global_blocks, query, keys, values, d_out)


CHUNKS = 4


def relay_kernel(source, *refs):
    targets, (held, in_sem, out_sem) = refs[:-3], refs[-3:]
    rows = held.shape[1] // CHUNKS
    parts = [pl.ds(part * rows, rows) for part in range(CHUNKS)]
    arrivals = [
        pltpu.make_async_copy(source.at[:, at], held.at[:, at], in_sem.at[part])
        for part, at in enumerate(parts)
    ]
    for copy in arrivals:
        copy.start()
    for copy, at in zip(arrivals, parts):
        copy.wait()
        for n, target in enumerate(targets):
            pltpu.make_async_copy(held.at[n, at], target.at[at], out_sem.at[0]).start()
    pltpu.make_async_copy(held, held, out_sem.at[0]).wait()


def relay(stacked):
    hbm = pl.BlockSpec(memory_space=pltpu.HBM)
    count, *shape = stacked.shape
    return pl.pallas_call(
        relay_kernel,
        out_shape=[jax.ShapeDtypeStruct(tuple(shape), stacked.dtype)] * count,
        in_specs=[hbm],
        out_specs=[hbm] * count,
        scratch_shapes=[
            pltpu.VMEM(stacked.shape, stacked.dtype),
            pltpu.SemaphoreType.DMA((CHUNKS,)),
            pltpu.SemaphoreType.DMA((1,)),
        ],
    )(stacked)


def solution(mesh):
    in_specs = (
        P(("grp", "seq"), None),
        P(("grp", "seq"), None),
        P(("grp", "seq"), None),
        P(("grp", "seq"), None),
        P(),
        P(),
    )
    out_specs = (
        P(("grp", "seq"), None),
        P(("grp", "seq"), None),
        P(("grp", "seq"), None),
        P(("grp", "seq"), None),
    )
    groups, columns = mesh.shape["grp"], mesh.shape["seq"]

    def run(query, *rest):
        rows, width = query.shape
        whole_column = rows == BLOCK and groups - 1 == RANDOMS and groups % 2 == 0
        if whole_column and rows % (16 * columns) == 0 and width == 2 * groups * LANES:
            return relay(fused(groups, columns, query, *rest))
        return body(query, *rest)

    return jax.shard_map(run, mesh=mesh, in_specs=in_specs, out_specs=out_specs, check_vma=False)
```
